32 devices in a mesh: narrow: 4 (over x, core), wide: 8 (over z, y).
Axes of the slice: x: 2, y: 2, z: 4, core: 2. Of those that a mesh axis runs over, the one named last changes fastest.
Arguments:
- panel: float32 [131072, 128], P(('narrow', 'wide')), may hold values from -6 to 6
- flips: int32 [131072], P(('narrow', 'wide')), may hold values from 0 to 1
- picks: int32 [8192], replicated, may hold values from 0 to 131071, as said below
Outputs:
- mixed: float32 [131072, 128], P(('narrow', 'wide'))
- sketch: float32 [8192, 128], P(('narrow', 'wide'))
- gram: float32 [128, 128], replicated
The draws below stay inside these ranges and needn't reach their ends.
Inputs may be any that keep to these rules, and one draw needn't show every extreme that they name: Split picks into aligned blocks of 256 entries, one block for each device in the order of narrow+wide. In every block, at most 8 entries name rows of any one device's block of 4096 rows, and some device's block is named exactly 8 times. Within a device's block the row is uniform; repeats may occur.
All inputs are finite; a program needn't handle non-finite values.
Results may differ from the reference program's by a relative error of at most 0.00011.
Values sent between devices are 32-bit elements; how exact they have to be, the bound alone decides.
No kernel may reach another device: no remote copies, remote signals or barrier semaphores. Data moves between devices by JAX's collectives and lax.ppermute only.
A program may use at most 64 MiB of HBM per device.

```python
import jax
import jax.numpy as jnp
from jax import lax

COLS = 128
ROWS_DEV = 4096
SAMPLES = 8192
ROWS = 131072
N_NARROW = 4
N_WIDE = 8


def draw_picks(key, part):
    key = jax.random.fold_in(key, 7)
    devices = N_NARROW * N_WIDE
    per_block = SAMPLES // devices
    block_keys = jax.random.split(jax.random.fold_in(key, 1), devices)
    orders = jax.vmap(lambda k: jax.random.permutation(k, devices))(block_keys)
    position = jnp.arange(per_block, dtype=jnp.int32) % devices
    owners = jnp.take(orders, position, axis=1).astype(jnp.int32)
    offsets = jax.random.randint(jax.random.fold_in(key, 2), (devices, per_block), 0, ROWS_DEV, dtype=jnp.int32)
    return (owners * ROWS_DEV + offsets).reshape(SAMPLES).astype(jnp.int32)


def with_ends(entries, stream_key, low, high):
    longest = entries.shape.index(max(entries.shape))
    spots = []
    for shift in (0, 1):
        where = [jax.random.randint(jax.random.fold_in(stream_key, axis), (), 0, length) for axis, length in enumerate(entries.shape)]
        where[longest] = (where[longest] + shift) % entries.shape[longest]
        spots.append(tuple(where))
    return entries.at[spots[0]].set(low).at[spots[1]].set(high)


def level_of(key, shape, pieces, low, largest):
    loudness, own = 1.0, jax.random.fold_in(key, 6)
    for dim, parts in pieces:
        steps = jnp.exp(jax.random.uniform(jax.random.fold_in(own, dim), (parts,), jnp.float32, low / len(pieces), largest / len(pieces)))
        loudness = loudness * jnp.repeat(steps, shape[dim] // parts).reshape([-1 if axis == dim else 1 for axis in range(len(shape))])
    return loudness


def gaussian(own_key, extent, width, bound, cuts=(), kind=jnp.bfloat16):
    values = jax.random.normal(own_key, extent, jnp.float32) * width
    if len(cuts) > 0:
        values = level_of(own_key, extent, cuts, -0.22, 0.18) * values
    return jnp.clip(values, min=-bound, max=bound).astype(kind)


def setup_inputs(seed: int = 0) -> dict:
    keys = jax.random.split(jax.random.key(seed), 4)
    return {
        "panel": gaussian(keys[0], (ROWS, COLS), 1.0, 6.0, ((0, 32),), jnp.float32),
        "flips": with_ends(jax.random.randint(keys[1], (ROWS,), 0, 2), jax.random.fold_in(keys[1], 1), 0, 1).astype(jnp.int32),
        "picks": draw_picks(jax.random.fold_in(keys[3], 71), 0),
    }


def hadamard(order):
    index = jnp.arange(order, dtype=jnp.int32)
    both = index[:, None] & index[None, :]
    parity = jnp.zeros((order, order), jnp.int32)
    level = 0
    while (1 << level) < order:
        parity = parity ^ ((both >> level) & 1)
        level += 1
    return (1 - 2 * parity).astype(jnp.float32)


def reference(panel, flips, picks):
    devices = N_NARROW * N_WIDE
    inner = ROWS_DEV // 64
    signed = panel * (1 - 2 * flips).astype(jnp.float32)[:, None]
    shaped = signed.reshape(devices, 64, inner, COLS)
    shaped = jnp.einsum("ap,dpqc->daqc", hadamard(64), shaped, precision=lax.Precision.HIGHEST)
    shaped = jnp.einsum("bq,daqc->dabc", hadamard(inner), shaped, precision=lax.Precision.HIGHEST)
    shaped = jnp.einsum("ed,dabc->eabc", hadamard(devices), shaped, precision=lax.Precision.HIGHEST)
    mixed = shaped.reshape(ROWS, COLS) * (1.0 / (float(ROWS) ** 0.5))
    sketch = jnp.take(mixed, picks, axis=0)
    gram = jnp.dot(sketch.T, sketch, precision=lax.Precision.HIGHEST, preferred_element_type=jnp.float32) / SAMPLES
    return mixed, sketch, gram
```

```python
import functools

import jax
import jax.numpy as jnp
from jax import lax
from jax.experimental import pallas as pl
from jax.experimental.pallas import tpu as pltpu
from jax.sharding import PartitionSpec as P

BLOCK = 256
AXES = ("narrow", "wide")


def signs(order):
    rows = lax.broadcasted_iota(jnp.int32, (order, order), 0)
    both = rows & lax.broadcasted_iota(jnp.int32, (order, order), 1)
    parity = jnp.zeros((order, order), jnp.int32)
    for level in range(order.bit_length() - 1):
        parity = parity ^ (both >> level & 1)
    return (1 - 2 * parity).astype(jnp.float32)


def local_kernel(scale, flips_ref, panel_ref, *refs):
    *outs, held = refs
    blocks = panel_ref.shape[0] // BLOCK
    width = panel_ref.shape[1]
    lanes = flips_ref.shape[1]
    per = BLOCK // lanes
    base = signs(BLOCK)
    for b in range(blocks):
        row = jnp.concatenate([flips_ref[b * per + i : b * per + i + 1, :] for i in range(per)], axis=1)
        mixer = (base * (1 - 2 * row).astype(jnp.float32)).astype(jnp.bfloat16)
        values = panel_ref[b * BLOCK : (b + 1) * BLOCK, :]
        high = values.astype(jnp.bfloat16)
        rest = values - high.astype(jnp.float32)
        middle = rest.astype(jnp.bfloat16)
        low = (rest - middle.astype(jnp.float32)).astype(jnp.bfloat16)
        parts = jnp.concatenate([high, middle, low], axis=1)
        out = jnp.dot(mixer, parts, preferred_element_type=jnp.float32)
        held[b] = out[:, :width] + out[:, width : 2 * width] + out[:, 2 * width :]
    strip = 16
    share = blocks // len(outs)

    def body(step, carry):
        at = pl.multiple_of(step * strip, strip)
        items = [held[b, pl.ds(at, strip), :] for b in range(blocks)]
        apart = 1
        while apart < blocks:
            items = [
                items[b] + items[b ^ apart] if b & apart == 0 else items[b ^ apart] - items[b]
                for b in range(blocks)
            ]
            apart *= 2
        for b in range(blocks):
            spot = pl.multiple_of((b % share) * BLOCK + at, strip)
            outs[b // share][pl.ds(spot, strip), :] = items[b] * scale
        return carry

    lax.fori_loop(0, BLOCK // strip, body, 0)


def local_transform(panel, flips, scale, pieces):
    rows, width = panel.shape
    return pl.pallas_call(
        functools.partial(local_kernel, scale),
        out_shape=[jax.ShapeDtypeStruct((rows // pieces, width), jnp.float32)] * pieces,
        in_specs=[pl.BlockSpec(memory_space=pltpu.VMEM)] * 2,
        out_specs=[pl.BlockSpec(memory_space=pltpu.VMEM)] * pieces,
        scratch_shapes=[pltpu.VMEM((rows // BLOCK, BLOCK, width), jnp.float32)],
        compiler_params=pltpu.CompilerParams(vmem_limit_bytes=32 * 2**20),
    )(flips.reshape(rows // 128, 128), panel)


def exchange(value, axis, level):
    mask = 2**level
    pairs = [(source, source ^ mask) for source in range(lax.axis_size(axis))]
    partner = lax.ppermute(value, axis, pairs)
    sign = (1 - 2 * (lax.axis_index(axis) >> level & 1)).astype(jnp.float32)
    return partner + sign * value


def send_rows(picks, base, rows_here, devices, most):
    offsets = picks.reshape(devices, -1) - base
    owned = (offsets >= 0) & (offsets < rows_here)
    rank = jnp.cumsum(owned.astype(jnp.int32), axis=1) - 1
    slot = jnp.arange(most, dtype=jnp.int32)
    hit = owned[:, None, :] & (rank[:, None, :] == slot[None, :, None])
    rows = jnp.sum(jnp.where(hit, offsets[:, None, :], 0), axis=2)
    return rows, jnp.any(hit, axis=2)


def landing(block, rows_here, most):
    owners = block // rows_here
    order = jnp.arange(block.shape[0], dtype=jnp.int32)
    earlier = (owners[:, None] == owners[None, :]) & (order[None, :] < order[:, None])
    return owners * most + jnp.sum(earlier.astype(jnp.int32), axis=1)


def on_device(panel, flips, picks):
    rows_here, width = panel.shape
    narrow, wide = lax.axis_size("narrow"), lax.axis_size("wide")
    devices = narrow * wide
    scale = 1.0 / float(rows_here * devices) ** 0.5
    stages = [("narrow", l) for l in range(narrow.bit_length() - 1)]
    stages += [("wide", l) for l in range(wide.bit_length() - 1)]
    head, rest = stages[0], stages[1:]
    orders = [
        [rest[-1]] + rest[:-1],
        [rest[-1]] + rest[:-1],
        rest,
        [rest[-2]] + rest[:-2] + [rest[-1]],
    ]
    chunks = local_transform(panel, flips, scale, len(orders))
    done = []
    for value, order in zip(chunks, orders):
        for axis, level in [head] + order:
            value = exchange(value, axis, level)
        done.append(value)
    mixed = jnp.concatenate(done, axis=0)

    me = lax.axis_index(AXES)
    per = picks.shape[0] // devices
    most = -(-per // devices)
    rows, filled = send_rows(picks, me * rows_here, rows_here, devices, most)
    chosen = jnp.take(mixed, rows.reshape(-1), axis=0, mode="clip")
    kept = jnp.where(filled.reshape(-1)[:, None], chosen, 0.0)
    part = lax.dot_general(
        kept, kept, (((0,), (0,)), ((), ())),
        precision=lax.Precision.HIGHEST, preferred_element_type=jnp.float32,
    )
    both = jnp.concatenate(
        [chosen.reshape(devices, most, width), part.reshape(devices, -1, width)], axis=1
    )
    landed = lax.all_to_all(both, AXES, 0, 0, tiled=True)
    spots = landing(lax.dynamic_slice(picks, (me * per,), (per,)), rows_here, most)
    sketch = jnp.take(landed[:, :most].reshape(devices * most, width), spots, axis=0, mode="clip")
    mine = jnp.sum(landed[:, most:], axis=0) / float(picks.shape[0])
    gram = lax.all_to_all(
        jnp.broadcast_to(mine[None], (devices,) + mine.shape), AXES, 0, 0, tiled=True
    ).reshape(width, width)
    return (mixed, sketch, gram)


def solution(mesh):
    in_specs = (P(AXES, None), P(AXES), P())
    out_specs = (P(AXES, None), P(AXES, None), P())
    return jax.shard_map(
        on_device, mesh=mesh, in_specs=in_specs, out_specs=out_specs, check_vma=False
    )
```

```python
import functools

import jax
import jax.numpy as jnp
from jax import lax
from jax.experimental import pallas as pl
from jax.experimental.pallas import tpu as pltpu
from jax.sharding import PartitionSpec as P

BLOCK = 256
AXES = ("narrow", "wide")


def signs(order):
    rows = lax.broadcasted_iota(jnp.int32, (order, order), 0)
    both = rows & lax.broadcasted_iota(jnp.int32, (order, order), 1)
    parity = jnp.zeros((order, order), jnp.int32)
    for level in range(order.bit_length() - 1):
        parity = parity ^ (both >> level & 1)
    return (1 - 2 * parity).astype(jnp.float32)


def local_kernel(scale, flips_ref, panel_ref, *refs):
    *outs, held = refs
    blocks = panel_ref.shape[0] // BLOCK
    width = panel_ref.shape[1]
    lanes = flips_ref.shape[1]
    per = BLOCK // lanes
    base = signs(BLOCK)
    for b in range(blocks):
        row = jnp.concatenate([flips_ref[b * per + i : b * per + i + 1, :] for i in range(per)], axis=1)
        mixer = (base * (1 - 2 * row).astype(jnp.float32)).astype(jnp.bfloat16)
        values = panel_ref[b * BLOCK : (b + 1) * BLOCK, :]
        high = values.astype(jnp.bfloat16)
        rest = values - high.astype(jnp.float32)
        middle = rest.astype(jnp.bfloat16)
        low = (rest - middle.astype(jnp.float32)).astype(jnp.bfloat16)
        parts = jnp.concatenate([high, middle, low], axis=1)
        out = jnp.dot(mixer, parts, preferred_element_type=jnp.float32)
        held[b] = out[:, :width] + out[:, width : 2 * width] + out[:, 2 * width :]
    strip = 16
    share = blocks // len(outs)

    def body(step, carry):
        at = pl.multiple_of(step * strip, strip)
        items = [held[b, pl.ds(at, strip), :] for b in range(blocks)]
        apart = 1
        while apart < blocks:
            items = [
                items[b] + items[b ^ apart] if b & apart == 0 else items[b ^ apart] - items[b]
                for b in range(blocks)
            ]
            apart *= 2
        for b in range(blocks):
            spot = pl.multiple_of((b % share) * BLOCK + at, strip)
            outs[b // share][pl.ds(spot, strip), :] = items[b] * scale
        return carry

    lax.fori_loop(0, BLOCK // strip, body, 0)


def local_transform(panel, flips, scale, pieces):
    rows, width = panel.shape
    return pl.pallas_call(
        functools.partial(local_kernel, scale),
        out_shape=[jax.ShapeDtypeStruct((rows // pieces, width), jnp.float32)] * pieces,
        in_specs=[pl.BlockSpec(memory_space=pltpu.VMEM)] * 2,
        out_specs=[pl.BlockSpec(memory_space=pltpu.VMEM)] * pieces,
        scratch_shapes=[pltpu.VMEM((rows // BLOCK, BLOCK, width), jnp.float32)],
        compiler_params=pltpu.CompilerParams(vmem_limit_bytes=32 * 2**20),
    )(flips.reshape(rows // 128, 128), panel)


def launch(value, stage):
    axis, level = stage
    pairs = [(source, source ^ 2**level) for source in range(lax.axis_size(axis))]
    return lax.ppermute(value, axis, pairs), value, stage


def sign_of(stage):
    axis, level = stage
    return (1 - 2 * (lax.axis_index(axis) >> level & 1)).astype(jnp.float32)


def bit_of(stage):
    axis, level = stage
    return 2**level * (lax.axis_size("wide") if axis == "narrow" else 1)


def land(sent, other):
    partner, value, stage = sent
    partner = after(partner, other)
    return partner + sign_of(stage) * value


def send_rows(picks, base, rows_here, devices, most):
    offsets = picks.reshape(devices, -1) - base
    owned = (offsets >= 0) & (offsets < rows_here)
    rank = jnp.cumsum(owned.astype(jnp.int32), axis=1) - 1
    slot = jnp.arange(most, dtype=jnp.int32)
    hit = owned[:, None, :] & (rank[:, None, :] == slot[None, :, None])
    rows = jnp.sum(jnp.where(hit, offsets[:, None, :], 0), axis=2)
    return rows, jnp.any(hit, axis=2)


def pick_rows(held, picks, owner, rows_here, devices, most):
    rows, _ = send_rows(picks, owner * rows_here, rows_here, devices, most)
    return jnp.take(held, rows.reshape(-1), axis=0, mode="clip")


def landing(block, rows_here, most):
    owners = block // rows_here
    order = jnp.arange(block.shape[0], dtype=jnp.int32)
    earlier = (owners[:, None] == owners[None, :]) & (order[None, :] < order[:, None])
    return owners * most + jnp.sum(earlier.astype(jnp.int32), axis=1)


def after(value, *others):
    return lax.optimization_barrier((value, others))[0]


def on_device(panel, flips, picks):
    rows_here, width = panel.shape
    narrow, wide = lax.axis_size("narrow"), lax.axis_size("wide")
    devices = narrow * wide
    scale = 1.0 / float(rows_here * devices) ** 0.5
    near = [("narrow", l) for l in range(narrow.bit_length() - 1)]
    near += [("wide", l) for l in range(wide.bit_length() - 3)]
    far, mid = ("wide", wide.bit_length() - 2), ("wide", wide.bit_length() - 3)
    near = [stage for stage in near if stage not in (far, mid)]
    head, first, second = near[0], near[1:], near[:0:-1]

    me = lax.axis_index(AXES)
    per = picks.shape[0] // devices
    most = -(-per // devices)

    c = local_transform(panel, flips, scale, 4)
    quarter = rows_here // 4
    z = {}
    z[0] = launch(c[0], far)
    z[2] = launch(c[2], mid)
    k = {1: launch(c[1], head), 3: launch(c[3], head)}
    last = c[0]

    def settle(sent, *stage):
        nonlocal last
        out = land(sent, last)
        last = out
        return out

    v = {1: settle(k[1]), 3: settle(k[3])}
    for one, two in zip(first, second):
        k = {1: launch(v[1], one), 3: launch(v[3], two)}
        v = {1: settle(k[1]), 3: settle(k[3])}
    z[1] = launch(v[1], far)
    z[3] = launch(v[3], mid)
    v[0] = settle(z[0])
    v[2] = settle(z[2])
    for one, two in zip([head] + first, [head] + second):
        k = {0: launch(v[0], one), 2: launch(v[2], two)}
        v[0], v[2] = settle(k[0]), settle(k[2])
    z[2] = launch(v[2], far)
    v[1] = settle(z[1])
    v[3] = settle(z[3])

    held = jnp.concatenate([v[0], v[1], v[2], v[3]], axis=0)
    near_mid = pick_rows(held, picks, me ^ bit_of(mid), rows_here, devices, most)
    near_far = pick_rows(held, picks, me ^ bit_of(far), rows_here, devices, most)
    give_mid = launch(near_mid, mid)
    give_far = launch(near_far, far)
    z[0] = launch(v[0], mid)
    z[3] = launch(v[3], far)
    z[1] = launch(v[1], mid)
    rows, filled = send_rows(picks, me * rows_here, rows_here, devices, most)
    rows, filled = rows.reshape(-1), filled.reshape(-1)
    own = jnp.take(held, rows, axis=0, mode="clip")
    upper = (rows >= 2 * quarter)[:, None]
    chosen = jnp.where(
        upper, give_far[0] + sign_of(far) * own, give_mid[0] + sign_of(mid) * own
    )
    kept = jnp.where(filled[:, None], chosen, 0.0)
    part = lax.dot_general(
        kept, kept, (((0,), (0,)), ((), ())),
        precision=lax.Precision.HIGHEST, preferred_element_type=jnp.float32,
    )
    both = jnp.concatenate(
        [chosen.reshape(devices, most, width), part.reshape(devices, -1, width)], axis=1
    )
    landed = lax.all_to_all(both, AXES, 0, 0, tiled=True)
    mine = jnp.sum(landed[:, most:], axis=0) / float(picks.shape[0])
    gram = lax.all_to_all(
        jnp.broadcast_to(mine[None], (devices,) + mine.shape), AXES, 0, 0, tiled=True
    ).reshape(width, width)
    spots = landing(lax.dynamic_slice(picks, (me * per,), (per,)), rows_here, most)
    sketch = jnp.take(landed[:, :most].reshape(devices * most, width), spots, axis=0, mode="clip")
    last = gram
    mixed = jnp.concatenate(
        [settle(z[0]), settle(z[1]), settle(z[2]), settle(z[3])], axis=0
    )
    return (mixed, sketch, gram)


def solution(mesh):
    in_specs = (P(AXES, None), P(AXES), P())
    out_specs = (P(AXES, None), P(AXES, None), P())
    return jax.shard_map(
        on_device, mesh=mesh, in_specs=in_specs, out_specs=out_specs, check_vma=False
    )
```

```python
import functools

import jax
import jax.numpy as jnp
from jax import lax
from jax.experimental import pallas as pl
from jax.experimental.pallas import tpu as pltpu
from jax.sharding import PartitionSpec as P

BLOCK = 256
AXES = ("narrow", "wide")


def signs(order):
    rows = lax.broadcasted_iota(jnp.int32, (order, order), 0)
    both = rows & lax.broadcasted_iota(jnp.int32, (order, order), 1)
    parity = jnp.zeros((order, order), jnp.int32)
    for level in range(order.bit_length() - 1):
        parity = parity ^ (both >> level & 1)
    return (1 - 2 * parity).astype(jnp.float32)


def local_kernel(scale, flips_ref, panel_ref, *refs):
    *outs, held = refs
    blocks = panel_ref.shape[0] // BLOCK
    width = panel_ref.shape[1]
    lanes = flips_ref.shape[1]
    per = BLOCK // lanes
    base = signs(BLOCK)
    for b in range(blocks):
        row = jnp.concatenate([flips_ref[b * per + i : b * per + i + 1, :] for i in range(per)], axis=1)
        mixer = (base * (1 - 2 * row).astype(jnp.float32)).astype(jnp.bfloat16)
        values = panel_ref[b * BLOCK : (b + 1) * BLOCK, :]
        high = values.astype(jnp.bfloat16)
        rest = values - high.astype(jnp.float32)
        middle = rest.astype(jnp.bfloat16)
        low = (rest - middle.astype(jnp.float32)).astype(jnp.bfloat16)
        parts = jnp.concatenate([high, middle, low], axis=1)
        out = jnp.dot(mixer, parts, preferred_element_type=jnp.float32)
        held[b] = out[:, :width] + out[:, width : 2 * width] + out[:, 2 * width :]
    strip = 16
    places = [(i, j) for i in range(len(outs)) for j in range(outs[i].shape[0] // BLOCK)]

    def body(step, carry):
        at = pl.multiple_of(step * strip, strip)
        items = [held[b, pl.ds(at, strip), :] for b in range(blocks)]
        apart = 1
        while apart < blocks:
            items = [
                items[b] + items[b ^ apart] if b & apart == 0 else items[b ^ apart] - items[b]
                for b in range(blocks)
            ]
            apart *= 2
        for b in range(blocks):
            which, place = places[b]
            spot = pl.multiple_of(place * BLOCK + at, strip)
            outs[which][pl.ds(spot, strip), :] = items[b] * scale
        return carry

    lax.fori_loop(0, BLOCK // strip, body, 0)


def local_transform(panel, flips, scale, shares):
    rows, width = panel.shape
    return pl.pallas_call(
        functools.partial(local_kernel, scale),
        out_shape=[jax.ShapeDtypeStruct((share, width), jnp.float32) for share in shares],
        in_specs=[pl.BlockSpec(memory_space=pltpu.VMEM)] * 2,
        out_specs=[pl.BlockSpec(memory_space=pltpu.VMEM)] * len(shares),
        scratch_shapes=[pltpu.VMEM((rows // BLOCK, BLOCK, width), jnp.float32)],
        compiler_params=pltpu.CompilerParams(vmem_limit_bytes=32 * 2**20),
    )(flips.reshape(rows // 128, 128), panel)


def launch(value, stage):
    axis, level = stage
    pairs = [(source, source ^ 2**level) for source in range(lax.axis_size(axis))]
    return lax.ppermute(value, axis, pairs), value, stage


def sign_of(stage):
    axis, level = stage
    return (1 - 2 * (lax.axis_index(axis) >> level & 1)).astype(jnp.float32)


def bit_of(stage):
    axis, level = stage
    return 2**level * (lax.axis_size("wide") if axis == "narrow" else 1)


class Chain:
    def __init__(self):
        self.last = ()

    def end(self, sent):
        partner, value, stage = sent
        partner = after(partner, self.last)
        self.last = partner + sign_of(stage) * value
        return self.last

    def begin(self, value, stages):
        for stage in stages[:-1]:
            value = self.end(launch(value, stage))
        return launch(value, stages[-1])


def split(value, parts):
    units = value.shape[0] // 16
    cuts = [16 * (units * i // parts) for i in range(parts + 1)]
    return [value[low:high] for low, high in zip(cuts, cuts[1:])]


def send_rows(picks, base, rows_here, devices, most):
    offsets = picks.reshape(devices, -1) - base
    owned = (offsets >= 0) & (offsets < rows_here)
    rank = jnp.cumsum(owned.astype(jnp.int32), axis=1) - 1
    slot = jnp.arange(most, dtype=jnp.int32)
    hit = owned[:, None, :] & (rank[:, None, :] == slot[None, :, None])
    rows = jnp.sum(jnp.where(hit, offsets[:, None, :], 0), axis=2)
    return rows, jnp.any(hit, axis=2)


def landing(block, rows_here, most):
    owners = block // rows_here
    order = jnp.arange(block.shape[0], dtype=jnp.int32)
    earlier = (owners[:, None] == owners[None, :]) & (order[None, :] < order[:, None])
    return owners * most + jnp.sum(earlier.astype(jnp.int32), axis=1)


def after(value, *others):
    return lax.optimization_barrier((value, others))[0]


def on_device(panel, flips, picks):
    rows_here, width = panel.shape
    narrow, wide = lax.axis_size("narrow"), lax.axis_size("wide")
    devices = narrow * wide
    scale = 1.0 / float(rows_here * devices) ** 0.5
    levels = wide.bit_length() - 1
    far, mid = ("wide", levels - 1), ("wide", levels - 2)
    near = [("narrow", l) for l in range(narrow.bit_length() - 1)]
    near += [("wide", l) for l in range(levels - 2)]
    core, first, second = near[:1], near[1:2], near[2:]

    me = lax.axis_index(AXES)
    per = picks.shape[0] // devices
    most = -(-per // devices)
    cuts = [0, 5, 8, 11, 16]
    cuts = [cut * rows_here // 16 for cut in cuts]

    c = local_transform(panel, flips, scale, [b - a for a, b in zip(cuts, cuts[1:])])
    chain = Chain()

    def halves(value):
        return [launch(part, far) for part in split(value, 2)]

    far0 = halves(c[0])
    mid2 = launch(c[2], mid)
    core1, core3 = chain.begin(c[1], core), chain.begin(c[3], core)
    rows, filled = send_rows(picks, me * rows_here, rows_here, devices, most)
    rows, filled = rows.reshape(-1), filled.reshape(-1)
    rows_mid = send_rows(picks, (me ^ bit_of(mid)) * rows_here, rows_here, devices, most)[0].reshape(-1)
    rows_far = send_rows(picks, (me ^ bit_of(far)) * rows_here, rows_here, devices, most)[0].reshape(-1)
    spots = landing(lax.dynamic_slice(picks, (me * per,), (per,)), rows_here, most)

    first1 = chain.begin(chain.end(core1), first)
    second3 = chain.begin(chain.end(core3), second)
    chain.last = (chain.last, rows, filled, rows_mid, rows_far, spots)
    second1 = chain.begin(chain.end(first1), second)
    v0 = [chain.end(far0[0])]
    mid3 = launch(chain.end(second3), mid)
    core2 = chain.begin(chain.end(mid2), core)
    first2 = chain.begin(chain.end(core2), first)
    far1 = halves(chain.end(second1))
    second2 = chain.begin(chain.end(first2), second)
    v0 = jnp.concatenate(v0 + [chain.end(far0[1])], axis=0)
    core0 = chain.begin(v0, core)
    first0 = chain.begin(chain.end(core0), first)
    v1 = [chain.end(far1[0])]
    far2 = halves(chain.end(second2))
    v1 = jnp.concatenate(v1 + [chain.end(far1[1])], axis=0)
    mid1 = launch(v1, mid)
    second0 = chain.begin(chain.end(first0), second)
    first3 = chain.begin(chain.end(mid3), first)
    v2 = [chain.end(far2[0])]
    v3 = chain.end(first3)
    v0 = chain.end(second0)
    v2 = jnp.concatenate(v2 + [chain.end(far2[1])], axis=0)
    v1 = chain.end(mid1)

    held = jnp.concatenate([v0, v1, v2, v3], axis=0)
    wanted = jnp.concatenate([rows_far, rows_mid, rows])
    taken = jnp.take(held, wanted, axis=0, mode="clip")
    count = devices * most
    give_far = launch(taken[:count], far)
    give_mid = launch(taken[count : 2 * count], mid)
    own = taken[2 * count :]
    parts0, parts3 = split(v0, 2), split(v3, 2)
    ends0, ends3 = [], []

    def more(step, gate):
        ends3.append(launch(after(parts3[step], gate), far))
        ends0.append(launch(after(parts0[step], gate), mid))

    got_far = chain.end((give_far[0], own, far))
    got_mid = chain.end((give_mid[0], own, mid))
    place = rows[:, None]
    chosen = jnp.where(
        place >= cuts[3], got_far, jnp.where(place < cuts[1], got_mid, own)
    )
    kept = jnp.where(filled[:, None], chosen, 0.0)
    part = lax.dot_general(
        kept, kept, (((0,), (0,)), ((), ())),
        precision=lax.Precision.HIGHEST, preferred_element_type=jnp.float32,
    )
    both = jnp.concatenate(
        [chosen.reshape(devices, most, width), part.reshape(devices, -1, width)], axis=1
    )
    landed = lax.all_to_all(both, AXES, 0, 0, tiled=True)
    more(0, both)
    mine = jnp.sum(landed[:, most:], axis=0) / float(picks.shape[0])
    shared = jnp.broadcast_to(mine[None], (devices,) + mine.shape)
    gram = lax.all_to_all(shared, AXES, 0, 0, tiled=True).reshape(width, width)
    more(1, shared)
    sketch = jnp.take(landed[:, :most].reshape(devices * most, width), spots, axis=0, mode="clip")
    chain.last = (chain.last, landed)
    final0, final3 = [], []
    for step in range(2):
        final3.append(chain.end(ends3[step]))
        final0.append(chain.end(ends0[step]))
        chain.last = (chain.last, gram, sketch)
    mixed = jnp.concatenate(final0 + [v1, v2] + final3, axis=0)
    return (mixed, sketch, gram)


def solution(mesh):
    in_specs = (P(AXES, None), P(AXES), P())
    out_specs = (P(AXES, None), P(AXES, None), P())
    return jax.shard_map(
        on_device, mesh=mesh, in_specs=in_specs, out_specs=out_specs, check_vma=False
    )
```

```python
import functools

import jax
import jax.numpy as jnp
from jax import lax
from jax.experimental import pallas as pl
from jax.experimental.pallas import tpu as pltpu
from jax.sharding import PartitionSpec as P

BLOCK = 256
AXES = ("narrow", "wide")


def signs(order):
    rows = lax.broadcasted_iota(jnp.int32, (order, order), 0)
    both = rows & lax.broadcasted_iota(jnp.int32, (order, order), 1)
    parity = jnp.zeros((order, order), jnp.int32)
    for level in range(order.bit_length() - 1):
        parity = parity ^ (both >> level & 1)
    return (1 - 2 * parity).astype(jnp.float32)


def local_kernel(scale, flips_ref, panel_ref, *refs):
    *outs, held = refs
    blocks = panel_ref.shape[0] // BLOCK
    width = panel_ref.shape[1]
    lanes = flips_ref.shape[1]
    per = BLOCK // lanes
    base = signs(BLOCK)
    for b in range(blocks):
        row = jnp.concatenate([flips_ref[b * per + i : b * per + i + 1, :] for i in range(per)], axis=1)
        mixer = (base * (1 - 2 * row).astype(jnp.float32)).astype(jnp.bfloat16)
        values = panel_ref[b * BLOCK : (b + 1) * BLOCK, :]
        high = values.astype(jnp.bfloat16)
        rest = values - high.astype(jnp.float32)
        middle = rest.astype(jnp.bfloat16)
        low = (rest - middle.astype(jnp.float32)).astype(jnp.bfloat16)
        parts = jnp.concatenate([high, middle, low], axis=1)
        out = jnp.dot(mixer, parts, preferred_element_type=jnp.float32)
        held[b] = out[:, :width] + out[:, width : 2 * width] + out[:, 2 * width :]
    strip = 16
    places = [(i, j) for i in range(len(outs)) for j in range(outs[i].shape[0] // BLOCK)]

    def body(step, carry):
        at = pl.multiple_of(step * strip, strip)
        items = [held[b, pl.ds(at, strip), :] for b in range(blocks)]
        apart = 1
        while apart < blocks:
            items = [
                items[b] + items[b ^ apart] if b & apart == 0 else items[b ^ apart] - items[b]
                for b in range(blocks)
            ]
            apart *= 2
        for b in range(blocks):
            which, place = places[b]
            spot = pl.multiple_of(place * BLOCK + at, strip)
            outs[which][pl.ds(spot, strip), :] = items[b] * scale
        return carry

    lax.fori_loop(0, BLOCK // strip, body, 0)


def local_transform(panel, flips, scale, shares):
    rows, width = panel.shape
    return pl.pallas_call(
        functools.partial(local_kernel, scale),
        out_shape=[jax.ShapeDtypeStruct((share, width), jnp.float32) for share in shares],
        in_specs=[pl.BlockSpec(memory_space=pltpu.VMEM)] * 2,
        out_specs=[pl.BlockSpec(memory_space=pltpu.VMEM)] * len(shares),
        scratch_shapes=[pltpu.VMEM((rows // BLOCK, BLOCK, width), jnp.float32)],
        compiler_params=pltpu.CompilerParams(vmem_limit_bytes=32 * 2**20),
    )(flips.reshape(rows // 128, 128), panel)


def launch(value, stage):
    axis, level = stage
    pairs = [(source, source ^ 2**level) for source in range(lax.axis_size(axis))]
    return lax.ppermute(value, axis, pairs), value, stage


def sign_of(stage):
    axis, level = stage
    return (1 - 2 * (lax.axis_index(axis) >> level & 1)).astype(jnp.float32)


def bit_of(stage):
    axis, level = stage
    return 2**level * (lax.axis_size("wide") if axis == "narrow" else 1)


class Chain:
    def __init__(self):
        self.last = ()

    def end(self, sent):
        partner, value, stage = sent
        partner = after(partner, self.last)
        self.last = partner + sign_of(stage) * value
        return self.last

    def begin(self, value, stages):
        for stage in stages[:-1]:
            value = self.end(launch(value, stage))
        return launch(value, stages[-1])


def split(value, parts):
    units = value.shape[0] // 16
    cuts = [16 * (units * i // parts) for i in range(parts + 1)]
    return [value[low:high] for low, high in zip(cuts, cuts[1:])]


def index_kernel(rows_here, most, bases_ref, picks_ref, out_ref):
    picks = picks_ref[...]
    devices, per = picks.shape
    before = lax.broadcasted_iota(jnp.int32, (per, per), 0)
    earlier = before < lax.broadcasted_iota(jnp.int32, (per, per), 1)
    earlier = jnp.where(earlier, 1.0, 0.0).astype(jnp.bfloat16)
    for which in range(out_ref.shape[0]):
        offsets = picks - bases_ref[which]
        owned = (offsets >= 0) & (offsets < rows_here)
        ones = jnp.where(owned, 1.0, 0.0).astype(jnp.bfloat16)
        rank = jnp.dot(ones, earlier, preferred_element_type=jnp.float32)
        rank = jnp.where(owned, rank, -1.0)
        marked = (offsets + 1).astype(jnp.float32)
        for slot in range(most):
            hit = jnp.where(rank == float(slot), marked, 0.0)
            row = jnp.sum(hit, axis=1, keepdims=True).astype(jnp.int32) - 1
            out_ref[which, :, slot : slot + 1] = row


def send_rows(picks, owners, rows_here, devices, most):
    bases = jnp.stack(owners) * rows_here
    rows = pl.pallas_call(
        functools.partial(index_kernel, rows_here, most),
        out_shape=jax.ShapeDtypeStruct((len(owners), devices, most), jnp.int32),
        in_specs=[
            pl.BlockSpec(memory_space=pltpu.SMEM),
            pl.BlockSpec(memory_space=pltpu.VMEM),
        ],
        out_specs=pl.BlockSpec(memory_space=pltpu.VMEM),
        compiler_params=pltpu.CompilerParams(vmem_limit_bytes=8 * 2**20),
    )(bases.astype(jnp.int32), picks.reshape(devices, -1))
    return rows.reshape(len(owners) * devices * most)


def landing(block, rows_here, most):
    owners = block // rows_here
    order = jnp.arange(block.shape[0], dtype=jnp.int32)
    earlier = (owners[:, None] == owners[None, :]) & (order[None, :] < order[:, None])
    return owners * most + jnp.sum(earlier.astype(jnp.int32), axis=1)


def after(value, *others):
    return lax.optimization_barrier((value, others))[0]


def on_device(panel, flips, picks):
    rows_here, width = panel.shape
    narrow, wide = lax.axis_size("narrow"), lax.axis_size("wide")
    devices = narrow * wide
    scale = 1.0 / float(rows_here * devices) ** 0.5
    levels = wide.bit_length() - 1
    far, mid = ("wide", levels - 1), ("wide", levels - 2)
    near = [("narrow", l) for l in range(narrow.bit_length() - 1)]
    near += [("wide", l) for l in range(levels - 2)]
    core, first, second = near[:1], near[1:2], near[2:]

    me = lax.axis_index(AXES)
    per = picks.shape[0] // devices
    most = -(-per // devices)
    cuts = [rows_here * cut // 4 for cut in range(5)]

    c = local_transform(panel, flips, scale, [b - a for a, b in zip(cuts, cuts[1:])])
    chain = Chain()
    core1, core2, core3 = [chain.begin(c[i], core) for i in (1, 2, 3)]
    wanted = send_rows(picks, [me ^ bit_of(far), me ^ bit_of(mid), me], rows_here, devices, most)
    spots = landing(lax.dynamic_slice(picks, (me * per,), (per,)), rows_here, most)
    v1, v2, v3 = chain.end(core1), chain.end(core2), chain.end(core3)
    mid1 = launch(v1, mid)
    far0 = launch(after(c[0], v1), far)
    first2 = chain.begin(v2, first)
    second3 = chain.begin(v3, second)
    chain.last = (chain.last, wanted, spots)
    first1 = chain.begin(chain.end(mid1), first)
    second2 = chain.begin(chain.end(first2), second)
    first3 = chain.begin(chain.end(second3), first)
    core0 = chain.begin(chain.end(far0), core)
    v1 = chain.end(first1)
    v2 = chain.end(second2)
    mid2 = launch(v2, mid)
    far1 = launch(after(v1, v2), far)
    second0 = chain.begin(chain.end(core0), second)
    v3 = chain.end(first3)
    mid3 = launch(v3, mid)
    second1 = chain.begin(chain.end(far1), second)
    v2 = chain.end(mid2)
    far2 = launch(after(v2, v3), far)
    first0 = chain.begin(chain.end(second0), first)
    v0 = chain.end(first0)
    v3 = chain.end(mid3)
    v1 = chain.end(second1)

    held = jnp.concatenate([v0, v1, v2, v3], axis=0)
    taken = jnp.take(held, wanted, axis=0, mode="clip")
    count = devices * most
    rows, filled = wanted[2 * count :], wanted[2 * count :] >= 0
    to_far, to_mid, own = lax.optimization_barrier(
        (taken[:count], taken[count : 2 * count], taken[2 * count :])
    )
    give_mid, give_far = launch(to_mid, mid), launch(to_far, far)
    parts0, parts3 = split(v0, 2), split(v3, 2)
    ends0, ends3 = [], []

    def more(step, gate):
        ends0.append(launch(after(parts0[step], gate), mid))
        ends3.append(launch(after(parts3[step], gate), far))

    got_mid = chain.end((give_mid[0], own, mid))
    v2 = chain.end(far2)
    got_far = chain.end((give_far[0], own, far))
    place = rows[:, None]
    chosen = jnp.where(
        place >= cuts[2], got_far, jnp.where(place < cuts[1], got_mid, own)
    )
    kept = jnp.where(filled[:, None], chosen, 0.0)
    part = lax.dot_general(
        kept, kept, (((0,), (0,)), ((), ())),
        precision=lax.Precision.HIGHEST, preferred_element_type=jnp.float32,
    )
    both = jnp.concatenate(
        [chosen.reshape(devices, most, width), part.reshape(devices, -1, width)], axis=1
    )
    landed = lax.all_to_all(both, AXES, 0, 0, tiled=True)
    more(0, both)
    mine = jnp.sum(landed[:, most:], axis=0) / float(picks.shape[0])
    shared = jnp.broadcast_to(mine[None], (devices,) + mine.shape)
    gram = lax.all_to_all(shared, AXES, 0, 0, tiled=True).reshape(width, width)
    more(1, shared)
    sketch = jnp.take(landed[:, :most].reshape(devices * most, width), spots, axis=0, mode="clip")
    chain.last = (chain.last, landed)
    final0, final3 = [], []
    for step in range(2):
        final0.append(chain.end(ends0[step]))
        final3.append(chain.end(ends3[step]))
        chain.last = (chain.last, gram, sketch)
    mixed = jnp.concatenate(final0 + [v1, v2] + final3, axis=0)
    return (mixed, sketch, gram)


def solution(mesh):
    in_specs = (P(AXES, None), P(AXES), P())
    out_specs = (P(AXES, None), P(AXES, None), P())
    return jax.shard_map(
        on_device, mesh=mesh, in_specs=in_specs, out_specs=out_specs, check_vma=False
    )
```

```python
import functools

import jax
import jax.numpy as jnp
from jax import lax
from jax.experimental import pallas as pl
from jax.experimental.pallas import tpu as pltpu
from jax.sharding import PartitionSpec as P

BLOCK = 256
AXES = ("narrow", "wide")


def signs(order):
    rows = lax.broadcasted_iota(jnp.int32, (order, order), 0)
    both = rows & lax.broadcasted_iota(jnp.int32, (order, order), 1)
    parity = jnp.zeros((order, order), jnp.int32)
    for level in range(order.bit_length() - 1):
        parity = parity ^ (both >> level & 1)
    return (1 - 2 * parity).astype(jnp.float32)


def local_kernel(scale, flips_ref, panel_ref, *refs):
    *outs, flags, held, arrived = refs
    blocks = panel_ref.shape[0] // BLOCK
    width = panel_ref.shape[1]
    per = BLOCK // flips_ref.shape[1]
    loads = [pltpu.make_async_copy(flips_ref, flags, arrived.at[blocks])]
    for b in range(blocks):
        source = panel_ref.at[pl.ds(b * BLOCK, BLOCK), :]
        loads.append(pltpu.make_async_copy(source, held.at[b], arrived.at[b]))
    for load in loads:
        load.start()
    base = signs(BLOCK)
    loads[0].wait()
    for b in range(blocks):
        row = jnp.concatenate([flags[b * per + i : b * per + i + 1, :] for i in range(per)], axis=1)
        mixer = (base * (1 - 2 * row).astype(jnp.float32)).astype(jnp.bfloat16)
        loads[b + 1].wait()
        values = held[b]
        high = values.astype(jnp.bfloat16)
        rest = values - high.astype(jnp.float32)
        middle = rest.astype(jnp.bfloat16)
        low = (rest - middle.astype(jnp.float32)).astype(jnp.bfloat16)
        parts = jnp.concatenate([high, middle, low], axis=1)
        out = jnp.dot(mixer, parts, preferred_element_type=jnp.float32)
        held[b] = out[:, :width] + out[:, width : 2 * width] + out[:, 2 * width :]
    strip = 16
    places = [(i, j) for i in range(len(outs)) for j in range(outs[i].shape[0] // BLOCK)]

    def body(step, carry):
        at = pl.multiple_of(step * strip, strip)
        items = [held[b, pl.ds(at, strip), :] for b in range(blocks)]
        apart = 1
        while apart < blocks:
            items = [
                items[b] + items[b ^ apart] if b & apart == 0 else items[b ^ apart] - items[b]
                for b in range(blocks)
            ]
            apart *= 2
        for b in range(blocks):
            which, place = places[b]
            spot = pl.multiple_of(place * BLOCK + at, strip)
            outs[which][pl.ds(spot, strip), :] = items[b] * scale
        return carry

    lax.fori_loop(0, BLOCK // strip, body, 0)


def local_transform(panel, flips, scale, shares):
    rows, width = panel.shape
    return pl.pallas_call(
        functools.partial(local_kernel, scale),
        out_shape=[jax.ShapeDtypeStruct((share, width), jnp.float32) for share in shares],
        in_specs=[pl.BlockSpec(memory_space=pltpu.HBM)] * 2,
        out_specs=[pl.BlockSpec(memory_space=pltpu.VMEM)] * len(shares),
        scratch_shapes=[
            pltpu.VMEM((rows // 128, 128), jnp.int32),
            pltpu.VMEM((rows // BLOCK, BLOCK, width), jnp.float32),
            pltpu.SemaphoreType.DMA((rows // BLOCK + 1,)),
        ],
        compiler_params=pltpu.CompilerParams(vmem_limit_bytes=60 * 2**20),
    )(flips.reshape(rows // 128, 128), panel)


def launch(value, stage):
    axis, level = stage
    pairs = [(source, source ^ 2**level) for source in range(lax.axis_size(axis))]
    return lax.ppermute(value, axis, pairs), value, stage


def sign_of(stage):
    axis, level = stage
    return (1 - 2 * (lax.axis_index(axis) >> level & 1)).astype(jnp.float32)


def bit_of(stage):
    axis, level = stage
    return 2**level * (lax.axis_size("wide") if axis == "narrow" else 1)


def store_kernel(*refs):
    *values, out_ref, sent = refs
    copies, at = [], 0
    for i, value in enumerate(values):
        rows = value.shape[0]
        copies.append(pltpu.make_async_copy(value, out_ref.at[pl.ds(at, rows), :], sent.at[i]))
        at += rows
    for copy in copies:
        copy.start()
    for copy in copies:
        copy.wait()


def store_rows(values, rows):
    return pl.pallas_call(
        store_kernel,
        out_shape=jax.ShapeDtypeStruct((rows, values[0].shape[1]), jnp.float32),
        in_specs=[pl.BlockSpec(memory_space=pltpu.VMEM)] * len(values),
        out_specs=pl.BlockSpec(memory_space=pl.ANY),
        scratch_shapes=[pltpu.SemaphoreType.DMA((len(values),))],
        compiler_params=pltpu.CompilerParams(vmem_limit_bytes=8 * 2**20),
    )(*values)


def finish_kernel(at, sign_ref, partner_ref, value_ref, whole_ref, out_ref, held, sent):
    del whole_ref
    held[...] = partner_ref[...] + sign_ref[0] * value_ref[...]
    rows = held.shape[0]
    copy = pltpu.make_async_copy(held, out_ref.at[pl.ds(at, rows), :], sent)
    copy.start()
    copy.wait()


def finish(whole, sent, at, *others):
    partner, value, stage = sent
    partner = after(partner, others)
    return pl.pallas_call(
        functools.partial(finish_kernel, at),
        out_shape=jax.ShapeDtypeStruct(whole.shape, jnp.float32),
        in_specs=[pl.BlockSpec(memory_space=pltpu.SMEM)]
        + [pl.BlockSpec(memory_space=pltpu.VMEM)] * 2
        + [pl.BlockSpec(memory_space=pl.ANY)],
        out_specs=pl.BlockSpec(memory_space=pl.ANY),
        scratch_shapes=[pltpu.VMEM(value.shape, jnp.float32), pltpu.SemaphoreType.DMA],
        input_output_aliases={3: 0},
        compiler_params=pltpu.CompilerParams(vmem_limit_bytes=8 * 2**20),
    )(sign_of(stage).reshape(1), partner, value, whole)


class Chain:
    def __init__(self):
        self.last = ()

    def end(self, sent):
        partner, value, stage = sent
        partner = after(partner, self.last)
        self.last = partner + sign_of(stage) * value
        return self.last

    def begin(self, value, stages):
        for stage in stages[:-1]:
            value = self.end(launch(value, stage))
        return launch(value, stages[-1])


def split(value, parts):
    units = value.shape[0] // 16
    cuts = [16 * (units * i // parts) for i in range(parts + 1)]
    return [value[low:high] for low, high in zip(cuts, cuts[1:])]


def index_kernel(rows_here, most, bases_ref, picks_ref, out_ref):
    picks = picks_ref[...]
    devices, per = picks.shape
    before = lax.broadcasted_iota(jnp.int32, (per, per), 0)
    earlier = before < lax.broadcasted_iota(jnp.int32, (per, per), 1)
    earlier = jnp.where(earlier, 1.0, 0.0).astype(jnp.bfloat16)
    for which in range(out_ref.shape[0]):
        offsets = picks - bases_ref[which]
        owned = (offsets >= 0) & (offsets < rows_here)
        ones = jnp.where(owned, 1.0, 0.0).astype(jnp.bfloat16)
        rank = jnp.dot(ones, earlier, preferred_element_type=jnp.float32)
        rank = jnp.where(owned, rank, -1.0)
        marked = (offsets + 1).astype(jnp.float32)
        for slot in range(most):
            hit = jnp.where(rank == float(slot), marked, 0.0)
            row = jnp.sum(hit, axis=1, keepdims=True).astype(jnp.int32) - 1
            out_ref[which, :, slot : slot + 1] = row


def send_rows(picks, owners, rows_here, devices, most):
    bases = jnp.stack(owners) * rows_here
    rows = pl.pallas_call(
        functools.partial(index_kernel, rows_here, most),
        out_shape=jax.ShapeDtypeStruct((len(owners), devices, most), jnp.int32),
        in_specs=[
            pl.BlockSpec(memory_space=pltpu.SMEM),
            pl.BlockSpec(memory_space=pltpu.VMEM),
        ],
        out_specs=pl.BlockSpec(memory_space=pltpu.VMEM),
        compiler_params=pltpu.CompilerParams(vmem_limit_bytes=8 * 2**20),
    )(bases.astype(jnp.int32), picks.reshape(devices, -1))
    return rows.reshape(len(owners) * devices * most)


def landing(block, rows_here, most):
    owners = block // rows_here
    order = jnp.arange(block.shape[0], dtype=jnp.int32)
    earlier = (owners[:, None] == owners[None, :]) & (order[None, :] < order[:, None])
    return owners * most + jnp.sum(earlier.astype(jnp.int32), axis=1)


def after(value, *others):
    return lax.optimization_barrier((value, others))[0]


def on_device(panel, flips, picks):
    rows_here, width = panel.shape
    narrow, wide = lax.axis_size("narrow"), lax.axis_size("wide")
    devices = narrow * wide
    scale = 1.0 / float(rows_here * devices) ** 0.5
    levels = wide.bit_length() - 1
    far, mid = ("wide", levels - 1), ("wide", levels - 2)
    near = [("narrow", l) for l in range(narrow.bit_length() - 1)]
    near += [("wide", l) for l in range(levels - 2)]
    core, first, second = near[:1], near[1:2], near[2:]

    me = lax.axis_index(AXES)
    per = picks.shape[0] // devices
    most = -(-per // devices)
    cuts = [rows_here * cut // 16 for cut in (0, 3, 6, 11, 16)]

    c = local_transform(panel, flips, scale, [b - a for a, b in zip(cuts, cuts[1:])])
    chain = Chain()
    far0, mid1 = launch(c[0], far), launch(c[1], mid)
    core2, core3 = chain.begin(c[2], core), chain.begin(c[3], core)
    wanted = send_rows(picks, [me ^ bit_of(far), me ^ bit_of(mid), me], rows_here, devices, most)
    spots = landing(lax.dynamic_slice(picks, (me * per,), (per,)), rows_here, most)
    first2 = chain.begin(chain.end(core2), first)
    second3 = chain.begin(chain.end(core3), second)
    mid0 = launch(chain.end(far0), mid)
    far1 = launch(chain.end(mid1), far)
    second2 = chain.begin(chain.end(first2), second)
    first3 = chain.begin(chain.end(second3), first)
    v2 = split(chain.end(second2), 2)
    far2 = [launch(part, far) for part in v2]
    v3 = split(chain.end(first3), 2)
    mid3 = [launch(part, mid) for part in v3]
    core0 = chain.begin(chain.end(mid0), core)
    core1 = chain.begin(chain.end(far1), core)
    first0 = chain.begin(chain.end(core0), first)
    second1 = chain.begin(chain.end(core1), second)
    v2, v3 = [chain.end(far2[0])], [chain.end(mid3[0])]
    second0 = chain.begin(chain.end(first0), second)
    first1 = chain.begin(chain.end(second1), first)
    v0, v1 = chain.end(second0), chain.end(first1)
    v2, v3 = v2 + [chain.end(far2[1])], v3 + [chain.end(mid3[1])]
    v2, v3 = jnp.concatenate(v2, axis=0), jnp.concatenate(v3, axis=0)

    held = jnp.concatenate([v0, v1, v2, v3], axis=0)
    taken = jnp.take(held, wanted, axis=0, mode="clip")
    count = devices * most
    rows, filled = wanted[2 * count :], wanted[2 * count :] >= 0
    to_far, to_mid, own = lax.optimization_barrier(
        (taken[:count], taken[count : 2 * count], taken[2 * count :])
    )
    give_mid, give_far = launch(to_mid, mid), launch(to_far, far)
    whole = store_rows([v0, v1], rows_here)
    parts2, parts3 = split(v2, 2), split(v3, 2)
    ends = []

    def more(step, gate):
        ends.append(launch(after(parts2[step], gate), mid))
        ends.append(launch(after(parts3[step], gate), far))

    more(0, to_far)
    got_mid = chain.end((give_mid[0], own, mid))
    got_far = chain.end((give_far[0], own, far))
    place = rows[:, None]
    chosen = jnp.where(
        place >= cuts[3], got_far, jnp.where(place >= cuts[2], got_mid, own)
    )
    kept = jnp.where(filled[:, None], chosen, 0.0)
    part = lax.dot_general(
        kept, kept, (((0,), (0,)), ((), ())),
        precision=lax.Precision.HIGHEST, preferred_element_type=jnp.float32,
    )
    both = jnp.concatenate(
        [chosen.reshape(devices, most, width), part.reshape(devices, -1, width)], axis=1
    )
    landed = lax.all_to_all(both, AXES, 0, 0, tiled=True)
    more(1, both)
    mine = jnp.sum(landed[:, most:], axis=0) / float(picks.shape[0])
    shared = jnp.broadcast_to(mine[None], (devices,) + mine.shape)
    gram = lax.all_to_all(shared, AXES, 0, 0, tiled=True).reshape(width, width)
    sketch = jnp.take(landed[:, :most].reshape(devices * most, width), spots, axis=0, mode="clip")
    half = parts2[0].shape[0]
    whole = finish(whole, ends[0], cuts[2], chain.last, landed)
    whole = finish(whole, ends[1], cuts[3], chain.last, landed)
    whole = finish(whole, ends[2], cuts[2] + half, gram, sketch)
    whole = finish(whole, ends[3], cuts[3] + half, gram, sketch)
    return (whole, sketch, gram)


def solution(mesh):
    in_specs = (P(AXES, None), P(AXES), P())
    out_specs = (P(AXES, None), P(AXES, None), P())
    return jax.shard_map(
        on_device, mesh=mesh, in_specs=in_specs, out_specs=out_specs, check_vma=False
    )
```

```python
import functools

import jax
import jax.numpy as jnp
from jax import lax
from jax.experimental import pallas as pl
from jax.experimental.pallas import tpu as pltpu
from jax.sharding import PartitionSpec as P

BLOCK = 256
AXES = ("narrow", "wide")


def signs(order):
    rows = lax.broadcasted_iota(jnp.int32, (order, order), 0)
    both = rows & lax.broadcasted_iota(jnp.int32, (order, order), 1)
    parity = jnp.zeros((order, order), jnp.int32)
    for level in range(order.bit_length() - 1):
        parity = parity ^ (both >> level & 1)
    return (1 - 2 * parity).astype(jnp.float32)


def local_kernel(scale, flips_ref, panel_ref, *refs):
    *outs, held = refs
    blocks = panel_ref.shape[0] // BLOCK
    width = panel_ref.shape[1]
    lanes = flips_ref.shape[1]
    per = BLOCK // lanes
    base = signs(BLOCK)
    for b in range(blocks):
        row = jnp.concatenate([flips_ref[b * per + i : b * per + i + 1, :] for i in range(per)], axis=1)
        mixer = (base * (1 - 2 * row).astype(jnp.float32)).astype(jnp.bfloat16)
        values = panel_ref[b * BLOCK : (b + 1) * BLOCK, :]
        high = values.astype(jnp.bfloat16)
        rest = values - high.astype(jnp.float32)
        middle = rest.astype(jnp.bfloat16)
        low = (rest - middle.astype(jnp.float32)).astype(jnp.bfloat16)
        parts = jnp.concatenate([high, middle, low], axis=1)
        out = jnp.dot(mixer, parts, preferred_element_type=jnp.float32)
        held[b] = out[:, :width] + out[:, width : 2 * width] + out[:, 2 * width :]
    strip = 16
    places = [(i, j) for i in range(len(outs)) for j in range(outs[i].shape[0] // BLOCK)]

    def body(step, carry):
        at = pl.multiple_of(step * strip, strip)
        items = [held[b, pl.ds(at, strip), :] for b in range(blocks)]
        apart = 1
        while apart < blocks:
            items = [
                items[b] + items[b ^ apart] if b & apart == 0 else items[b ^ apart] - items[b]
                for b in range(blocks)
            ]
            apart *= 2
        for b in range(blocks):
            which, place = places[b]
            spot = pl.multiple_of(place * BLOCK + at, strip)
            outs[which][pl.ds(spot, strip), :] = items[b] * scale
        return carry

    lax.fori_loop(0, BLOCK // strip, body, 0)


def local_transform(panel, flips, scale, shares):
    rows, width = panel.shape
    return pl.pallas_call(
        functools.partial(local_kernel, scale),
        out_shape=[jax.ShapeDtypeStruct((share, width), jnp.float32) for share in shares],
        in_specs=[pl.BlockSpec(memory_space=pltpu.VMEM)] * 2,
        out_specs=[pl.BlockSpec(memory_space=pltpu.VMEM)] * len(shares),
        scratch_shapes=[pltpu.VMEM((rows // BLOCK, BLOCK, width), jnp.float32)],
        compiler_params=pltpu.CompilerParams(vmem_limit_bytes=32 * 2**20),
    )(flips.reshape(rows // 128, 128), panel)


def launch(value, stage):
    axis, level = stage
    pairs = [(source, source ^ 2**level) for source in range(lax.axis_size(axis))]
    return lax.ppermute(value, axis, pairs), value, stage


def sign_of(stage):
    axis, level = stage
    return (1 - 2 * (lax.axis_index(axis) >> level & 1)).astype(jnp.float32)


def bit_of(stage):
    axis, level = stage
    return 2**level * (lax.axis_size("wide") if axis == "narrow" else 1)


def store_kernel(*refs):
    *values, out_ref, sent = refs
    copies, at = [], 0
    for i, value in enumerate(values):
        rows = value.shape[0]
        copies.append(pltpu.make_async_copy(value, out_ref.at[pl.ds(at, rows), :], sent.at[i]))
        at += rows
    for copy in copies:
        copy.start()
    for copy in copies:
        copy.wait()


def store_rows(values, rows):
    return pl.pallas_call(
        store_kernel,
        out_shape=jax.ShapeDtypeStruct((rows, values[0].shape[1]), jnp.float32),
        in_specs=[pl.BlockSpec(memory_space=pltpu.VMEM)] * len(values),
        out_specs=pl.BlockSpec(memory_space=pl.ANY),
        scratch_shapes=[pltpu.SemaphoreType.DMA((len(values),))],
        compiler_params=pltpu.CompilerParams(vmem_limit_bytes=8 * 2**20),
    )(*values)


def finish_kernel(at, sign_ref, partner_ref, value_ref, whole_ref, out_ref, held, sent):
    del whole_ref
    held[...] = partner_ref[...] + sign_ref[0] * value_ref[...]
    rows = held.shape[0]
    copy = pltpu.make_async_copy(held, out_ref.at[pl.ds(at, rows), :], sent)
    copy.start()
    copy.wait()


def finish(whole, sent, at, *others):
    partner, value, stage = sent
    partner = after(partner, others)
    return pl.pallas_call(
        functools.partial(finish_kernel, at),
        out_shape=jax.ShapeDtypeStruct(whole.shape, jnp.float32),
        in_specs=[pl.BlockSpec(memory_space=pltpu.SMEM)]
        + [pl.BlockSpec(memory_space=pltpu.VMEM)] * 2
        + [pl.BlockSpec(memory_space=pl.ANY)],
        out_specs=pl.BlockSpec(memory_space=pl.ANY),
        scratch_shapes=[pltpu.VMEM(value.shape, jnp.float32), pltpu.SemaphoreType.DMA],
        input_output_aliases={3: 0},
        compiler_params=pltpu.CompilerParams(vmem_limit_bytes=8 * 2**20),
    )(sign_of(stage).reshape(1), partner, value, whole)


class Chain:
    def __init__(self):
        self.last = ()

    def end(self, sent):
        partner, value, stage = sent
        partner = after(partner, self.last)
        self.last = partner + sign_of(stage) * value
        return self.last

    def begin(self, value, stages):
        for stage in stages[:-1]:
            value = self.end(launch(value, stage))
        return launch(value, stages[-1])


def index_kernel(rows_here, most, bases_ref, picks_ref, out_ref):
    picks = picks_ref[...]
    devices, per = picks.shape
    before = lax.broadcasted_iota(jnp.int32, (per, per), 0)
    earlier = before < lax.broadcasted_iota(jnp.int32, (per, per), 1)
    earlier = jnp.where(earlier, 1.0, 0.0).astype(jnp.bfloat16)
    for which in range(out_ref.shape[0]):
        offsets = picks - bases_ref[which]
        owned = (offsets >= 0) & (offsets < rows_here)
        ones = jnp.where(owned, 1.0, 0.0).astype(jnp.bfloat16)
        rank = jnp.dot(ones, earlier, preferred_element_type=jnp.float32)
        rank = jnp.where(owned, rank, -1.0)
        marked = (offsets + 1).astype(jnp.float32)
        for slot in range(most):
            hit = jnp.where(rank == float(slot), marked, 0.0)
            row = jnp.sum(hit, axis=1, keepdims=True).astype(jnp.int32) - 1
            out_ref[which, :, slot : slot + 1] = row


def send_rows(picks, owners, rows_here, devices, most):
    bases = jnp.stack(owners) * rows_here
    rows = pl.pallas_call(
        functools.partial(index_kernel, rows_here, most),
        out_shape=jax.ShapeDtypeStruct((len(owners), devices, most), jnp.int32),
        in_specs=[
            pl.BlockSpec(memory_space=pltpu.SMEM),
            pl.BlockSpec(memory_space=pltpu.VMEM),
        ],
        out_specs=pl.BlockSpec(memory_space=pltpu.VMEM),
        compiler_params=pltpu.CompilerParams(vmem_limit_bytes=8 * 2**20),
    )(bases.astype(jnp.int32), picks.reshape(devices, -1))
    return rows.reshape(len(owners) * devices * most)


def landing(block, rows_here, most):
    owners = block // rows_here
    order = jnp.arange(block.shape[0], dtype=jnp.int32)
    earlier = (owners[:, None] == owners[None, :]) & (order[None, :] < order[:, None])
    return owners * most + jnp.sum(earlier.astype(jnp.int32), axis=1)


def after(value, *others):
    return lax.optimization_barrier((value, others))[0]


def on_device(panel, flips, picks):
    rows_here, width = panel.shape
    narrow, wide = lax.axis_size("narrow"), lax.axis_size("wide")
    devices = narrow * wide
    scale = 1.0 / float(rows_here * devices) ** 0.5
    levels = wide.bit_length() - 1
    far, mid = ("wide", levels - 1), ("wide", levels - 2)
    near = [("narrow", l) for l in range(narrow.bit_length() - 1)]
    near += [("wide", l) for l in range(levels - 2)]
    core, first, second = near[:1], near[1:2], near[2:]

    me = lax.axis_index(AXES)
    per = picks.shape[0] // devices
    most = -(-per // devices)
    cuts = [rows_here * cut // 16 for cut in (0, 5, 8, 12, 16)]

    c = local_transform(panel, flips, scale, [b - a for a, b in zip(cuts, cuts[1:])])
    chain = Chain()
    half = cuts[1] // 2
    far0 = [launch(c[0][:half], far), launch(c[0][half:], far)]
    far1 = launch(c[1], far)
    core2, core3 = chain.begin(c[2], core), chain.begin(c[3], core)
    wanted = send_rows(picks, [me], rows_here, devices, most)
    spots = landing(lax.dynamic_slice(picks, (me * per,), (per,)), rows_here, most)
    first2 = chain.begin(chain.end(core2), first)
    mid3 = launch(chain.end(core3), mid)
    v0 = [chain.end(far0[0])]
    second2 = chain.begin(chain.end(first2), second)
    second3 = chain.begin(chain.end(mid3), second)
    mid2 = launch(chain.end(second2), mid)
    v0 = jnp.concatenate(v0 + [chain.end(far0[1])], axis=0)
    core0 = chain.begin(v0, core)
    first3 = chain.begin(chain.end(second3), first)
    second0 = chain.begin(chain.end(core0), second)
    far2 = launch(chain.end(mid2), far)
    far3 = launch(chain.end(first3), far)
    core1 = chain.begin(chain.end(far1), core)
    first0 = chain.begin(chain.end(second0), first)
    mid1 = launch(chain.end(core1), mid)
    mid0 = launch(chain.end(first0), mid)
    second1 = chain.begin(chain.end(mid1), second)
    v2 = chain.end(far2)
    first1 = chain.begin(chain.end(second1), first)
    v0, v1 = chain.end(mid0), chain.end(first1)
    whole = store_rows([v0, v1, v2], rows_here)
    whole = finish(whole, far3, cuts[3], chain.last, wanted, spots)

    filled = wanted >= 0
    chosen = jnp.take(whole, wanted, axis=0, mode="clip")
    kept = jnp.where(filled[:, None], chosen, 0.0)
    part = lax.dot_general(
        kept, kept, (((0,), (0,)), ((), ())),
        precision=lax.Precision.HIGHEST, preferred_element_type=jnp.float32,
    )
    both = jnp.concatenate(
        [chosen.reshape(devices, most, width), part.reshape(devices, -1, width)], axis=1
    )
    landed = lax.all_to_all(both, AXES, 0, 0, tiled=True)
    mine = jnp.sum(landed[:, most:], axis=0) / float(picks.shape[0])
    shared = jnp.broadcast_to(mine[None], (devices,) + mine.shape)
    gram = lax.all_to_all(shared, AXES, 0, 0, tiled=True).reshape(width, width)
    sketch = jnp.take(landed[:, :most].reshape(devices * most, width), spots, axis=0, mode="clip")
    return (whole, sketch, gram)


def solution(mesh):
    in_specs = (P(AXES, None), P(AXES), P())
    out_specs = (P(AXES, None), P(AXES, None), P())
    return jax.shard_map(
        on_device, mesh=mesh, in_specs=in_specs, out_specs=out_specs, check_vma=False
    )
```

```python
import functools

import jax
import jax.numpy as jnp
from jax import lax
from jax.experimental import pallas as pl
from jax.experimental.pallas import tpu as pltpu
from jax.sharding import PartitionSpec as P

BLOCK = 256
AXES = ("narrow", "wide")


def signs(order):
    rows = lax.broadcasted_iota(jnp.int32, (order, order), 0)
    both = rows & lax.broadcasted_iota(jnp.int32, (order, order), 1)
    parity = jnp.zeros((order, order), jnp.int32)
    for level in range(order.bit_length() - 1):
        parity = parity ^ (both >> level & 1)
    return (1 - 2 * parity).astype(jnp.float32)


def local_kernel(scale, flips_ref, panel_ref, *refs):
    *outs, held = refs
    blocks = panel_ref.shape[0] // BLOCK
    width = panel_ref.shape[1]
    lanes = flips_ref.shape[1]
    per = BLOCK // lanes
    base = signs(BLOCK)
    for b in range(blocks):
        row = jnp.concatenate([flips_ref[b * per + i : b * per + i + 1, :] for i in range(per)], axis=1)
        mixer = (base * (1 - 2 * row).astype(jnp.float32)).astype(jnp.bfloat16)
        values = panel_ref[b * BLOCK : (b + 1) * BLOCK, :]
        high = values.astype(jnp.bfloat16)
        rest = values - high.astype(jnp.float32)
        middle = rest.astype(jnp.bfloat16)
        low = (rest - middle.astype(jnp.float32)).astype(jnp.bfloat16)
        parts = jnp.concatenate([high, middle, low], axis=1)
        out = jnp.dot(mixer, parts, preferred_element_type=jnp.float32)
        held[b] = out[:, :width] + out[:, width : 2 * width] + out[:, 2 * width :]
    strip = 16
    places = [(i, j) for i in range(len(outs)) for j in range(outs[i].shape[0] // BLOCK)]

    def body(step, carry):
        at = pl.multiple_of(step * strip, strip)
        items = [held[b, pl.ds(at, strip), :] for b in range(blocks)]
        apart = 1
        while apart < blocks:
            items = [
                items[b] + items[b ^ apart] if b & apart == 0 else items[b ^ apart] - items[b]
                for b in range(blocks)
            ]
            apart *= 2
        for b in range(blocks):
            which, place = places[b]
            spot = pl.multiple_of(place * BLOCK + at, strip)
            outs[which][pl.ds(spot, strip), :] = items[b] * scale
        return carry

    lax.fori_loop(0, BLOCK // strip, body, 0)


def local_transform(panel, flips, scale, shares):
    rows, width = panel.shape
    return pl.pallas_call(
        functools.partial(local_kernel, scale),
        out_shape=[jax.ShapeDtypeStruct((share, width), jnp.float32) for share in shares],
        in_specs=[pl.BlockSpec(memory_space=pltpu.VMEM)] * 2,
        out_specs=[pl.BlockSpec(memory_space=pltpu.VMEM)] * len(shares),
        scratch_shapes=[pltpu.VMEM((rows // BLOCK, BLOCK, width), jnp.float32)],
        compiler_params=pltpu.CompilerParams(vmem_limit_bytes=32 * 2**20),
    )(flips.reshape(rows // 128, 128), panel)


def launch(value, stage):
    axis, level = stage
    pairs = [(source, source ^ 2**level) for source in range(lax.axis_size(axis))]
    return lax.ppermute(value, axis, pairs), value, stage


def sign_of(stage):
    axis, level = stage
    return (1 - 2 * (lax.axis_index(axis) >> level & 1)).astype(jnp.float32)


def store_kernel(at, *refs):
    value_ref, out_ref, sent = refs[0], refs[-2], refs[-1]
    rows = value_ref.shape[0]
    copy = pltpu.make_async_copy(value_ref, out_ref.at[pl.ds(at, rows), :], sent)
    copy.start()
    copy.wait()


def store(whole, value, at, rows):
    operands = [value] if whole is None else [value, whole]
    return pl.pallas_call(
        functools.partial(store_kernel, at),
        out_shape=jax.ShapeDtypeStruct((rows, value.shape[1]), jnp.float32),
        in_specs=[pl.BlockSpec(memory_space=pl.ANY)] * len(operands),
        out_specs=pl.BlockSpec(memory_space=pl.ANY),
        scratch_shapes=[pltpu.SemaphoreType.DMA],
        input_output_aliases={} if whole is None else {1: 0},
    )(*operands)


def turn(value, groups):
    rows, width = value.shape
    value = value.reshape(4, rows // 4, width)
    value = lax.all_to_all(value, "wide", 0, 0, axis_index_groups=groups, tiled=True)
    return value.reshape(rows, width)


def sums_of_four(value):
    rows, width = value.shape
    a, b, c, d = value.reshape(4, rows // 4, width)
    a, b, c, d = a + b, a - b, c + d, c - d
    return jnp.concatenate([a + c, b + d, a - c, b - d], axis=0)


class Chain:
    def __init__(self):
        self.last = ()

    def end(self, sent):
        partner, value, stage = sent
        partner = after(partner, self.last)
        self.last = partner + sign_of(stage) * value
        return self.last

    def begin(self, value, stages):
        for stage in stages[:-1]:
            value = self.end(launch(value, stage))
        return launch(value, stages[-1])


def index_kernel(rows_here, most, bases_ref, picks_ref, out_ref):
    picks = picks_ref[...]
    devices, per = picks.shape
    before = lax.broadcasted_iota(jnp.int32, (per, per), 0)
    earlier = before < lax.broadcasted_iota(jnp.int32, (per, per), 1)
    earlier = jnp.where(earlier, 1.0, 0.0).astype(jnp.bfloat16)
    for which in range(out_ref.shape[0]):
        offsets = picks - bases_ref[which]
        owned = (offsets >= 0) & (offsets < rows_here)
        ones = jnp.where(owned, 1.0, 0.0).astype(jnp.bfloat16)
        rank = jnp.dot(ones, earlier, preferred_element_type=jnp.float32)
        rank = jnp.where(owned, rank, -1.0)
        marked = (offsets + 1).astype(jnp.float32)
        for slot in range(most):
            hit = jnp.where(rank == float(slot), marked, 0.0)
            row = jnp.sum(hit, axis=1, keepdims=True).astype(jnp.int32) - 1
            out_ref[which, :, slot : slot + 1] = row


def send_rows(picks, owners, rows_here, devices, most):
    bases = jnp.stack(owners) * rows_here
    rows = pl.pallas_call(
        functools.partial(index_kernel, rows_here, most),
        out_shape=jax.ShapeDtypeStruct((len(owners), devices, most), jnp.int32),
        in_specs=[
            pl.BlockSpec(memory_space=pltpu.SMEM),
            pl.BlockSpec(memory_space=pltpu.VMEM),
        ],
        out_specs=pl.BlockSpec(memory_space=pltpu.VMEM),
        compiler_params=pltpu.CompilerParams(vmem_limit_bytes=8 * 2**20),
    )(bases.astype(jnp.int32), picks.reshape(devices, -1))
    return rows.reshape(len(owners) * devices * most)


def landing(block, rows_here, most):
    owners = block // rows_here
    order = jnp.arange(block.shape[0], dtype=jnp.int32)
    earlier = (owners[:, None] == owners[None, :]) & (order[None, :] < order[:, None])
    return owners * most + jnp.sum(earlier.astype(jnp.int32), axis=1)


def after(value, *others):
    return lax.optimization_barrier((value, others))[0]


def on_device(panel, flips, picks):
    rows_here, width = panel.shape
    narrow, wide = lax.axis_size("narrow"), lax.axis_size("wide")
    devices = narrow * wide
    scale = 1.0 / float(rows_here * devices) ** 0.5
    levels = wide.bit_length() - 1
    near = [("narrow", l) for l in range(narrow.bit_length() - 1)]
    near += [("wide", l) for l in range(levels - 2)]
    core, first, second = near[:1], near[1:2], near[2:]
    low = wide // 4
    groups = [[place * low + group for place in range(4)] for group in range(low)]

    me = lax.axis_index(AXES)
    per = picks.shape[0] // devices
    most = -(-per // devices)
    count = 4
    size = rows_here // count

    c = local_transform(panel, flips, scale, [size] * count)
    chain = Chain()
    wanted = send_rows(picks, [me], rows_here, devices, most)
    spots = landing(lax.dynamic_slice(picks, (me * per,), (per,)), rows_here, most)
    turned = [turn(value, groups) for value in c]
    sent_core, sent_first, sent_second, back = {}, {}, {}, {}
    whole = None
    for step in range(2 * count):
        if step < count:
            value = sums_of_four(after(turned[step], chain.last))
            chain.last = value
            sent_core[step] = chain.begin(value, core)
        i = step - 1
        if 0 <= i < count:
            sent_second[i] = chain.begin(chain.end(sent_first[i]), second)
        if step < count:
            sent_first[step] = chain.begin(chain.end(sent_core[step]), first)
        i = step - 2
        if 0 <= i < count:
            back[i] = turn(chain.end(sent_second[i]), groups)
        i = step - 4
        if 0 <= i < count:
            whole = store(whole, after(back[i], chain.last), i * size, rows_here)
            chain.last = whole

    filled = wanted >= 0
    chosen = jnp.take(whole, wanted, axis=0, mode="clip")
    kept = jnp.where(filled[:, None], chosen, 0.0)
    part = lax.dot_general(
        kept, kept, (((0,), (0,)), ((), ())),
        precision=lax.Precision.HIGHEST, preferred_element_type=jnp.float32,
    )
    both = jnp.concatenate(
        [chosen.reshape(devices, most, width), part.reshape(devices, -1, width)], axis=1
    )
    landed = lax.all_to_all(both, AXES, 0, 0, tiled=True)
    mine = jnp.sum(landed[:, most:], axis=0) / float(picks.shape[0])
    shared = jnp.broadcast_to(mine[None], (devices,) + mine.shape)
    gram = lax.all_to_all(shared, AXES, 0, 0, tiled=True).reshape(width, width)
    sketch = jnp.take(landed[:, :most].reshape(devices * most, width), spots, axis=0, mode="clip")
    return (whole, sketch, gram)


def solution(mesh):
    in_specs = (P(AXES, None), P(AXES), P())
    out_specs = (P(AXES, None), P(AXES, None), P())
    return jax.shard_map(
        on_device, mesh=mesh, in_specs=in_specs, out_specs=out_specs, check_vma=False
    )
```

```python
import functools

import jax
import jax.numpy as jnp
from jax import lax
from jax.experimental import pallas as pl
from jax.experimental.pallas import tpu as pltpu
from jax.sharding import PartitionSpec as P

BLOCK = 256
AXES = ("narrow", "wide")


def signs(order):
    rows = lax.broadcasted_iota(jnp.int32, (order, order), 0)
    both = rows & lax.broadcasted_iota(jnp.int32, (order, order), 1)
    parity = jnp.zeros((order, order), jnp.int32)
    for level in range(order.bit_length() - 1):
        parity = parity ^ (both >> level & 1)
    return (1 - 2 * parity).astype(jnp.float32)


def local_kernel(scale, turns_ref, flips_ref, panel_ref, *refs):
    *outs, held = refs
    blocks = panel_ref.shape[0] // BLOCK
    width = panel_ref.shape[1]
    lanes = flips_ref.shape[1]
    per = BLOCK // lanes
    base = signs(BLOCK)
    for b in range(blocks):
        row = jnp.concatenate([flips_ref[b * per + i : b * per + i + 1, :] for i in range(per)], axis=1)
        turned = (1 - 2 * row) * turns_ref[b % 4]
        mixer = (base * turned.astype(jnp.float32)).astype(jnp.bfloat16)
        values = panel_ref[b * BLOCK : (b + 1) * BLOCK, :]
        high = values.astype(jnp.bfloat16)
        rest = values - high.astype(jnp.float32)
        middle = rest.astype(jnp.bfloat16)
        low = (rest - middle.astype(jnp.float32)).astype(jnp.bfloat16)
        parts = jnp.concatenate([high, middle, low], axis=1)
        out = jnp.dot(mixer, parts, preferred_element_type=jnp.float32)
        held[b] = out[:, :width] + out[:, width : 2 * width] + out[:, 2 * width :]
    strip = 16
    places = [(i, j) for i in range(len(outs)) for j in range(outs[i].shape[0] // BLOCK)]

    def body(step, carry):
        at = pl.multiple_of(step * strip, strip)
        items = [held[b, pl.ds(at, strip), :] for b in range(blocks)]
        apart = 1
        while apart < blocks:
            items = [
                items[b] + items[b ^ apart] if b & apart == 0 else items[b ^ apart] - items[b]
                for b in range(blocks)
            ]
            apart *= 2
        for b in range(blocks):
            which, place = places[b]
            spot = pl.multiple_of(place * BLOCK + at, strip)
            outs[which][pl.ds(spot, strip), :] = items[b] * scale
        return carry

    lax.fori_loop(0, BLOCK // strip, body, 0)


def local_transform(panel, flips, turns, scale):
    rows, width = panel.shape
    blocks = rows // BLOCK
    return pl.pallas_call(
        functools.partial(local_kernel, scale),
        out_shape=[jax.ShapeDtypeStruct((BLOCK, width), jnp.float32)] * blocks,
        in_specs=[pl.BlockSpec(memory_space=pltpu.SMEM)]
        + [pl.BlockSpec(memory_space=pltpu.VMEM)] * 2,
        out_specs=[pl.BlockSpec(memory_space=pltpu.VMEM)] * blocks,
        scratch_shapes=[pltpu.VMEM((blocks, BLOCK, width), jnp.float32)],
        compiler_params=pltpu.CompilerParams(vmem_limit_bytes=32 * 2**20),
    )(turns, flips.reshape(rows // 128, 128), panel)


def launch(value, stage):
    axis, level = stage
    pairs = [(source, source ^ 2**level) for source in range(lax.axis_size(axis))]
    return lax.ppermute(value, axis, pairs), value, stage


def sign_of(stage):
    axis, level = stage
    return (1 - 2 * (lax.axis_index(axis) >> level & 1)).astype(jnp.float32)


def store_kernel(ats_ref, *refs):
    values, out_ref, sent = refs[:4], refs[-2], refs[-1]
    rows = values[0].shape[0]
    copies = []
    for i, value in enumerate(values):
        at = pl.multiple_of(ats_ref[i], rows)
        copies.append(pltpu.make_async_copy(value, out_ref.at[pl.ds(at, rows), :], sent.at[i]))
    for copy in copies:
        copy.start()
    for copy in copies:
        copy.wait()


def store(whole, values, ats, rows):
    operands = list(values) + ([] if whole is None else [whole])
    kinds = [pltpu.SMEM] + [pltpu.VMEM] * 4 + ([] if whole is None else [pl.ANY])
    return pl.pallas_call(
        store_kernel,
        out_shape=jax.ShapeDtypeStruct((rows, values[0].shape[1]), jnp.float32),
        in_specs=[pl.BlockSpec(memory_space=kind) for kind in kinds],
        out_specs=pl.BlockSpec(memory_space=pl.ANY),
        scratch_shapes=[pltpu.SemaphoreType.DMA((4,))],
        input_output_aliases={} if whole is None else {5: 0},
        compiler_params=pltpu.CompilerParams(vmem_limit_bytes=8 * 2**20),
    )(ats, *operands)


def turn(parts, low):
    size = lax.axis_size("wide")
    sent = [parts[0]]
    for j in (1, 2, 3):
        pairs = [(source, source ^ j * low) for source in range(size)]
        sent.append(lax.ppermute(parts[j], "wide", pairs))
    return sent


def sums_of_four(parts, turns, whole_turn):
    a, b, c, d = [part * turns[k] for k, part in enumerate(parts)]
    a, b, c, d = a + b, a - b, c + d, c - d
    outs = [a + c, b + d, a - c, b - d]
    return jnp.concatenate([out * (turns[j] * whole_turn) for j, out in enumerate(outs)], axis=0)


class Chain:
    def __init__(self):
        self.last = ()

    def end(self, sent):
        partner, value, stage = sent
        partner = after(partner, self.last)
        self.last = partner + sign_of(stage) * value
        return self.last

    def begin(self, value, stages):
        for stage in stages[:-1]:
            value = self.end(launch(value, stage))
        return launch(value, stages[-1])


def index_kernel(rows_here, most, bases_ref, picks_ref, out_ref):
    picks = picks_ref[...]
    devices, per = picks.shape
    before = lax.broadcasted_iota(jnp.int32, (per, per), 0)
    earlier = before < lax.broadcasted_iota(jnp.int32, (per, per), 1)
    earlier = jnp.where(earlier, 1.0, 0.0).astype(jnp.bfloat16)
    for which in range(out_ref.shape[0]):
        offsets = picks - bases_ref[which]
        owned = (offsets >= 0) & (offsets < rows_here)
        ones = jnp.where(owned, 1.0, 0.0).astype(jnp.bfloat16)
        rank = jnp.dot(ones, earlier, preferred_element_type=jnp.float32)
        rank = jnp.where(owned, rank, -1.0)
        marked = (offsets + 1).astype(jnp.float32)
        for slot in range(most):
            hit = jnp.where(rank == float(slot), marked, 0.0)
            row = jnp.sum(hit, axis=1, keepdims=True).astype(jnp.int32) - 1
            out_ref[which, :, slot : slot + 1] = row


def send_rows(picks, owners, rows_here, devices, most):
    bases = jnp.stack(owners) * rows_here
    rows = pl.pallas_call(
        functools.partial(index_kernel, rows_here, most),
        out_shape=jax.ShapeDtypeStruct((len(owners), devices, most), jnp.int32),
        in_specs=[
            pl.BlockSpec(memory_space=pltpu.SMEM),
            pl.BlockSpec(memory_space=pltpu.VMEM),
        ],
        out_specs=pl.BlockSpec(memory_space=pltpu.VMEM),
        compiler_params=pltpu.CompilerParams(vmem_limit_bytes=8 * 2**20),
    )(bases.astype(jnp.int32), picks.reshape(devices, -1))
    return rows.reshape(len(owners) * devices * most)


def landing(block, rows_here, most):
    owners = block // rows_here
    order = jnp.arange(block.shape[0], dtype=jnp.int32)
    earlier = (owners[:, None] == owners[None, :]) & (order[None, :] < order[:, None])
    return owners * most + jnp.sum(earlier.astype(jnp.int32), axis=1)


def after(value, *others):
    return lax.optimization_barrier((value, others))[0]


def on_device(panel, flips, picks):
    rows_here, width = panel.shape
    narrow, wide = lax.axis_size("narrow"), lax.axis_size("wide")
    devices = narrow * wide
    scale = 1.0 / float(rows_here * devices) ** 0.5
    levels = wide.bit_length() - 1
    near = [("narrow", l) for l in range(narrow.bit_length() - 1)]
    near += [("wide", l) for l in range(levels - 2)]
    core, first, second = near[:1], near[1:2], near[2:]
    low = wide // 4
    place = lax.axis_index("wide") // low
    turns = [1 - 2 * ((place & j & 1) ^ ((place & j) >> 1)) for j in range(4)]
    real_turns = [turn_j.astype(jnp.float32) for turn_j in turns]
    whole_turn = real_turns[3]

    me = lax.axis_index(AXES)
    per = picks.shape[0] // devices
    most = -(-per // devices)
    count = rows_here // (4 * BLOCK)

    blocks = local_transform(panel, flips, jnp.stack(turns), scale)
    chain = Chain()
    wanted = send_rows(picks, [me], rows_here, devices, most)
    spots = landing(lax.dynamic_slice(picks, (me * per,), (per,)), rows_here, most)
    away = [turn(blocks[4 * i : 4 * i + 4], low) for i in range(count)]
    sent_core, sent_first, sent_second, back = {}, {}, {}, {}
    whole = None

    def arrive(parts):
        out = lax.optimization_barrier((list(parts), chain.last))[0]
        return out

    for step in range(2 * count):
        if step < count:
            value = sums_of_four(arrive(away[step]), real_turns, whole_turn)
            chain.last = value
            sent_core[step] = chain.begin(value, core)
        i = step - 4
        if 0 <= i < count:
            ats = jnp.stack([((place ^ j) + 4 * i) * BLOCK for j in range(4)])
            whole = store(whole, arrive(back[i]), ats.astype(jnp.int32), rows_here)
            chain.last = whole
        i = step - 1
        if 0 <= i < count:
            sent_second[i] = chain.begin(chain.end(sent_first[i]), second)
        if step < count:
            sent_first[step] = chain.begin(chain.end(sent_core[step]), first)
        i = step - 2
        if 0 <= i < count:
            value = chain.end(sent_second[i])
            back[i] = turn([value[j * BLOCK : (j + 1) * BLOCK] for j in range(4)], low)

    filled = wanted >= 0
    chosen = jnp.take(whole, wanted, axis=0, mode="clip")
    kept = jnp.where(filled[:, None], chosen, 0.0)
    part = lax.dot_general(
        kept, kept, (((0,), (0,)), ((), ())),
        precision=lax.Precision.HIGHEST, preferred_element_type=jnp.float32,
    )
    both = jnp.concatenate(
        [chosen.reshape(devices, most, width), part.reshape(devices, -1, width)], axis=1
    )
    landed = lax.all_to_all(both, AXES, 0, 0, tiled=True)
    mine = jnp.sum(landed[:, most:], axis=0) / float(picks.shape[0])
    shared = jnp.broadcast_to(mine[None], (devices,) + mine.shape)
    gram = lax.all_to_all(shared, AXES, 0, 0, tiled=True).reshape(width, width)
    sketch = jnp.take(landed[:, :most].reshape(devices * most, width), spots, axis=0, mode="clip")
    return (whole, sketch, gram)


def solution(mesh):
    in_specs = (P(AXES, None), P(AXES), P())
    out_specs = (P(AXES, None), P(AXES, None), P())
    return jax.shard_map(
        on_device, mesh=mesh, in_specs=in_specs, out_specs=out_specs, check_vma=False
    )
```

```python
import functools

import jax
import jax.numpy as jnp
from jax import lax
from jax.experimental import pallas as pl
from jax.experimental.pallas import tpu as pltpu
from jax.sharding import PartitionSpec as P

BLOCK = 256
AXES = ("narrow", "wide")


def signs(order):
    rows = lax.broadcasted_iota(jnp.int32, (order, order), 0)
    both = rows & lax.broadcasted_iota(jnp.int32, (order, order), 1)
    parity = jnp.zeros((order, order), jnp.int32)
    for level in range(order.bit_length() - 1):
        parity = parity ^ (both >> level & 1)
    return (1 - 2 * parity).astype(jnp.float32)


def local_kernel(scale, turns_ref, flips_ref, panel_ref, *refs):
    *outs, held = refs
    blocks = panel_ref.shape[0] // BLOCK
    width = panel_ref.shape[1]
    lanes = flips_ref.shape[1]
    per = BLOCK // lanes
    base = signs(BLOCK)
    for b in range(blocks):
        row = jnp.concatenate([flips_ref[b * per + i : b * per + i + 1, :] for i in range(per)], axis=1)
        turned = (1 - 2 * row) * turns_ref[b % 4]
        mixer = (base * turned.astype(jnp.float32)).astype(jnp.bfloat16)
        values = panel_ref[b * BLOCK : (b + 1) * BLOCK, :]
        high = values.astype(jnp.bfloat16)
        rest = values - high.astype(jnp.float32)
        middle = rest.astype(jnp.bfloat16)
        low = (rest - middle.astype(jnp.float32)).astype(jnp.bfloat16)
        parts = jnp.concatenate([high, middle, low], axis=1)
        out = jnp.dot(mixer, parts, preferred_element_type=jnp.float32)
        held[b] = out[:, :width] + out[:, width : 2 * width] + out[:, 2 * width :]
    strip = 16
    places = [(i, j) for i in range(len(outs)) for j in range(outs[i].shape[0] // BLOCK)]

    def body(step, carry):
        at = pl.multiple_of(step * strip, strip)
        items = [held[b, pl.ds(at, strip), :] for b in range(blocks)]
        apart = 1
        while apart < blocks:
            items = [
                items[b] + items[b ^ apart] if b & apart == 0 else items[b ^ apart] - items[b]
                for b in range(blocks)
            ]
            apart *= 2
        for b in range(blocks):
            which, place = places[b]
            spot = pl.multiple_of(place * BLOCK + at, strip)
            outs[which][pl.ds(spot, strip), :] = items[b] * scale
        return carry

    lax.fori_loop(0, BLOCK // strip, body, 0)


def local_transform(panel, flips, turns, scale):
    rows, width = panel.shape
    blocks = rows // BLOCK
    return pl.pallas_call(
        functools.partial(local_kernel, scale),
        out_shape=[jax.ShapeDtypeStruct((BLOCK, width), jnp.float32)] * 4
        + [jax.ShapeDtypeStruct((rows - 4 * BLOCK, width), jnp.float32)],
        in_specs=[pl.BlockSpec(memory_space=pltpu.SMEM)]
        + [pl.BlockSpec(memory_space=pltpu.VMEM)] * 2,
        out_specs=[pl.BlockSpec(memory_space=pltpu.VMEM)] * 5,
        scratch_shapes=[pltpu.VMEM((blocks, BLOCK, width), jnp.float32)],
        compiler_params=pltpu.CompilerParams(vmem_limit_bytes=32 * 2**20),
    )(turns, flips.reshape(rows // 128, 128), panel)


def launch(value, stage):
    axis, level = stage
    pairs = [(source, source ^ 2**level) for source in range(lax.axis_size(axis))]
    return lax.ppermute(value, axis, pairs), value, stage


def sign_of(stage):
    axis, level = stage
    return (1 - 2 * (lax.axis_index(axis) >> level & 1)).astype(jnp.float32)


def store_kernel(ats_ref, *refs):
    values, out_ref, sent = refs[:4], refs[-2], refs[-1]
    rows = values[0].shape[0]
    copies = []
    for i, value in enumerate(values):
        at = pl.multiple_of(ats_ref[i], rows)
        copies.append(pltpu.make_async_copy(value, out_ref.at[pl.ds(at, rows), :], sent.at[i]))
    for copy in copies:
        copy.start()
    for copy in copies:
        copy.wait()


def store(whole, values, ats, rows):
    operands = list(values) + ([] if whole is None else [whole])
    kinds = [pltpu.SMEM] + [pltpu.VMEM] * 4 + ([] if whole is None else [pl.ANY])
    return pl.pallas_call(
        store_kernel,
        out_shape=jax.ShapeDtypeStruct((rows, values[0].shape[1]), jnp.float32),
        in_specs=[pl.BlockSpec(memory_space=kind) for kind in kinds],
        out_specs=pl.BlockSpec(memory_space=pl.ANY),
        scratch_shapes=[pltpu.SemaphoreType.DMA((4,))],
        input_output_aliases={} if whole is None else {5: 0},
        compiler_params=pltpu.CompilerParams(vmem_limit_bytes=8 * 2**20),
    )(ats, *operands)


def turn(parts, low):
    size = lax.axis_size("wide")
    sent = {0: parts[0]}
    for j in (3, 2, 1):
        pairs = [(source, source ^ j * low) for source in range(size)]
        sent[j] = lax.ppermute(parts[j], "wide", pairs)
    return [sent[j] for j in range(4)]


def sums_of_four(parts, turns, whole_turn):
    a, b, c, d = [part * turns[k] for k, part in enumerate(parts)]
    a, b, c, d = a + b, a - b, c + d, c - d
    outs = [a + c, b + d, a - c, b - d]
    return jnp.concatenate([out * (turns[j] * whole_turn) for j, out in enumerate(outs)], axis=0)


class Chain:
    def __init__(self):
        self.last = ()

    def end(self, sent):
        partner, value, stage = sent
        partner = after(partner, self.last)
        self.last = partner + sign_of(stage) * value
        return self.last

    def begin(self, value, stages):
        for stage in stages[:-1]:
            value = self.end(launch(value, stage))
        return launch(value, stages[-1])


def index_kernel(rows_here, most, bases_ref, picks_ref, out_ref):
    picks = picks_ref[...]
    devices, per = picks.shape
    before = lax.broadcasted_iota(jnp.int32, (per, per), 0)
    earlier = before < lax.broadcasted_iota(jnp.int32, (per, per), 1)
    earlier = jnp.where(earlier, 1.0, 0.0).astype(jnp.bfloat16)
    for which in range(out_ref.shape[0]):
        offsets = picks - bases_ref[which]
        owned = (offsets >= 0) & (offsets < rows_here)
        ones = jnp.where(owned, 1.0, 0.0).astype(jnp.bfloat16)
        rank = jnp.dot(ones, earlier, preferred_element_type=jnp.float32)
        rank = jnp.where(owned, rank, -1.0)
        marked = (offsets + 1).astype(jnp.float32)
        for slot in range(most):
            hit = jnp.where(rank == float(slot), marked, 0.0)
            row = jnp.sum(hit, axis=1, keepdims=True).astype(jnp.int32) - 1
            out_ref[which, :, slot : slot + 1] = row


def send_rows(picks, owners, rows_here, devices, most):
    bases = jnp.stack(owners) * rows_here
    rows = pl.pallas_call(
        functools.partial(index_kernel, rows_here, most),
        out_shape=jax.ShapeDtypeStruct((len(owners), devices, most), jnp.int32),
        in_specs=[
            pl.BlockSpec(memory_space=pltpu.SMEM),
            pl.BlockSpec(memory_space=pltpu.VMEM),
        ],
        out_specs=pl.BlockSpec(memory_space=pltpu.VMEM),
        compiler_params=pltpu.CompilerParams(vmem_limit_bytes=8 * 2**20),
    )(bases.astype(jnp.int32), picks.reshape(devices, -1))
    return rows.reshape(len(owners) * devices * most)


def landing(block, rows_here, most):
    owners = block // rows_here
    order = jnp.arange(block.shape[0], dtype=jnp.int32)
    earlier = (owners[:, None] == owners[None, :]) & (order[None, :] < order[:, None])
    return owners * most + jnp.sum(earlier.astype(jnp.int32), axis=1)


def after(value, *others):
    return lax.optimization_barrier((value, others))[0]


def on_device(panel, flips, picks):
    rows_here, width = panel.shape
    narrow, wide = lax.axis_size("narrow"), lax.axis_size("wide")
    devices = narrow * wide
    scale = 1.0 / float(rows_here * devices) ** 0.5
    levels = wide.bit_length() - 1
    near = [("narrow", l) for l in range(narrow.bit_length() - 1)]
    near += [("wide", l) for l in range(levels - 2)]
    core, first, second = near[:1], near[1:2], near[2:]
    low = wide // 4
    place = lax.axis_index("wide") // low
    turns = [1 - 2 * ((place & j & 1) ^ ((place & j) >> 1)) for j in range(4)]
    real_turns = [turn_j.astype(jnp.float32) for turn_j in turns]
    whole_turn = real_turns[3]

    me = lax.axis_index(AXES)
    per = picks.shape[0] // devices
    most = -(-per // devices)
    count = rows_here // (4 * BLOCK)

    *chunk, rest = local_transform(panel, flips, jnp.stack(turns), scale)
    chain = Chain()

    def pieces(value):
        return [value[j * BLOCK : (j + 1) * BLOCK] for j in range(value.shape[0] // BLOCK)]

    def arrive(parts):
        return lax.optimization_barrier((list(parts), chain.last))[0]

    def gather_z(parts):
        chain.last = sums_of_four(arrive(parts), real_turns, whole_turn)
        return chain.last

    away = [turn(chunk, low)]
    sent_rest = chain.begin(rest, core)
    wanted = send_rows(picks, [me], rows_here, devices, most)
    spots = landing(lax.dynamic_slice(picks, (me * per,), (per,)), rows_here, most)
    rest = pieces(chain.end(sent_rest))
    away += [turn(rest[4 * i : 4 * i + 4], low) for i in range(count - 1)]

    back, one, two = {}, {}, {}
    whole = None

    def keep(i):
        nonlocal whole
        ats = jnp.stack([((place ^ j) + 4 * i) * BLOCK for j in range(4)])
        back[i] = arrive(back[i])
        whole = store(whole, back[i], ats.astype(jnp.int32), rows_here)
        chain.last = whole

    one[0] = chain.begin(gather_z(away[0]), first)
    one[1] = chain.begin(gather_z(away[1]), first)
    two[0] = chain.begin(chain.end(one[0]), second)
    one[2] = chain.begin(gather_z(away[2]), first)
    chain.last = (chain.last, wanted, spots)
    two[1] = chain.begin(chain.end(one[1]), second)
    sent0 = chain.begin(chain.end(two[0]), core)
    one[3] = chain.begin(gather_z(away[3]), first)
    back[0] = turn(pieces(chain.end(sent0)), low)
    two[2] = chain.begin(chain.end(one[2]), second)
    keep(0)
    back[1] = turn(pieces(chain.end(two[1])), low)
    two[3] = chain.begin(chain.end(one[3]), second)
    back[2] = turn(pieces(chain.end(two[2])), low)
    keep(1)
    back[3] = turn(pieces(chain.end(two[3])), low)
    keep(2)
    keep(3)

    filled = wanted >= 0
    held = jnp.concatenate([part for i in range(count) for part in back[i]], axis=0)
    chosen = jnp.take(held, wanted ^ place * BLOCK, axis=0, mode="clip")
    kept = jnp.where(filled[:, None], chosen, 0.0)
    part = lax.dot_general(
        kept, kept, (((0,), (0,)), ((), ())),
        precision=lax.Precision.HIGHEST, preferred_element_type=jnp.float32,
    )
    both = jnp.concatenate(
        [chosen.reshape(devices, most, width), part.reshape(devices, -1, width)], axis=1
    )
    landed = lax.all_to_all(both, AXES, 0, 0, tiled=True)
    mine = jnp.sum(landed[:, most:], axis=0) / float(picks.shape[0])
    shared = jnp.broadcast_to(mine[None], (devices,) + mine.shape)
    gram = lax.all_to_all(shared, AXES, 0, 0, tiled=True).reshape(width, width)
    sketch = jnp.take(landed[:, :most].reshape(devices * most, width), spots, axis=0, mode="clip")
    return (whole, sketch, gram)


def solution(mesh):
    in_specs = (P(AXES, None), P(AXES), P())
    out_specs = (P(AXES, None), P(AXES, None), P())
    return jax.shard_map(
        on_device, mesh=mesh, in_specs=in_specs, out_specs=out_specs, check_vma=False
    )
```

```python
import functools

import jax
import jax.numpy as jnp
from jax import lax
from jax.experimental import pallas as pl
from jax.experimental.pallas import tpu as pltpu
from jax.sharding import PartitionSpec as P

BLOCK = 256
AXES = ("narrow", "wide")


def signs(order):
    rows = lax.broadcasted_iota(jnp.int32, (order, order), 0)
    both = rows & lax.broadcasted_iota(jnp.int32, (order, order), 1)
    parity = jnp.zeros((order, order), jnp.int32)
    for level in range(order.bit_length() - 1):
        parity = parity ^ (both >> level & 1)
    return (1 - 2 * parity).astype(jnp.float32)


def local_kernel(scale, flips_ref, panel_ref, *refs):
    *outs, held = refs
    blocks = panel_ref.shape[0] // BLOCK
    width = panel_ref.shape[1]
    lanes = flips_ref.shape[1]
    per = BLOCK // lanes
    base = signs(BLOCK)
    for b in range(blocks):
        row = jnp.concatenate([flips_ref[b * per + i : b * per + i + 1, :] for i in range(per)], axis=1)
        mixer = (base * (1 - 2 * row).astype(jnp.float32)).astype(jnp.bfloat16)
        values = panel_ref[b * BLOCK : (b + 1) * BLOCK, :]
        high = values.astype(jnp.bfloat16)
        rest = values - high.astype(jnp.float32)
        middle = rest.astype(jnp.bfloat16)
        low = (rest - middle.astype(jnp.float32)).astype(jnp.bfloat16)
        parts = jnp.concatenate([high, middle, low], axis=1)
        out = jnp.dot(mixer, parts, preferred_element_type=jnp.float32)
        held[b] = out[:, :width] + out[:, width : 2 * width] + out[:, 2 * width :]
    strip = 16
    places = [(i, j) for i in range(len(outs)) for j in range(outs[i].shape[0] // BLOCK)]

    def body(step, carry):
        at = pl.multiple_of(step * strip, strip)
        items = [held[b, pl.ds(at, strip), :] for b in range(blocks)]
        apart = 1
        while apart < blocks:
            items = [
                items[b] + items[b ^ apart] if b & apart == 0 else items[b ^ apart] - items[b]
                for b in range(blocks)
            ]
            apart *= 2
        for b in range(blocks):
            which, place = places[b]
            spot = pl.multiple_of(place * BLOCK + at, strip)
            outs[which][pl.ds(spot, strip), :] = items[b] * scale
        return carry

    lax.fori_loop(0, BLOCK // strip, body, 0)


def local_transform(panel, flips, scale, shares):
    rows, width = panel.shape
    return pl.pallas_call(
        functools.partial(local_kernel, scale),
        out_shape=[jax.ShapeDtypeStruct((share, width), jnp.float32) for share in shares],
        in_specs=[pl.BlockSpec(memory_space=pltpu.VMEM)] * 2,
        out_specs=[pl.BlockSpec(memory_space=pltpu.VMEM)] * len(shares),
        scratch_shapes=[pltpu.VMEM((rows // BLOCK, BLOCK, width), jnp.float32)],
        compiler_params=pltpu.CompilerParams(vmem_limit_bytes=32 * 2**20),
    )(flips.reshape(rows // 128, 128), panel)


def device_kernel(in_ref, out_ref):
    devices, rows, _ = in_ref.shape
    strip = 8

    def body(step, carry):
        at = pl.multiple_of(step * strip, strip)
        items = [in_ref[d, pl.ds(at, strip), :] for d in range(devices)]
        apart = 1
        while apart < devices:
            items = [
                items[d] + items[d ^ apart] if d & apart == 0 else items[d ^ apart] - items[d]
                for d in range(devices)
            ]
            apart *= 2
        for d in range(devices):
            out_ref[d, pl.ds(at, strip), :] = items[d]
        return carry

    lax.fori_loop(0, rows // strip, body, 0)


def device_sums(value):
    return pl.pallas_call(
        device_kernel,
        out_shape=jax.ShapeDtypeStruct(value.shape, jnp.float32),
        in_specs=[pl.BlockSpec(memory_space=pltpu.VMEM)],
        out_specs=pl.BlockSpec(memory_space=pltpu.VMEM),
        compiler_params=pltpu.CompilerParams(vmem_limit_bytes=32 * 2**20),
    )(value)


def index_kernel(rows_here, most, bases_ref, picks_ref, out_ref):
    picks = picks_ref[...]
    devices, per = picks.shape
    before = lax.broadcasted_iota(jnp.int32, (per, per), 0)
    earlier = before < lax.broadcasted_iota(jnp.int32, (per, per), 1)
    earlier = jnp.where(earlier, 1.0, 0.0).astype(jnp.bfloat16)
    for which in range(out_ref.shape[0]):
        offsets = picks - bases_ref[which]
        owned = (offsets >= 0) & (offsets < rows_here)
        ones = jnp.where(owned, 1.0, 0.0).astype(jnp.bfloat16)
        rank = jnp.dot(ones, earlier, preferred_element_type=jnp.float32)
        rank = jnp.where(owned, rank, -1.0)
        marked = (offsets + 1).astype(jnp.float32)
        for slot in range(most):
            hit = jnp.where(rank == float(slot), marked, 0.0)
            row = jnp.sum(hit, axis=1, keepdims=True).astype(jnp.int32) - 1
            out_ref[which, :, slot : slot + 1] = row


def send_rows(picks, owners, rows_here, devices, most):
    bases = jnp.stack(owners) * rows_here
    rows = pl.pallas_call(
        functools.partial(index_kernel, rows_here, most),
        out_shape=jax.ShapeDtypeStruct((len(owners), devices, most), jnp.int32),
        in_specs=[
            pl.BlockSpec(memory_space=pltpu.SMEM),
            pl.BlockSpec(memory_space=pltpu.VMEM),
        ],
        out_specs=pl.BlockSpec(memory_space=pltpu.VMEM),
        compiler_params=pltpu.CompilerParams(vmem_limit_bytes=8 * 2**20),
    )(bases.astype(jnp.int32), picks.reshape(devices, -1))
    return rows.reshape(len(owners) * devices * most)


def landing(block, rows_here, most):
    owners = block // rows_here
    order = jnp.arange(block.shape[0], dtype=jnp.int32)
    earlier = (owners[:, None] == owners[None, :]) & (order[None, :] < order[:, None])
    return owners * most + jnp.sum(earlier.astype(jnp.int32), axis=1)


def on_device(panel, flips, picks):
    rows_here, width = panel.shape
    devices = lax.axis_size("narrow") * lax.axis_size("wide")
    scale = 1.0 / float(rows_here * devices) ** 0.5
    me = lax.axis_index(AXES)
    per = picks.shape[0] // devices
    most = -(-per // devices)

    local = local_transform(panel, flips, scale, [rows_here])[0]
    local = local.reshape(devices, rows_here // devices, width)
    wanted = send_rows(picks, [me], rows_here, devices, most)
    spots = landing(lax.dynamic_slice(picks, (me * per,), (per,)), rows_here, most)
    slices = lax.all_to_all(local, AXES, 0, 0, tiled=True)
    slices, wanted, spots = lax.optimization_barrier((slices, wanted, spots))
    mixed = lax.all_to_all(device_sums(slices), AXES, 0, 0, tiled=True)
    whole = mixed.reshape(rows_here, width)

    filled = wanted >= 0
    chosen = jnp.take(whole, wanted, axis=0, mode="clip")
    kept = jnp.where(filled[:, None], chosen, 0.0)
    part = lax.dot_general(
        kept, kept, (((0,), (0,)), ((), ())),
        precision=lax.Precision.HIGHEST, preferred_element_type=jnp.float32,
    )
    both = jnp.concatenate(
        [chosen.reshape(devices, most, width), part.reshape(devices, -1, width)], axis=1
    )
    landed = lax.all_to_all(both, AXES, 0, 0, tiled=True)
    mine = jnp.sum(landed[:, most:], axis=0) / float(picks.shape[0])
    shared = jnp.broadcast_to(mine[None], (devices,) + mine.shape)
    gram = lax.all_to_all(shared, AXES, 0, 0, tiled=True).reshape(width, width)
    sketch = jnp.take(landed[:, :most].reshape(devices * most, width), spots, axis=0, mode="clip")
    return (whole, sketch, gram)


def solution(mesh):
    in_specs = (P(AXES, None), P(AXES), P())
    out_specs = (P(AXES, None), P(AXES, None), P())
    return jax.shard_map(
        on_device, mesh=mesh, in_specs=in_specs, out_specs=out_specs, check_vma=False
    )
```

```python
import functools

import jax
import jax.numpy as jnp
from jax import lax
from jax.experimental import pallas as pl
from jax.experimental.pallas import tpu as pltpu
from jax.sharding import PartitionSpec as P

BLOCK = 256
AXES = ("narrow", "wide")


def signs(order):
    rows = lax.broadcasted_iota(jnp.int32, (order, order), 0)
    both = rows & lax.broadcasted_iota(jnp.int32, (order, order), 1)
    parity = jnp.zeros((order, order), jnp.int32)
    for level in range(order.bit_length() - 1):
        parity = parity ^ (both >> level & 1)
    return (1 - 2 * parity).astype(jnp.float32)


def local_kernel(scale, flips_ref, panel_ref, *refs):
    *outs, held = refs
    blocks = panel_ref.shape[0] // BLOCK
    width = panel_ref.shape[1]
    lanes = flips_ref.shape[1]
    per = BLOCK // lanes
    base = signs(BLOCK)
    for b in range(blocks):
        row = jnp.concatenate([flips_ref[b * per + i : b * per + i + 1, :] for i in range(per)], axis=1)
        mixer = (base * (1 - 2 * row).astype(jnp.float32)).astype(jnp.bfloat16)
        values = panel_ref[b * BLOCK : (b + 1) * BLOCK, :]
        high = values.astype(jnp.bfloat16)
        rest = values - high.astype(jnp.float32)
        middle = rest.astype(jnp.bfloat16)
        low = (rest - middle.astype(jnp.float32)).astype(jnp.bfloat16)
        parts = jnp.concatenate([high, middle, low], axis=1)
        out = jnp.dot(mixer, parts, preferred_element_type=jnp.float32)
        held[b] = out[:, :width] + out[:, width : 2 * width] + out[:, 2 * width :]
    strip = 16
    places = [(i, j) for i in range(len(outs)) for j in range(outs[i].shape[0] // BLOCK)]

    def body(step, carry):
        at = pl.multiple_of(step * strip, strip)
        items = [held[b, pl.ds(at, strip), :] for b in range(blocks)]
        apart = 1
        while apart < blocks:
            items = [
                items[b] + items[b ^ apart] if b & apart == 0 else items[b ^ apart] - items[b]
                for b in range(blocks)
            ]
            apart *= 2
        for b in range(blocks):
            which, place = places[b]
            spot = pl.multiple_of(place * BLOCK + at, strip)
            outs[which][pl.ds(spot, strip), :] = items[b] * scale
        return carry

    lax.fori_loop(0, BLOCK // strip, body, 0)


def local_transform(panel, flips, scale, shares):
    rows, width = panel.shape
    return pl.pallas_call(
        functools.partial(local_kernel, scale),
        out_shape=[jax.ShapeDtypeStruct((share, width), jnp.float32) for share in shares],
        in_specs=[pl.BlockSpec(memory_space=pltpu.VMEM)] * 2,
        out_specs=[pl.BlockSpec(memory_space=pltpu.VMEM)] * len(shares),
        scratch_shapes=[pltpu.VMEM((rows // BLOCK, BLOCK, width), jnp.float32)],
        compiler_params=pltpu.CompilerParams(vmem_limit_bytes=32 * 2**20),
    )(flips.reshape(rows // 128, 128), panel)


def device_kernel(in_ref, out_ref):
    devices, rows, _ = in_ref.shape
    strip = 8

    def body(step, carry):
        at = pl.multiple_of(step * strip, strip)
        items = [in_ref[d, pl.ds(at, strip), :] for d in range(devices)]
        apart = 1
        while apart < devices:
            items = [
                items[d] + items[d ^ apart] if d & apart == 0 else items[d ^ apart] - items[d]
                for d in range(devices)
            ]
            apart *= 2
        for d in range(devices):
            out_ref[d, pl.ds(at, strip), :] = items[d]
        return carry

    lax.fori_loop(0, rows // strip, body, 0)


def device_sums(value):
    return pl.pallas_call(
        device_kernel,
        out_shape=jax.ShapeDtypeStruct(value.shape, jnp.float32),
        in_specs=[pl.BlockSpec(memory_space=pltpu.VMEM)],
        out_specs=pl.BlockSpec(memory_space=pltpu.VMEM),
        compiler_params=pltpu.CompilerParams(vmem_limit_bytes=32 * 2**20),
    )(value)


def index_kernel(rows_here, most, bases_ref, picks_ref, out_ref):
    picks = picks_ref[...]
    devices, per = picks.shape
    before = lax.broadcasted_iota(jnp.int32, (per, per), 0)
    earlier = before < lax.broadcasted_iota(jnp.int32, (per, per), 1)
    earlier = jnp.where(earlier, 1.0, 0.0).astype(jnp.bfloat16)
    for which in range(out_ref.shape[0]):
        offsets = picks - bases_ref[which]
        owned = (offsets >= 0) & (offsets < rows_here)
        ones = jnp.where(owned, 1.0, 0.0).astype(jnp.bfloat16)
        rank = jnp.dot(ones, earlier, preferred_element_type=jnp.float32)
        rank = jnp.where(owned, rank, -1.0)
        marked = (offsets + 1).astype(jnp.float32)
        for slot in range(most):
            hit = jnp.where(rank == float(slot), marked, 0.0)
            row = jnp.sum(hit, axis=1, keepdims=True).astype(jnp.int32) - 1
            out_ref[which, :, slot : slot + 1] = row


def send_rows(picks, owners, rows_here, devices, most):
    bases = jnp.stack(owners) * rows_here
    rows = pl.pallas_call(
        functools.partial(index_kernel, rows_here, most),
        out_shape=jax.ShapeDtypeStruct((len(owners), devices, most), jnp.int32),
        in_specs=[
            pl.BlockSpec(memory_space=pltpu.SMEM),
            pl.BlockSpec(memory_space=pltpu.VMEM),
        ],
        out_specs=pl.BlockSpec(memory_space=pltpu.VMEM),
        compiler_params=pltpu.CompilerParams(vmem_limit_bytes=8 * 2**20),
    )(bases.astype(jnp.int32), picks.reshape(devices, -1))
    return rows.reshape(len(owners) * devices * most)


def count_kernel(rows_here, me_ref, picks_ref, out_ref):
    picks = picks_ref[...]
    rows, devices = out_ref.shape
    owner = picks >> rows_here.bit_length() - 1
    local = picks & rows_here - 1
    held = local >> rows.bit_length() - 1 == me_ref[0]
    place = jnp.where(held, local & rows - 1, -1)
    shape = (devices, picks.shape[1])
    owners = jnp.where(lax.broadcasted_iota(jnp.int32, shape, 0) == owner, 1.0, 0.0)
    shape = (rows, picks.shape[1])
    places = jnp.where(lax.broadcasted_iota(jnp.int32, shape, 0) == place, 1.0, 0.0)
    out_ref[...] = lax.dot_general(
        places.astype(jnp.bfloat16),
        owners.astype(jnp.bfloat16),
        (((1,), (1,)), ((), ())),
        preferred_element_type=jnp.float32,
    )


def count_picks(picks, me, rows_here, devices):
    return pl.pallas_call(
        functools.partial(count_kernel, rows_here),
        out_shape=jax.ShapeDtypeStruct((rows_here // devices, devices), jnp.float32),
        in_specs=[
            pl.BlockSpec(memory_space=pltpu.SMEM),
            pl.BlockSpec(memory_space=pltpu.VMEM),
        ],
        out_specs=pl.BlockSpec(memory_space=pltpu.VMEM),
        compiler_params=pltpu.CompilerParams(vmem_limit_bytes=32 * 2**20),
    )(me.reshape(1).astype(jnp.int32), picks.reshape(1, -1))


def part_kernel(counts_ref, held_ref, out_ref):
    devices, _, width = held_ref.shape
    total = jnp.zeros((width, width), jnp.float32)
    for d in range(devices):
        rows = held_ref[d]
        total = total + lax.dot_general(
            rows,
            rows * counts_ref[:, d : d + 1],
            (((0,), (0,)), ((), ())),
            precision=lax.Precision.HIGHEST,
            preferred_element_type=jnp.float32,
        )
    out_ref[...] = total


def gram_part(counts, held):
    width = held.shape[2]
    return pl.pallas_call(
        part_kernel,
        out_shape=jax.ShapeDtypeStruct((width, width), jnp.float32),
        in_specs=[pl.BlockSpec(memory_space=pltpu.VMEM)] * 2,
        out_specs=pl.BlockSpec(memory_space=pltpu.VMEM),
        compiler_params=pltpu.CompilerParams(vmem_limit_bytes=32 * 2**20),
    )(counts, held)


def sum_over_devices(value):
    for axis in AXES:
        size = lax.axis_size(axis)
        for level in range(size.bit_length() - 1):
            pairs = [(source, source ^ 2**level) for source in range(size)]
            value = value + lax.ppermute(value, axis, pairs)
    return value


def landing(block, rows_here, most):
    owners = block // rows_here
    order = jnp.arange(block.shape[0], dtype=jnp.int32)
    earlier = (owners[:, None] == owners[None, :]) & (order[None, :] < order[:, None])
    return owners * most + jnp.sum(earlier.astype(jnp.int32), axis=1)


def on_device(panel, flips, picks):
    rows_here, width = panel.shape
    devices = lax.axis_size("narrow") * lax.axis_size("wide")
    scale = 1.0 / float(rows_here * devices) ** 0.5
    me = lax.axis_index(AXES)
    per = picks.shape[0] // devices
    most = -(-per // devices)

    local = local_transform(panel, flips, scale, [rows_here])[0]
    local = local.reshape(devices, rows_here // devices, width)
    wanted = send_rows(picks, [me], rows_here, devices, most)
    spots = landing(lax.dynamic_slice(picks, (me * per,), (per,)), rows_here, most)
    counts = count_picks(picks, me, rows_here, devices)
    slices = lax.all_to_all(local, AXES, 0, 0, tiled=True)
    slices, wanted, spots, counts = lax.optimization_barrier((slices, wanted, spots, counts))
    slices = device_sums(slices)
    mixed = lax.all_to_all(slices, AXES, 0, 0, tiled=True)
    gram = sum_over_devices(gram_part(counts, slices)) / float(picks.shape[0])
    mixed, gram = lax.optimization_barrier((mixed, gram))
    mixed = mixed.reshape(rows_here, width)

    chosen = jnp.take(mixed, wanted, axis=0, mode="clip")
    landed = lax.all_to_all(chosen.reshape(devices, most, width), AXES, 0, 0, tiled=True)
    sketch = jnp.take(landed.reshape(devices * most, width), spots, axis=0, mode="clip")
    return (mixed, sketch, gram)


def solution(mesh):
    in_specs = (P(AXES, None), P(AXES), P())
    out_specs = (P(AXES, None), P(AXES, None), P())
    return jax.shard_map(
        on_device, mesh=mesh, in_specs=in_specs, out_specs=out_specs, check_vma=False
    )
```

```python
import functools

import jax
import jax.numpy as jnp
from jax import lax
from jax.experimental import pallas as pl
from jax.experimental.pallas import tpu as pltpu
from jax.sharding import PartitionSpec as P

BLOCK = 256
AXES = ("narrow", "wide")


def signs(order):
    rows = lax.broadcasted_iota(jnp.int32, (order, order), 0)
    both = rows & lax.broadcasted_iota(jnp.int32, (order, order), 1)
    parity = jnp.zeros((order, order), jnp.int32)
    for level in range(order.bit_length() - 1):
        parity = parity ^ (both >> level & 1)
    return (1 - 2 * parity).astype(jnp.float32)


def local_kernel(scale, flips_ref, panel_ref, *refs):
    *outs, held = refs
    blocks = panel_ref.shape[0] // BLOCK
    width = panel_ref.shape[1]
    lanes = flips_ref.shape[1]
    per = BLOCK // lanes
    base = signs(BLOCK)
    for b in range(blocks):
        row = jnp.concatenate([flips_ref[b * per + i : b * per + i + 1, :] for i in range(per)], axis=1)
        mixer = (base * (1 - 2 * row).astype(jnp.float32)).astype(jnp.bfloat16)
        values = panel_ref[b * BLOCK : (b + 1) * BLOCK, :]
        high = values.astype(jnp.bfloat16)
        rest = values - high.astype(jnp.float32)
        middle = rest.astype(jnp.bfloat16)
        low = (rest - middle.astype(jnp.float32)).astype(jnp.bfloat16)
        parts = jnp.concatenate([high, middle, low], axis=1)
        out = jnp.dot(mixer, parts, preferred_element_type=jnp.float32)
        held[b] = out[:, :width] + out[:, width : 2 * width] + out[:, 2 * width :]
    strip = 16
    places = [(i, j) for i in range(len(outs)) for j in range(outs[i].shape[0] // BLOCK)]

    def body(step, carry):
        at = pl.multiple_of(step * strip, strip)
        items = [held[b, pl.ds(at, strip), :] for b in range(blocks)]
        apart = 1
        while apart < blocks:
            items = [
                items[b] + items[b ^ apart] if b & apart == 0 else items[b ^ apart] - items[b]
                for b in range(blocks)
            ]
            apart *= 2
        for b in range(blocks):
            which, place = places[b]
            spot = pl.multiple_of(place * BLOCK + at, strip)
            outs[which][pl.ds(spot, strip), :] = items[b] * scale
        return carry

    lax.fori_loop(0, BLOCK // strip, body, 0)


def local_transform(panel, flips, scale, shares):
    rows, width = panel.shape
    return pl.pallas_call(
        functools.partial(local_kernel, scale),
        out_shape=[jax.ShapeDtypeStruct((share, width), jnp.float32) for share in shares],
        in_specs=[pl.BlockSpec(memory_space=pltpu.VMEM)] * 2,
        out_specs=[pl.BlockSpec(memory_space=pltpu.VMEM)] * len(shares),
        scratch_shapes=[pltpu.VMEM((rows // BLOCK, BLOCK, width), jnp.float32)],
        compiler_params=pltpu.CompilerParams(vmem_limit_bytes=32 * 2**20),
    )(flips.reshape(rows // 128, 128), panel)


def device_kernel(in_ref, out_ref, held, sent):
    devices, rows, _ = in_ref.shape
    strip = 8
    quarter = rows // 4

    def body(step, carry):
        at = pl.multiple_of(step * strip, strip)
        items = [in_ref[d, pl.ds(at, strip), :] for d in range(devices)]
        apart = 1
        while apart < devices:
            items = [
                items[d] + items[d ^ apart] if d & apart == 0 else items[d ^ apart] - items[d]
                for d in range(devices)
            ]
            apart *= 2
        for d in range(devices):
            held[d, pl.ds(at, strip), :] = items[d]
        return carry

    copies = []
    for part in range(4):
        first = part * quarter // strip
        lax.fori_loop(first, first + quarter // strip, body, 0)
        span = pl.ds(part * quarter, quarter)
        copies.append(
            pltpu.make_async_copy(held.at[:, span, :], out_ref.at[:, span, :], sent.at[part])
        )
        copies[-1].start()
    for copy in copies:
        copy.wait()


def device_sums(value):
    return pl.pallas_call(
        device_kernel,
        out_shape=jax.ShapeDtypeStruct(value.shape, jnp.float32),
        in_specs=[pl.BlockSpec(memory_space=pltpu.VMEM)],
        out_specs=pl.BlockSpec(memory_space=pl.ANY),
        scratch_shapes=[
            pltpu.VMEM(value.shape, jnp.float32),
            pltpu.SemaphoreType.DMA((4,)),
        ],
        compiler_params=pltpu.CompilerParams(vmem_limit_bytes=32 * 2**20),
    )(value)


def store_kernel(value_ref, out_ref, sent):
    copy = pltpu.make_async_copy(value_ref, out_ref, sent)
    copy.start()
    copy.wait()


def store(value):
    return pl.pallas_call(
        store_kernel,
        out_shape=jax.ShapeDtypeStruct(value.shape, jnp.float32),
        in_specs=[pl.BlockSpec(memory_space=pltpu.VMEM)],
        out_specs=pl.BlockSpec(memory_space=pl.ANY),
        scratch_shapes=[pltpu.SemaphoreType.DMA],
        compiler_params=pltpu.CompilerParams(vmem_limit_bytes=8 * 2**20),
    )(value)


def index_kernel(rows_here, most, bases_ref, picks_ref, out_ref):
    picks = picks_ref[...]
    devices, per = picks.shape
    before = lax.broadcasted_iota(jnp.int32, (per, per), 0)
    earlier = before < lax.broadcasted_iota(jnp.int32, (per, per), 1)
    earlier = jnp.where(earlier, 1.0, 0.0).astype(jnp.bfloat16)
    for which in range(out_ref.shape[0]):
        offsets = picks - bases_ref[which]
        owned = (offsets >= 0) & (offsets < rows_here)
        ones = jnp.where(owned, 1.0, 0.0).astype(jnp.bfloat16)
        rank = jnp.dot(ones, earlier, preferred_element_type=jnp.float32)
        rank = jnp.where(owned, rank, -1.0)
        marked = (offsets + 1).astype(jnp.float32)
        for slot in range(most):
            hit = jnp.where(rank == float(slot), marked, 0.0)
            row = jnp.sum(hit, axis=1, keepdims=True).astype(jnp.int32) - 1
            out_ref[which, :, slot : slot + 1] = row


def send_rows(picks, owners, rows_here, devices, most):
    bases = jnp.stack(owners) * rows_here
    rows = pl.pallas_call(
        functools.partial(index_kernel, rows_here, most),
        out_shape=jax.ShapeDtypeStruct((len(owners), devices, most), jnp.int32),
        in_specs=[
            pl.BlockSpec(memory_space=pltpu.SMEM),
            pl.BlockSpec(memory_space=pltpu.VMEM),
        ],
        out_specs=pl.BlockSpec(memory_space=pltpu.VMEM),
        compiler_params=pltpu.CompilerParams(vmem_limit_bytes=8 * 2**20),
    )(bases.astype(jnp.int32), picks.reshape(devices, -1))
    return rows.reshape(len(owners) * devices * most)


def count_kernel(rows_here, me_ref, picks_ref, out_ref):
    picks = picks_ref[...]
    rows, devices = out_ref.shape
    owner = picks >> rows_here.bit_length() - 1
    local = picks & rows_here - 1
    held = local >> rows.bit_length() - 1 == me_ref[0]
    place = jnp.where(held, local & rows - 1, -1)
    shape = (devices, picks.shape[1])
    owners = jnp.where(lax.broadcasted_iota(jnp.int32, shape, 0) == owner, 1.0, 0.0)
    shape = (rows, picks.shape[1])
    places = jnp.where(lax.broadcasted_iota(jnp.int32, shape, 0) == place, 1.0, 0.0)
    out_ref[...] = lax.dot_general(
        places.astype(jnp.bfloat16),
        owners.astype(jnp.bfloat16),
        (((1,), (1,)), ((), ())),
        preferred_element_type=jnp.float32,
    )


def count_picks(picks, me, rows_here, devices):
    return pl.pallas_call(
        functools.partial(count_kernel, rows_here),
        out_shape=jax.ShapeDtypeStruct((rows_here // devices, devices), jnp.float32),
        in_specs=[
            pl.BlockSpec(memory_space=pltpu.SMEM),
            pl.BlockSpec(memory_space=pltpu.VMEM),
        ],
        out_specs=pl.BlockSpec(memory_space=pltpu.VMEM),
        compiler_params=pltpu.CompilerParams(vmem_limit_bytes=32 * 2**20),
    )(me.reshape(1).astype(jnp.int32), picks.reshape(1, -1))


def halves(value):
    high = value.astype(jnp.bfloat16)
    return high, (value - high.astype(jnp.float32)).astype(jnp.bfloat16)


def part_kernel(counts_ref, held_ref, out_ref):
    devices, _, width = held_ref.shape
    total = jnp.zeros((width, 2 * width), jnp.float32)
    rest = jnp.zeros((width, width), jnp.float32)
    for d in range(devices):
        rows = held_ref[d]
        high, low = halves(rows)
        weighted, spare = halves(rows * counts_ref[:, d : d + 1])
        over_rows = (((0,), (0,)), ((), ()))
        both = jnp.concatenate([weighted, spare], axis=1)
        total += lax.dot_general(high, both, over_rows, preferred_element_type=jnp.float32)
        rest += lax.dot_general(low, weighted, over_rows, preferred_element_type=jnp.float32)
    out_ref[...] = total[:, :width] + total[:, width:] + rest


def gram_part(counts, held):
    width = held.shape[2]
    return pl.pallas_call(
        part_kernel,
        out_shape=jax.ShapeDtypeStruct((width, width), jnp.float32),
        in_specs=[pl.BlockSpec(memory_space=pltpu.VMEM)] * 2,
        out_specs=pl.BlockSpec(memory_space=pltpu.VMEM),
        compiler_params=pltpu.CompilerParams(vmem_limit_bytes=32 * 2**20),
    )(counts, held)


def add_partner(value, axis, level):
    pairs = [(source, source ^ 2**level) for source in range(lax.axis_size(axis))]
    return value + lax.ppermute(value, axis, pairs)


def landing(block, rows_here, most):
    owners = block // rows_here
    order = jnp.arange(block.shape[0], dtype=jnp.int32)
    earlier = (owners[:, None] == owners[None, :]) & (order[None, :] < order[:, None])
    return owners * most + jnp.sum(earlier.astype(jnp.int32), axis=1)


def on_device(panel, flips, picks):
    rows_here, width = panel.shape
    devices = lax.axis_size("narrow") * lax.axis_size("wide")
    scale = 1.0 / float(rows_here * devices) ** 0.5
    me = lax.axis_index(AXES)
    per = picks.shape[0] // devices
    most = -(-per // devices)

    local = local_transform(panel, flips, scale, [rows_here])[0]
    local = local.reshape(devices, rows_here // devices, width)
    wanted = send_rows(picks, [me], rows_here, devices, most)
    spots = landing(lax.dynamic_slice(picks, (me * per,), (per,)), rows_here, most)
    counts = count_picks(picks, me, rows_here, devices)
    slices = lax.all_to_all(local, AXES, 0, 0, tiled=True)
    slices, wanted, spots, counts = lax.optimization_barrier((slices, wanted, spots, counts))
    slices = device_sums(slices)
    mixed = lax.all_to_all(slices, AXES, 0, 0, tiled=True)
    gram = gram_part(counts, slices)
    levels = [(axis, l) for axis in AXES for l in range(lax.axis_size(axis).bit_length() - 1)]
    for axis, level in levels[:-1]:
        gram = add_partner(gram, axis, level)
    mixed, gram = lax.optimization_barrier((mixed, gram))
    mixed = mixed.reshape(rows_here, width)
    chosen = jnp.take(mixed, wanted, axis=0, mode="clip")
    landed = lax.all_to_all(chosen.reshape(devices, most, width), AXES, 0, 0, tiled=True)
    gram = add_partner(gram, *levels[-1]) / float(picks.shape[0])
    mixed = store(mixed)
    landed, mixed, gram = lax.optimization_barrier((landed, mixed, gram))
    sketch = jnp.take(landed.reshape(devices * most, width), spots, axis=0, mode="clip")
    return (mixed, sketch, gram)


def solution(mesh):
    in_specs = (P(AXES, None), P(AXES), P())
    out_specs = (P(AXES, None), P(AXES, None), P())
    return jax.shard_map(
        on_device, mesh=mesh, in_specs=in_specs, out_specs=out_specs, check_vma=False
    )
```

```python
import functools

import jax
import jax.numpy as jnp
from jax import lax
from jax.experimental import pallas as pl
from jax.experimental.pallas import tpu as pltpu
from jax.sharding import PartitionSpec as P

BLOCK = 256
AXES = ("narrow", "wide")
TURNED = ("wide", "narrow")


def signs(order):
    rows = lax.broadcasted_iota(jnp.int32, (order, order), 0)
    both = rows & lax.broadcasted_iota(jnp.int32, (order, order), 1)
    parity = jnp.zeros((order, order), jnp.int32)
    for level in range(order.bit_length() - 1):
        parity = parity ^ (both >> level & 1)
    return (1 - 2 * parity).astype(jnp.float32)


def local_kernel(scale, flips_ref, panel_ref, *refs):
    *outs, held = refs
    blocks = panel_ref.shape[0] // BLOCK
    width = panel_ref.shape[1]
    lanes = flips_ref.shape[1]
    per = BLOCK // lanes
    base = signs(BLOCK)
    for b in range(blocks):
        row = jnp.concatenate([flips_ref[b * per + i : b * per + i + 1, :] for i in range(per)], axis=1)
        mixer = (base * (1 - 2 * row).astype(jnp.float32)).astype(jnp.bfloat16)
        values = panel_ref[b * BLOCK : (b + 1) * BLOCK, :]
        high = values.astype(jnp.bfloat16)
        rest = values - high.astype(jnp.float32)
        middle = rest.astype(jnp.bfloat16)
        low = (rest - middle.astype(jnp.float32)).astype(jnp.bfloat16)
        parts = jnp.concatenate([high, middle, low], axis=1)
        out = jnp.dot(mixer, parts, preferred_element_type=jnp.float32)
        held[b] = out[:, :width] + out[:, width : 2 * width] + out[:, 2 * width :]
    strip = 16
    places = [(i, j) for i in range(len(outs)) for j in range(outs[i].shape[0] // BLOCK)]

    def body(step, carry):
        at = pl.multiple_of(step * strip, strip)
        items = [held[b, pl.ds(at, strip), :] for b in range(blocks)]
        apart = 1
        while apart < blocks:
            items = [
                items[b] + items[b ^ apart] if b & apart == 0 else items[b ^ apart] - items[b]
                for b in range(blocks)
            ]
            apart *= 2
        for b in range(blocks):
            which, place = places[b]
            spot = pl.multiple_of(place * BLOCK + at, strip)
            outs[which][pl.ds(spot, strip), :] = items[b] * scale
        return carry

    lax.fori_loop(0, BLOCK // strip, body, 0)


def local_transform(panel, flips, scale, shares):
    rows, width = panel.shape
    return pl.pallas_call(
        functools.partial(local_kernel, scale),
        out_shape=[jax.ShapeDtypeStruct((share, width), jnp.float32) for share in shares],
        in_specs=[pl.BlockSpec(memory_space=pltpu.VMEM)] * 2,
        out_specs=[pl.BlockSpec(memory_space=pltpu.VMEM)] * len(shares),
        scratch_shapes=[pltpu.VMEM((rows // BLOCK, BLOCK, width), jnp.float32)],
        compiler_params=pltpu.CompilerParams(vmem_limit_bytes=32 * 2**20),
    )(flips.reshape(rows // 128, 128), panel)


def device_kernel(in_ref, out_ref, held, sent):
    devices, rows, _ = in_ref.shape
    strip = 8
    quarter = rows // 4

    def body(step, carry):
        at = pl.multiple_of(step * strip, strip)
        items = [in_ref[d, pl.ds(at, strip), :] for d in range(devices)]
        apart = 1
        while apart < devices:
            items = [
                items[d] + items[d ^ apart] if d & apart == 0 else items[d ^ apart] - items[d]
                for d in range(devices)
            ]
            apart *= 2
        for d in range(devices):
            held[d, pl.ds(at, strip), :] = items[d]
        return carry

    copies = []
    for part in range(4):
        first = part * quarter // strip
        lax.fori_loop(first, first + quarter // strip, body, 0)
        span = pl.ds(part * quarter, quarter)
        copies.append(
            pltpu.make_async_copy(held.at[:, span, :], out_ref.at[:, span, :], sent.at[part])
        )
        copies[-1].start()
    for copy in copies:
        copy.wait()


def device_sums(value):
    return pl.pallas_call(
        device_kernel,
        out_shape=jax.ShapeDtypeStruct(value.shape, jnp.float32),
        in_specs=[pl.BlockSpec(memory_space=pltpu.VMEM)],
        out_specs=pl.BlockSpec(memory_space=pl.ANY),
        scratch_shapes=[
            pltpu.VMEM(value.shape, jnp.float32),
            pltpu.SemaphoreType.DMA((4,)),
        ],
        compiler_params=pltpu.CompilerParams(vmem_limit_bytes=32 * 2**20),
    )(value)


def store_kernel(value_ref, out_ref, sent):
    copy = pltpu.make_async_copy(value_ref, out_ref, sent)
    copy.start()
    copy.wait()


def store(value):
    return pl.pallas_call(
        store_kernel,
        out_shape=jax.ShapeDtypeStruct(value.shape, jnp.float32),
        in_specs=[pl.BlockSpec(memory_space=pltpu.VMEM)],
        out_specs=pl.BlockSpec(memory_space=pl.ANY),
        scratch_shapes=[pltpu.SemaphoreType.DMA],
        compiler_params=pltpu.CompilerParams(vmem_limit_bytes=8 * 2**20),
    )(value)


def index_kernel(rows_here, most, bases_ref, picks_ref, out_ref):
    picks = picks_ref[...]
    devices, per = picks.shape
    before = lax.broadcasted_iota(jnp.int32, (per, per), 0)
    earlier = before < lax.broadcasted_iota(jnp.int32, (per, per), 1)
    earlier = jnp.where(earlier, 1.0, 0.0).astype(jnp.bfloat16)
    for which in range(out_ref.shape[0]):
        offsets = picks - bases_ref[which]
        owned = (offsets >= 0) & (offsets < rows_here)
        ones = jnp.where(owned, 1.0, 0.0).astype(jnp.bfloat16)
        rank = jnp.dot(ones, earlier, preferred_element_type=jnp.float32)
        rank = jnp.where(owned, rank, -1.0)
        marked = (offsets + 1).astype(jnp.float32)
        for slot in range(most):
            hit = jnp.where(rank == float(slot), marked, 0.0)
            row = jnp.sum(hit, axis=1, keepdims=True).astype(jnp.int32) - 1
            out_ref[which, :, slot : slot + 1] = row


def send_rows(picks, owners, rows_here, devices, most):
    bases = jnp.stack(owners) * rows_here
    rows = pl.pallas_call(
        functools.partial(index_kernel, rows_here, most),
        out_shape=jax.ShapeDtypeStruct((len(owners), devices, most), jnp.int32),
        in_specs=[
            pl.BlockSpec(memory_space=pltpu.SMEM),
            pl.BlockSpec(memory_space=pltpu.VMEM),
        ],
        out_specs=pl.BlockSpec(memory_space=pltpu.VMEM),
        compiler_params=pltpu.CompilerParams(vmem_limit_bytes=8 * 2**20),
    )(bases.astype(jnp.int32), picks.reshape(devices, -1))
    return rows.reshape(len(owners) * devices * most)


def count_kernel(rows_here, wide, me_ref, picks_ref, out_ref):
    picks = picks_ref[...]
    rows, devices = out_ref.shape
    owner = picks >> rows_here.bit_length() - 1
    owner = (owner & wide - 1) * (devices // wide) + (owner >> wide.bit_length() - 1)
    local = picks & rows_here - 1
    held = local >> rows.bit_length() - 1 == me_ref[0]
    place = jnp.where(held, local & rows - 1, -1)
    shape = (devices, picks.shape[1])
    owners = jnp.where(lax.broadcasted_iota(jnp.int32, shape, 0) == owner, 1.0, 0.0)
    shape = (rows, picks.shape[1])
    places = jnp.where(lax.broadcasted_iota(jnp.int32, shape, 0) == place, 1.0, 0.0)
    out_ref[...] = lax.dot_general(
        places.astype(jnp.bfloat16),
        owners.astype(jnp.bfloat16),
        (((1,), (1,)), ((), ())),
        preferred_element_type=jnp.float32,
    )


def count_picks(picks, me, rows_here, devices):
    return pl.pallas_call(
        functools.partial(count_kernel, rows_here, lax.axis_size("wide")),
        out_shape=jax.ShapeDtypeStruct((rows_here // devices, devices), jnp.float32),
        in_specs=[
            pl.BlockSpec(memory_space=pltpu.SMEM),
            pl.BlockSpec(memory_space=pltpu.VMEM),
        ],
        out_specs=pl.BlockSpec(memory_space=pltpu.VMEM),
        compiler_params=pltpu.CompilerParams(vmem_limit_bytes=32 * 2**20),
    )(me.reshape(1).astype(jnp.int32), picks.reshape(1, -1))


def halves(value):
    high = value.astype(jnp.bfloat16)
    return high, (value - high.astype(jnp.float32)).astype(jnp.bfloat16)


def part_kernel(counts_ref, held_ref, out_ref):
    devices, _, width = held_ref.shape
    total = jnp.zeros((width, 2 * width), jnp.float32)
    rest = jnp.zeros((width, width), jnp.float32)
    for d in range(devices):
        rows = held_ref[d]
        high, low = halves(rows)
        weighted, spare = halves(rows * counts_ref[:, d : d + 1])
        over_rows = (((0,), (0,)), ((), ()))
        both = jnp.concatenate([weighted, spare], axis=1)
        total += lax.dot_general(high, both, over_rows, preferred_element_type=jnp.float32)
        rest += lax.dot_general(low, weighted, over_rows, preferred_element_type=jnp.float32)
    out_ref[...] = total[:, :width] + total[:, width:] + rest


def gram_part(counts, held):
    width = held.shape[2]
    return pl.pallas_call(
        part_kernel,
        out_shape=jax.ShapeDtypeStruct((width, width), jnp.float32),
        in_specs=[pl.BlockSpec(memory_space=pltpu.VMEM)] * 2,
        out_specs=pl.BlockSpec(memory_space=pltpu.VMEM),
        compiler_params=pltpu.CompilerParams(vmem_limit_bytes=32 * 2**20),
    )(counts, held)


def add_partner(value, axis, level):
    pairs = [(source, source ^ 2**level) for source in range(lax.axis_size(axis))]
    return value + lax.ppermute(value, axis, pairs)


def landing(block, rows_here, most):
    owners = block // rows_here
    order = jnp.arange(block.shape[0], dtype=jnp.int32)
    earlier = (owners[:, None] == owners[None, :]) & (order[None, :] < order[:, None])
    return owners * most + jnp.sum(earlier.astype(jnp.int32), axis=1)


def on_device(panel, flips, picks):
    rows_here, width = panel.shape
    devices = lax.axis_size("narrow") * lax.axis_size("wide")
    scale = 1.0 / float(rows_here * devices) ** 0.5
    me = lax.axis_index(AXES)
    per = picks.shape[0] // devices
    most = -(-per // devices)

    local = local_transform(panel, flips, scale, [rows_here])[0]
    local = local.reshape(devices, rows_here // devices, width)
    wanted = send_rows(picks, [me], rows_here, devices, most)
    spots = landing(lax.dynamic_slice(picks, (me * per,), (per,)), rows_here, most)
    counts = count_picks(picks, lax.axis_index(TURNED), rows_here, devices)
    slices = lax.all_to_all(local, TURNED, 0, 0, tiled=True)
    slices, wanted, spots, counts = lax.optimization_barrier((slices, wanted, spots, counts))
    slices = device_sums(slices)
    mixed = lax.all_to_all(slices, TURNED, 0, 0, tiled=True)
    gram = gram_part(counts, slices)
    levels = [(axis, l) for axis in AXES for l in range(lax.axis_size(axis).bit_length() - 1)]
    levels = levels[::-1]
    for axis, level in levels[:-1]:
        gram = add_partner(gram, axis, level)
    mixed, gram = lax.optimization_barrier((mixed, gram))
    mixed = mixed.reshape(rows_here, width)
    chosen = jnp.take(mixed, wanted, axis=0, mode="clip")
    landed = lax.all_to_all(chosen.reshape(devices, most, width), AXES, 0, 0, tiled=True)
    gram = add_partner(gram, *levels[-1]) / float(picks.shape[0])
    mixed = store(mixed)
    landed, mixed, gram = lax.optimization_barrier((landed, mixed, gram))
    sketch = jnp.take(landed.reshape(devices * most, width), spots, axis=0, mode="clip")
    return (mixed, sketch, gram)


def solution(mesh):
    in_specs = (P(AXES, None), P(AXES), P())
    out_specs = (P(AXES, None), P(AXES, None), P())
    return jax.shard_map(
        on_device, mesh=mesh, in_specs=in_specs, out_specs=out_specs, check_vma=False
    )
```

```python
import functools

import jax
import jax.numpy as jnp
from jax import lax
from jax.experimental import pallas as pl
from jax.experimental.pallas import tpu as pltpu
from jax.sharding import PartitionSpec as P

BLOCK = 256
AXES = ("narrow", "wide")
TURNED = ("wide", "narrow")


def signs(order):
    rows = lax.broadcasted_iota(jnp.int32, (order, order), 0)
    both = rows & lax.broadcasted_iota(jnp.int32, (order, order), 1)
    parity = jnp.zeros((order, order), jnp.int32)
    for level in range(order.bit_length() - 1):
        parity = parity ^ (both >> level & 1)
    return (1 - 2 * parity).astype(jnp.float32)


def local_kernel(scale, flips_ref, panel_ref, out_ref, held, sent):
    blocks, _, width = panel_ref.shape
    per = BLOCK // flips_ref.shape[1]
    base = signs(BLOCK)
    for b in range(blocks):
        row = jnp.concatenate([flips_ref[b * per + i : b * per + i + 1, :] for i in range(per)], axis=1)
        mixer = (base * (1 - 2 * row).astype(jnp.float32)).astype(jnp.bfloat16)
        values = panel_ref[b]
        high = values.astype(jnp.bfloat16)
        rest = values - high.astype(jnp.float32)
        middle = rest.astype(jnp.bfloat16)
        low = (rest - middle.astype(jnp.float32)).astype(jnp.bfloat16)
        parts = jnp.concatenate([high, middle, low], axis=1)
        out = jnp.dot(mixer, parts, preferred_element_type=jnp.float32)
        held[b] = out[:, :width] + out[:, width : 2 * width] + out[:, 2 * width :]
    strip = 16
    quarter = BLOCK // 4

    def body(step, carry):
        at = pl.multiple_of(step * strip, strip)
        items = [held[b, pl.ds(at, strip), :] for b in range(blocks)]
        apart = 1
        while apart < blocks:
            items = [
                items[b] + items[b ^ apart] if b & apart == 0 else items[b ^ apart] - items[b]
                for b in range(blocks)
            ]
            apart *= 2
        for b in range(blocks):
            held[b, pl.ds(at, strip), :] = items[b] * scale
        return carry

    copies = []
    for part in range(4):
        first = part * quarter // strip
        lax.fori_loop(first, first + quarter // strip, body, 0)
        span = pl.ds(part * quarter, quarter)
        copies.append(
            pltpu.make_async_copy(held.at[:, span, :], out_ref.at[:, span, :], sent.at[part])
        )
        copies[-1].start()
    for copy in copies:
        copy.wait()


def local_transform(panel, flips, scale):
    rows, width = panel.shape
    shape = (rows // BLOCK, BLOCK, width)
    return pl.pallas_call(
        functools.partial(local_kernel, scale),
        out_shape=jax.ShapeDtypeStruct(shape, jnp.float32),
        in_specs=[pl.BlockSpec(memory_space=pltpu.VMEM)] * 2,
        out_specs=pl.BlockSpec(memory_space=pl.ANY),
        scratch_shapes=[pltpu.VMEM(shape, jnp.float32), pltpu.SemaphoreType.DMA((4,))],
        compiler_params=pltpu.CompilerParams(vmem_limit_bytes=32 * 2**20),
    )(flips.reshape(rows // 128, 128), panel.reshape(shape))


def device_kernel(in_ref, out_ref, held, sent):
    devices, rows, _ = in_ref.shape
    strip = 8
    quarter = rows // 4

    def body(step, carry):
        at = pl.multiple_of(step * strip, strip)
        items = [in_ref[d, pl.ds(at, strip), :] for d in range(devices)]
        apart = 1
        while apart < devices:
            items = [
                items[d] + items[d ^ apart] if d & apart == 0 else items[d ^ apart] - items[d]
                for d in range(devices)
            ]
            apart *= 2
        for d in range(devices):
            held[d, pl.ds(at, strip), :] = items[d]
        return carry

    copies = []
    for part in range(4):
        first = part * quarter // strip
        lax.fori_loop(first, first + quarter // strip, body, 0)
        span = pl.ds(part * quarter, quarter)
        copies.append(
            pltpu.make_async_copy(held.at[:, span, :], out_ref.at[:, span, :], sent.at[part])
        )
        copies[-1].start()
    for copy in copies:
        copy.wait()


def device_sums(value):
    return pl.pallas_call(
        device_kernel,
        out_shape=jax.ShapeDtypeStruct(value.shape, jnp.float32),
        in_specs=[pl.BlockSpec(memory_space=pltpu.VMEM)],
        out_specs=pl.BlockSpec(memory_space=pl.ANY),
        scratch_shapes=[
            pltpu.VMEM(value.shape, jnp.float32),
            pltpu.SemaphoreType.DMA((4,)),
        ],
        compiler_params=pltpu.CompilerParams(vmem_limit_bytes=32 * 2**20),
    )(value)


def store_kernel(value_ref, out_ref, sent):
    copy = pltpu.make_async_copy(value_ref, out_ref, sent)
    copy.start()
    copy.wait()


def store(value):
    return pl.pallas_call(
        store_kernel,
        out_shape=jax.ShapeDtypeStruct(value.shape, jnp.float32),
        in_specs=[pl.BlockSpec(memory_space=pltpu.VMEM)],
        out_specs=pl.BlockSpec(memory_space=pl.ANY),
        scratch_shapes=[pltpu.SemaphoreType.DMA],
        compiler_params=pltpu.CompilerParams(vmem_limit_bytes=8 * 2**20),
    )(value)


def index_kernel(rows_here, most, bases_ref, picks_ref, out_ref):
    picks = picks_ref[...]
    devices, per = picks.shape
    before = lax.broadcasted_iota(jnp.int32, (per, per), 0)
    earlier = before < lax.broadcasted_iota(jnp.int32, (per, per), 1)
    earlier = jnp.where(earlier, 1.0, 0.0).astype(jnp.bfloat16)
    for which in range(out_ref.shape[0]):
        offsets = picks - bases_ref[which]
        owned = (offsets >= 0) & (offsets < rows_here)
        ones = jnp.where(owned, 1.0, 0.0).astype(jnp.bfloat16)
        rank = jnp.dot(ones, earlier, preferred_element_type=jnp.float32)
        rank = jnp.where(owned, rank, -1.0)
        marked = (offsets + 1).astype(jnp.float32)
        for slot in range(most):
            hit = jnp.where(rank == float(slot), marked, 0.0)
            row = jnp.sum(hit, axis=1, keepdims=True).astype(jnp.int32) - 1
            out_ref[which, :, slot : slot + 1] = row


def send_rows(picks, owners, rows_here, devices, most):
    bases = jnp.stack(owners) * rows_here
    rows = pl.pallas_call(
        functools.partial(index_kernel, rows_here, most),
        out_shape=jax.ShapeDtypeStruct((len(owners), devices, most), jnp.int32),
        in_specs=[
            pl.BlockSpec(memory_space=pltpu.SMEM),
            pl.BlockSpec(memory_space=pltpu.VMEM),
        ],
        out_specs=pl.BlockSpec(memory_space=pltpu.VMEM),
        compiler_params=pltpu.CompilerParams(vmem_limit_bytes=8 * 2**20),
    )(bases.astype(jnp.int32), picks.reshape(devices, -1))
    return rows.reshape(len(owners) * devices * most)


def count_kernel(rows_here, wide, me_ref, picks_ref, out_ref):
    picks = picks_ref[...]
    rows, devices = out_ref.shape
    owner = picks >> rows_here.bit_length() - 1
    owner = (owner & wide - 1) * (devices // wide) + (owner >> wide.bit_length() - 1)
    local = picks & rows_here - 1
    held = local >> rows.bit_length() - 1 == me_ref[0]
    place = jnp.where(held, local & rows - 1, -1)
    shape = (devices, picks.shape[1])
    owners = jnp.where(lax.broadcasted_iota(jnp.int32, shape, 0) == owner, 1.0, 0.0)
    shape = (rows, picks.shape[1])
    places = jnp.where(lax.broadcasted_iota(jnp.int32, shape, 0) == place, 1.0, 0.0)
    out_ref[...] = lax.dot_general(
        places.astype(jnp.bfloat16),
        owners.astype(jnp.bfloat16),
        (((1,), (1,)), ((), ())),
        preferred_element_type=jnp.float32,
    )


def count_picks(picks, me, rows_here, devices):
    return pl.pallas_call(
        functools.partial(count_kernel, rows_here, lax.axis_size("wide")),
        out_shape=jax.ShapeDtypeStruct((rows_here // devices, devices), jnp.float32),
        in_specs=[
            pl.BlockSpec(memory_space=pltpu.SMEM),
            pl.BlockSpec(memory_space=pltpu.VMEM),
        ],
        out_specs=pl.BlockSpec(memory_space=pltpu.VMEM),
        compiler_params=pltpu.CompilerParams(vmem_limit_bytes=32 * 2**20),
    )(me.reshape(1).astype(jnp.int32), picks.reshape(1, -1))


def halves(value):
    high = value.astype(jnp.bfloat16)
    return high, (value - high.astype(jnp.float32)).astype(jnp.bfloat16)


def part_kernel(counts_ref, held_ref, out_ref):
    devices, _, width = held_ref.shape
    total = jnp.zeros((width, 2 * width), jnp.float32)
    rest = jnp.zeros((width, width), jnp.float32)
    for d in range(devices):
        rows = held_ref[d]
        high, low = halves(rows)
        weighted, spare = halves(rows * counts_ref[:, d : d + 1])
        over_rows = (((0,), (0,)), ((), ()))
        both = jnp.concatenate([weighted, spare], axis=1)
        total += lax.dot_general(high, both, over_rows, preferred_element_type=jnp.float32)
        rest += lax.dot_general(low, weighted, over_rows, preferred_element_type=jnp.float32)
    out_ref[...] = total[:, :width] + total[:, width:] + rest


def gram_part(counts, held):
    width = held.shape[2]
    return pl.pallas_call(
        part_kernel,
        out_shape=jax.ShapeDtypeStruct((width, width), jnp.float32),
        in_specs=[pl.BlockSpec(memory_space=pltpu.VMEM)] * 2,
        out_specs=pl.BlockSpec(memory_space=pltpu.VMEM),
        compiler_params=pltpu.CompilerParams(vmem_limit_bytes=32 * 2**20),
    )(counts, held)


def add_partner(value, axis, level):
    pairs = [(source, source ^ 2**level) for source in range(lax.axis_size(axis))]
    return value + lax.ppermute(value, axis, pairs)


def landing(block, rows_here, most):
    owners = block // rows_here
    order = jnp.arange(block.shape[0], dtype=jnp.int32)
    earlier = (owners[:, None] == owners[None, :]) & (order[None, :] < order[:, None])
    return owners * most + jnp.sum(earlier.astype(jnp.int32), axis=1)


def on_device(panel, flips, picks):
    rows_here, width = panel.shape
    devices = lax.axis_size("narrow") * lax.axis_size("wide")
    scale = 1.0 / float(rows_here * devices) ** 0.5
    me = lax.axis_index(AXES)
    per = picks.shape[0] // devices
    most = -(-per // devices)

    local = local_transform(panel, flips, scale)
    local = local.reshape(devices, rows_here // devices, width)
    wanted = send_rows(picks, [me], rows_here, devices, most)
    spots = landing(lax.dynamic_slice(picks, (me * per,), (per,)), rows_here, most)
    counts = count_picks(picks, lax.axis_index(TURNED), rows_here, devices)
    slices = lax.all_to_all(local, TURNED, 0, 0, tiled=True)
    slices, wanted, spots, counts = lax.optimization_barrier((slices, wanted, spots, counts))
    slices = device_sums(slices)
    mixed = lax.all_to_all(slices, TURNED, 0, 0, tiled=True)
    gram = gram_part(counts, slices)
    levels = [(axis, l) for axis in AXES for l in range(lax.axis_size(axis).bit_length() - 1)]
    levels = levels[1:] + levels[:1]
    for axis, level in levels[:-1]:
        gram = add_partner(gram, axis, level)
    mixed, gram = lax.optimization_barrier((mixed, gram))
    mixed = mixed.reshape(rows_here, width)
    chosen = jnp.take(mixed, wanted, axis=0, mode="clip")
    landed = lax.all_to_all(chosen.reshape(devices, most, width), AXES, 0, 0, tiled=True)
    gram = add_partner(gram, *levels[-1]) / float(picks.shape[0])
    mixed = store(mixed)
    landed, mixed, gram = lax.optimization_barrier((landed, mixed, gram))
    sketch = jnp.take(landed.reshape(devices * most, width), spots, axis=0, mode="clip")
    return (mixed, sketch, gram)


def solution(mesh):
    in_specs = (P(AXES, None), P(AXES), P())
    out_specs = (P(AXES, None), P(AXES, None), P())
    return jax.shard_map(
        on_device, mesh=mesh, in_specs=in_specs, out_specs=out_specs, check_vma=False
    )
```

```python
import functools

import jax
import jax.numpy as jnp
from jax import lax
from jax.experimental import pallas as pl
from jax.experimental.pallas import tpu as pltpu
from jax.sharding import PartitionSpec as P

BLOCK = 256
AXES = ("narrow", "wide")
TURNED = ("wide", "narrow")


def signs(order):
    rows = lax.broadcasted_iota(jnp.int32, (order, order), 0)
    both = rows & lax.broadcasted_iota(jnp.int32, (order, order), 1)
    parity = jnp.zeros((order, order), jnp.int32)
    for level in range(order.bit_length() - 1):
        parity = parity ^ (both >> level & 1)
    return (1 - 2 * parity).astype(jnp.float32)


def local_kernel(scale, flips_ref, panel_ref, out_ref, flags, held, arrived, sent):
    blocks, _, width = panel_ref.shape
    per = BLOCK // flips_ref.shape[1]
    share = blocks // 4
    loads = [pltpu.make_async_copy(flips_ref, flags, arrived.at[4])]
    for part in range(4):
        span = pl.ds(part * share, share)
        loads.append(pltpu.make_async_copy(panel_ref.at[span], held.at[span], arrived.at[part]))
    for load in loads:
        load.start()
    base = signs(BLOCK)
    loads[0].wait()
    for b in range(blocks):
        if b % share == 0:
            loads[1 + b // share].wait()
        row = jnp.concatenate([flags[b * per + i : b * per + i + 1, :] for i in range(per)], axis=1)
        mixer = (base * (1 - 2 * row).astype(jnp.float32)).astype(jnp.bfloat16)
        values = held[b]
        high = values.astype(jnp.bfloat16)
        rest = values - high.astype(jnp.float32)
        middle = rest.astype(jnp.bfloat16)
        low = (rest - middle.astype(jnp.float32)).astype(jnp.bfloat16)
        parts = jnp.concatenate([high, middle, low], axis=1)
        out = jnp.dot(mixer, parts, preferred_element_type=jnp.float32)
        held[b] = out[:, :width] + out[:, width : 2 * width] + out[:, 2 * width :]
    strip = 16
    quarter = BLOCK // 4

    def body(step, carry):
        at = pl.multiple_of(step * strip, strip)
        items = [held[b, pl.ds(at, strip), :] for b in range(blocks)]
        apart = 1
        while apart < blocks:
            items = [
                items[b] + items[b ^ apart] if b & apart == 0 else items[b ^ apart] - items[b]
                for b in range(blocks)
            ]
            apart *= 2
        for b in range(blocks):
            held[b, pl.ds(at, strip), :] = items[b] * scale
        return carry

    copies = []
    for part in range(4):
        first = part * quarter // strip
        lax.fori_loop(first, first + quarter // strip, body, 0)
        span = pl.ds(part * quarter, quarter)
        copies.append(
            pltpu.make_async_copy(held.at[:, span, :], out_ref.at[:, span, :], sent.at[part])
        )
        copies[-1].start()
    for copy in copies:
        copy.wait()


def local_transform(panel, flips, scale):
    rows, width = panel.shape
    shape = (rows // BLOCK, BLOCK, width)
    return pl.pallas_call(
        functools.partial(local_kernel, scale),
        out_shape=jax.ShapeDtypeStruct(shape, jnp.float32),
        in_specs=[pl.BlockSpec(memory_space=pl.ANY)] * 2,
        out_specs=pl.BlockSpec(memory_space=pl.ANY),
        scratch_shapes=[
            pltpu.VMEM((rows // 128, 128), jnp.int32),
            pltpu.VMEM(shape, jnp.float32),
            pltpu.SemaphoreType.DMA((5,)),
            pltpu.SemaphoreType.DMA((4,)),
        ],
        compiler_params=pltpu.CompilerParams(vmem_limit_bytes=61 * 2**20),
    )(flips.reshape(rows // 128, 128), panel.reshape(shape))


def device_kernel(in_ref, out_ref, held, sent):
    devices, rows, _ = in_ref.shape
    strip = 8
    quarter = rows // 4

    def body(step, carry):
        at = pl.multiple_of(step * strip, strip)
        items = [in_ref[d, pl.ds(at, strip), :] for d in range(devices)]
        apart = 1
        while apart < devices:
            items = [
                items[d] + items[d ^ apart] if d & apart == 0 else items[d ^ apart] - items[d]
                for d in range(devices)
            ]
            apart *= 2
        for d in range(devices):
            held[d, pl.ds(at, strip), :] = items[d]
        return carry

    copies = []
    for part in range(4):
        first = part * quarter // strip
        lax.fori_loop(first, first + quarter // strip, body, 0)
        span = pl.ds(part * quarter, quarter)
        copies.append(
            pltpu.make_async_copy(held.at[:, span, :], out_ref.at[:, span, :], sent.at[part])
        )
        copies[-1].start()
    for copy in copies:
        copy.wait()


def device_sums(value):
    return pl.pallas_call(
        device_kernel,
        out_shape=jax.ShapeDtypeStruct(value.shape, jnp.float32),
        in_specs=[pl.BlockSpec(memory_space=pltpu.VMEM)],
        out_specs=pl.BlockSpec(memory_space=pl.ANY),
        scratch_shapes=[
            pltpu.VMEM(value.shape, jnp.float32),
            pltpu.SemaphoreType.DMA((4,)),
        ],
        compiler_params=pltpu.CompilerParams(vmem_limit_bytes=32 * 2**20),
    )(value)


def store_kernel(value_ref, out_ref, sent):
    copy = pltpu.make_async_copy(value_ref, out_ref, sent)
    copy.start()
    copy.wait()


def store(value):
    return pl.pallas_call(
        store_kernel,
        out_shape=jax.ShapeDtypeStruct(value.shape, jnp.float32),
        in_specs=[pl.BlockSpec(memory_space=pltpu.VMEM)],
        out_specs=pl.BlockSpec(memory_space=pl.ANY),
        scratch_shapes=[pltpu.SemaphoreType.DMA],
        compiler_params=pltpu.CompilerParams(vmem_limit_bytes=8 * 2**20),
    )(value)


def index_kernel(rows_here, most, bases_ref, picks_ref, out_ref):
    picks = picks_ref[...]
    devices, per = picks.shape
    before = lax.broadcasted_iota(jnp.int32, (per, per), 0)
    earlier = before < lax.broadcasted_iota(jnp.int32, (per, per), 1)
    earlier = jnp.where(earlier, 1.0, 0.0).astype(jnp.bfloat16)
    for which in range(out_ref.shape[0]):
        offsets = picks - bases_ref[which]
        owned = (offsets >= 0) & (offsets < rows_here)
        ones = jnp.where(owned, 1.0, 0.0).astype(jnp.bfloat16)
        rank = jnp.dot(ones, earlier, preferred_element_type=jnp.float32)
        rank = jnp.where(owned, rank, -1.0)
        marked = (offsets + 1).astype(jnp.float32)
        for slot in range(most):
            hit = jnp.where(rank == float(slot), marked, 0.0)
            row = jnp.sum(hit, axis=1, keepdims=True).astype(jnp.int32) - 1
            out_ref[which, :, slot : slot + 1] = row


def send_rows(picks, owners, rows_here, devices, most):
    bases = jnp.stack(owners) * rows_here
    rows = pl.pallas_call(
        functools.partial(index_kernel, rows_here, most),
        out_shape=jax.ShapeDtypeStruct((len(owners), devices, most), jnp.int32),
        in_specs=[
            pl.BlockSpec(memory_space=pltpu.SMEM),
            pl.BlockSpec(memory_space=pltpu.VMEM),
        ],
        out_specs=pl.BlockSpec(memory_space=pltpu.VMEM),
        compiler_params=pltpu.CompilerParams(vmem_limit_bytes=8 * 2**20),
    )(bases.astype(jnp.int32), picks.reshape(devices, -1))
    return rows.reshape(len(owners) * devices * most)


def count_kernel(rows_here, wide, me_ref, picks_ref, out_ref):
    picks = picks_ref[...]
    rows, devices = out_ref.shape
    owner = picks >> rows_here.bit_length() - 1
    owner = (owner & wide - 1) * (devices // wide) + (owner >> wide.bit_length() - 1)
    local = picks & rows_here - 1
    held = local >> rows.bit_length() - 1 == me_ref[0]
    place = jnp.where(held, local & rows - 1, -1)
    shape = (devices, picks.shape[1])
    owners = jnp.where(lax.broadcasted_iota(jnp.int32, shape, 0) == owner, 1.0, 0.0)
    shape = (rows, picks.shape[1])
    places = jnp.where(lax.broadcasted_iota(jnp.int32, shape, 0) == place, 1.0, 0.0)
    out_ref[...] = lax.dot_general(
        places.astype(jnp.bfloat16),
        owners.astype(jnp.bfloat16),
        (((1,), (1,)), ((), ())),
        preferred_element_type=jnp.float32,
    )


def count_picks(picks, me, rows_here, devices):
    return pl.pallas_call(
        functools.partial(count_kernel, rows_here, lax.axis_size("wide")),
        out_shape=jax.ShapeDtypeStruct((rows_here // devices, devices), jnp.float32),
        in_specs=[
            pl.BlockSpec(memory_space=pltpu.SMEM),
            pl.BlockSpec(memory_space=pltpu.VMEM),
        ],
        out_specs=pl.BlockSpec(memory_space=pltpu.VMEM),
        compiler_params=pltpu.CompilerParams(vmem_limit_bytes=32 * 2**20),
    )(me.reshape(1).astype(jnp.int32), picks.reshape(1, -1))


def halves(value):
    high = value.astype(jnp.bfloat16)
    return high, (value - high.astype(jnp.float32)).astype(jnp.bfloat16)


def part_kernel(counts_ref, held_ref, out_ref):
    devices, _, width = held_ref.shape
    total = jnp.zeros((width, 2 * width), jnp.float32)
    rest = jnp.zeros((width, width), jnp.float32)
    for d in range(devices):
        rows = held_ref[d]
        high, low = halves(rows)
        weighted, spare = halves(rows * counts_ref[:, d : d + 1])
        over_rows = (((0,), (0,)), ((), ()))
        both = jnp.concatenate([weighted, spare], axis=1)
        total += lax.dot_general(high, both, over_rows, preferred_element_type=jnp.float32)
        rest += lax.dot_general(low, weighted, over_rows, preferred_element_type=jnp.float32)
    out_ref[...] = total[:, :width] + total[:, width:] + rest


def gram_part(counts, held):
    width = held.shape[2]
    return pl.pallas_call(
        part_kernel,
        out_shape=jax.ShapeDtypeStruct((width, width), jnp.float32),
        in_specs=[pl.BlockSpec(memory_space=pltpu.VMEM)] * 2,
        out_specs=pl.BlockSpec(memory_space=pltpu.VMEM),
        compiler_params=pltpu.CompilerParams(vmem_limit_bytes=32 * 2**20),
    )(counts, held)


def add_partner(value, axis, level):
    pairs = [(source, source ^ 2**level) for source in range(lax.axis_size(axis))]
    return value + lax.ppermute(value, axis, pairs)


def landing(block, rows_here, most):
    owners = block // rows_here
    order = jnp.arange(block.shape[0], dtype=jnp.int32)
    earlier = (owners[:, None] == owners[None, :]) & (order[None, :] < order[:, None])
    return owners * most + jnp.sum(earlier.astype(jnp.int32), axis=1)


def on_device(panel, flips, picks):
    rows_here, width = panel.shape
    devices = lax.axis_size("narrow") * lax.axis_size("wide")
    scale = 1.0 / float(rows_here * devices) ** 0.5
    me = lax.axis_index(AXES)
    per = picks.shape[0] // devices
    most = -(-per // devices)

    local = local_transform(panel, flips, scale)
    local = local.reshape(devices, rows_here // devices, width)
    wanted = send_rows(picks, [me], rows_here, devices, most)
    spots = landing(lax.dynamic_slice(picks, (me * per,), (per,)), rows_here, most)
    counts = count_picks(picks, lax.axis_index(TURNED), rows_here, devices)
    slices = lax.all_to_all(local, TURNED, 0, 0, tiled=True)
    slices, wanted, spots, counts = lax.optimization_barrier((slices, wanted, spots, counts))
    slices = device_sums(slices)
    mixed = lax.all_to_all(slices, TURNED, 0, 0, tiled=True)
    gram = gram_part(counts, slices)
    levels = [(axis, l) for axis in AXES for l in range(lax.axis_size(axis).bit_length() - 1)]
    levels = levels[:1] + levels[2:] + levels[1:2]
    for axis, level in levels[:-1]:
        gram = add_partner(gram, axis, level)
    mixed, gram = lax.optimization_barrier((mixed, gram))
    mixed = mixed.reshape(rows_here, width)
    chosen = jnp.take(mixed, wanted, axis=0, mode="clip")
    landed = lax.all_to_all(chosen.reshape(devices, most, width), AXES, 0, 0, tiled=True)
    gram = add_partner(gram, *levels[-1]) / float(picks.shape[0])
    mixed = store(mixed)
    landed, mixed, gram = lax.optimization_barrier((landed, mixed, gram))
    sketch = jnp.take(landed.reshape(devices * most, width), spots, axis=0, mode="clip")
    return (mixed, sketch, gram)


def solution(mesh):
    in_specs = (P(AXES, None), P(AXES), P())
    out_specs = (P(AXES, None), P(AXES, None), P())
    return jax.shard_map(
        on_device, mesh=mesh, in_specs=in_specs, out_specs=out_specs, check_vma=False
    )
```

```python
import functools

import jax
import jax.numpy as jnp
from jax import lax
from jax.experimental import pallas as pl
from jax.experimental.pallas import tpu as pltpu
from jax.sharding import PartitionSpec as P

BLOCK = 256
AXES = ("narrow", "wide")
TURNED = ("wide", "narrow")


def signs(order):
    rows = lax.broadcasted_iota(jnp.int32, (order, order), 0)
    both = rows & lax.broadcasted_iota(jnp.int32, (order, order), 1)
    parity = jnp.zeros((order, order), jnp.int32)
    for level in range(order.bit_length() - 1):
        parity = parity ^ (both >> level & 1)
    return (1 - 2 * parity).astype(jnp.float32)


def local_kernel(scale, flips_ref, panel_ref, out_ref, flags, held, arrived, sent):
    blocks, _, width = panel_ref.shape
    per = BLOCK // flips_ref.shape[1]
    share = blocks // 4
    loads = [pltpu.make_async_copy(flips_ref, flags, arrived.at[4])]
    for part in range(4):
        span = pl.ds(part * share, share)
        loads.append(pltpu.make_async_copy(panel_ref.at[span], held.at[span], arrived.at[part]))
    for load in loads:
        load.start()
    base = signs(BLOCK)
    loads[0].wait()
    for b in range(blocks):
        if b % share == 0:
            loads[1 + b // share].wait()
        row = jnp.concatenate([flags[b * per + i : b * per + i + 1, :] for i in range(per)], axis=1)
        mixer = (base * (1 - 2 * row).astype(jnp.float32)).astype(jnp.bfloat16)
        values = held[b]
        high = values.astype(jnp.bfloat16)
        rest = values - high.astype(jnp.float32)
        middle = rest.astype(jnp.bfloat16)
        low = (rest - middle.astype(jnp.float32)).astype(jnp.bfloat16)
        parts = jnp.concatenate([high, middle, low], axis=1)
        out = jnp.dot(mixer, parts, preferred_element_type=jnp.float32)
        held[b] = out[:, :width] + out[:, width : 2 * width] + out[:, 2 * width :]
    strip = 16
    quarter = BLOCK // 4

    def body(step, carry):
        at = pl.multiple_of(step * strip, strip)
        items = [held[b, pl.ds(at, strip), :] for b in range(blocks)]
        apart = 1
        while apart < blocks:
            items = [
                items[b] + items[b ^ apart] if b & apart == 0 else items[b ^ apart] - items[b]
                for b in range(blocks)
            ]
            apart *= 2
        for b in range(blocks):
            held[b, pl.ds(at, strip), :] = items[b] * scale
        return carry

    copies = []
    for part in range(4):
        first = part * quarter // strip
        lax.fori_loop(first, first + quarter // strip, body, 0)
        span = pl.ds(part * quarter, quarter)
        copies.append(
            pltpu.make_async_copy(held.at[:, span, :], out_ref.at[:, span, :], sent.at[part])
        )
        copies[-1].start()
    for copy in copies:
        copy.wait()


def local_transform(panel, flips, scale):
    rows, width = panel.shape
    shape = (rows // BLOCK, BLOCK, width)
    return pl.pallas_call(
        functools.partial(local_kernel, scale),
        out_shape=jax.ShapeDtypeStruct(shape, jnp.float32),
        in_specs=[pl.BlockSpec(memory_space=pl.ANY)] * 2,
        out_specs=pl.BlockSpec(memory_space=pl.ANY),
        scratch_shapes=[
            pltpu.VMEM((rows // 128, 128), jnp.int32),
            pltpu.VMEM(shape, jnp.float32),
            pltpu.SemaphoreType.DMA((5,)),
            pltpu.SemaphoreType.DMA((4,)),
        ],
        compiler_params=pltpu.CompilerParams(vmem_limit_bytes=61 * 2**20),
    )(flips.reshape(rows // 128, 128), panel.reshape(shape))


def device_kernel(in_ref, out_ref, held, sent):
    devices, rows, _ = in_ref.shape
    strip = 8
    quarter = rows // 4

    def body(step, carry):
        at = pl.multiple_of(step * strip, strip)
        items = [in_ref[d, pl.ds(at, strip), :] for d in range(devices)]
        apart = 1
        while apart < devices:
            items = [
                items[d] + items[d ^ apart] if d & apart == 0 else items[d ^ apart] - items[d]
                for d in range(devices)
            ]
            apart *= 2
        for d in range(devices):
            held[d, pl.ds(at, strip), :] = items[d]
        return carry

    copies = []
    for part in range(4):
        first = part * quarter // strip
        lax.fori_loop(first, first + quarter // strip, body, 0)
        span = pl.ds(part * quarter, quarter)
        copies.append(
            pltpu.make_async_copy(held.at[:, span, :], out_ref.at[:, span, :], sent.at[part])
        )
        copies[-1].start()
    for copy in copies:
        copy.wait()


def device_sums(value):
    return pl.pallas_call(
        device_kernel,
        out_shape=jax.ShapeDtypeStruct(value.shape, jnp.float32),
        in_specs=[pl.BlockSpec(memory_space=pltpu.VMEM)],
        out_specs=pl.BlockSpec(memory_space=pl.ANY),
        scratch_shapes=[
            pltpu.VMEM(value.shape, jnp.float32),
            pltpu.SemaphoreType.DMA((4,)),
        ],
        compiler_params=pltpu.CompilerParams(vmem_limit_bytes=32 * 2**20),
    )(value)


def store_kernel(value_ref, out_ref, sent):
    copy = pltpu.make_async_copy(value_ref, out_ref, sent)
    copy.start()
    copy.wait()


def store(value):
    return pl.pallas_call(
        store_kernel,
        out_shape=jax.ShapeDtypeStruct(value.shape, jnp.float32),
        in_specs=[pl.BlockSpec(memory_space=pltpu.VMEM)],
        out_specs=pl.BlockSpec(memory_space=pl.ANY),
        scratch_shapes=[pltpu.SemaphoreType.DMA],
        compiler_params=pltpu.CompilerParams(vmem_limit_bytes=8 * 2**20),
    )(value)


def index_kernel(rows_here, most, bases_ref, picks_ref, out_ref):
    picks = picks_ref[...]
    devices, per = picks.shape
    before = lax.broadcasted_iota(jnp.int32, (per, per), 0)
    earlier = before < lax.broadcasted_iota(jnp.int32, (per, per), 1)
    earlier = jnp.where(earlier, 1.0, 0.0).astype(jnp.bfloat16)
    for which in range(out_ref.shape[0]):
        offsets = picks - bases_ref[which]
        owned = (offsets >= 0) & (offsets < rows_here)
        ones = jnp.where(owned, 1.0, 0.0).astype(jnp.bfloat16)
        rank = jnp.dot(ones, earlier, preferred_element_type=jnp.float32)
        rank = jnp.where(owned, rank, -1.0)
        marked = (offsets + 1).astype(jnp.float32)
        for slot in range(most):
            hit = jnp.where(rank == float(slot), marked, 0.0)
            row = jnp.sum(hit, axis=1, keepdims=True).astype(jnp.int32) - 1
            out_ref[which, :, slot : slot + 1] = row


def send_rows(picks, owners, rows_here, devices, most):
    bases = jnp.stack(owners) * rows_here
    rows = pl.pallas_call(
        functools.partial(index_kernel, rows_here, most),
        out_shape=jax.ShapeDtypeStruct((len(owners), devices, most), jnp.int32),
        in_specs=[
            pl.BlockSpec(memory_space=pltpu.SMEM),
            pl.BlockSpec(memory_space=pltpu.VMEM),
        ],
        out_specs=pl.BlockSpec(memory_space=pltpu.VMEM),
        compiler_params=pltpu.CompilerParams(vmem_limit_bytes=8 * 2**20),
    )(bases.astype(jnp.int32), picks.reshape(devices, -1))
    return rows.reshape(len(owners) * devices * most)


def count_kernel(rows_here, wide, me_ref, picks_ref, out_ref):
    picks = picks_ref[...]
    rows, devices = out_ref.shape
    owner = picks >> rows_here.bit_length() - 1
    owner = (owner & wide - 1) * (devices // wide) + (owner >> wide.bit_length() - 1)
    local = picks & rows_here - 1
    held = local >> rows.bit_length() - 1 == me_ref[0]
    place = jnp.where(held, local & rows - 1, -1)
    shape = (devices, picks.shape[1])
    owners = jnp.where(lax.broadcasted_iota(jnp.int32, shape, 0) == owner, 1.0, 0.0)
    shape = (rows, picks.shape[1])
    places = jnp.where(lax.broadcasted_iota(jnp.int32, shape, 0) == place, 1.0, 0.0)
    out_ref[...] = lax.dot_general(
        places.astype(jnp.bfloat16),
        owners.astype(jnp.bfloat16),
        (((1,), (1,)), ((), ())),
        preferred_element_type=jnp.float32,
    )


def count_picks(picks, me, rows_here, devices):
    return pl.pallas_call(
        functools.partial(count_kernel, rows_here, lax.axis_size("wide")),
        out_shape=jax.ShapeDtypeStruct((rows_here // devices, devices), jnp.float32),
        in_specs=[
            pl.BlockSpec(memory_space=pltpu.SMEM),
            pl.BlockSpec(memory_space=pltpu.VMEM),
        ],
        out_specs=pl.BlockSpec(memory_space=pltpu.VMEM),
        compiler_params=pltpu.CompilerParams(vmem_limit_bytes=32 * 2**20),
    )(me.reshape(1).astype(jnp.int32), picks.reshape(1, -1))


def halves(value):
    high = value.astype(jnp.bfloat16)
    return high, (value - high.astype(jnp.float32)).astype(jnp.bfloat16)


def part_kernel(counts_ref, held_ref, out_ref):
    devices, _, width = held_ref.shape
    total = jnp.zeros((width, 2 * width), jnp.float32)
    rest = jnp.zeros((width, width), jnp.float32)
    for d in range(devices):
        rows = held_ref[d]
        high, low = halves(rows)
        weighted, spare = halves(rows * counts_ref[:, d : d + 1])
        over_rows = (((0,), (0,)), ((), ()))
        both = jnp.concatenate([weighted, spare], axis=1)
        total += lax.dot_general(high, both, over_rows, preferred_element_type=jnp.float32)
        rest += lax.dot_general(low, weighted, over_rows, preferred_element_type=jnp.float32)
    out_ref[...] = total[:, :width] + total[:, width:] + rest


def gram_part(counts, held):
    width = held.shape[2]
    return pl.pallas_call(
        part_kernel,
        out_shape=jax.ShapeDtypeStruct((width, width), jnp.float32),
        in_specs=[pl.BlockSpec(memory_space=pltpu.VMEM)] * 2,
        out_specs=pl.BlockSpec(memory_space=pltpu.VMEM),
        compiler_params=pltpu.CompilerParams(vmem_limit_bytes=32 * 2**20),
    )(counts, held)


def swap(value, axis, apart):
    pairs = [(source, source ^ apart) for source in range(lax.axis_size(axis))]
    return lax.ppermute(value, axis, pairs)


def scatter_sum(value, axis):
    upper = lax.axis_index(axis) & 1
    half = value.shape[0] // 2
    keep = lax.dynamic_slice_in_dim(value, upper * half, half)
    give = lax.dynamic_slice_in_dim(value, (1 - upper) * half, half)
    return keep + swap(give, axis, 1)


def join(value, axis):
    upper = lax.axis_index(axis) & 1 == 1
    other = swap(value, axis, 1)
    first = jnp.where(upper, other, value)
    return jnp.concatenate([first, jnp.where(upper, value, other)], axis=0)


def landing(block, rows_here, most):
    owners = block // rows_here
    order = jnp.arange(block.shape[0], dtype=jnp.int32)
    earlier = (owners[:, None] == owners[None, :]) & (order[None, :] < order[:, None])
    return owners * most + jnp.sum(earlier.astype(jnp.int32), axis=1)


def on_device(panel, flips, picks):
    rows_here, width = panel.shape
    devices = lax.axis_size("narrow") * lax.axis_size("wide")
    scale = 1.0 / float(rows_here * devices) ** 0.5
    me = lax.axis_index(AXES)
    per = picks.shape[0] // devices
    most = -(-per // devices)

    local = local_transform(panel, flips, scale)
    local = local.reshape(devices, rows_here // devices, width)
    wanted = send_rows(picks, [me], rows_here, devices, most)
    spots = landing(lax.dynamic_slice(picks, (me * per,), (per,)), rows_here, most)
    counts = count_picks(picks, lax.axis_index(TURNED), rows_here, devices)
    slices = lax.all_to_all(local, TURNED, 0, 0, tiled=True)
    slices, wanted, spots, counts = lax.optimization_barrier((slices, wanted, spots, counts))
    slices = device_sums(slices)
    mixed = lax.all_to_all(slices, TURNED, 0, 0, tiled=True)
    gram = gram_part(counts, slices)
    gram = scatter_sum(scatter_sum(gram, "narrow"), "wide")
    far = lax.axis_size("wide") // 4
    near, one, two = [swap(gram, "wide", apart * far) for apart in (1, 2, 3)]
    gram = (gram + near) + (one + two)
    mixed, gram = lax.optimization_barrier((mixed, gram))
    mixed = mixed.reshape(rows_here, width)
    chosen = jnp.take(mixed, wanted, axis=0, mode="clip")
    chosen, gram = lax.optimization_barrier((chosen, gram))
    landed = lax.all_to_all(chosen.reshape(devices, most, width), AXES, 0, 0, tiled=True)
    for axis, low, high in (("narrow", 2, lax.axis_size("narrow")), ("wide", 2, far)):
        while low < high:
            gram = gram + swap(gram, axis, low)
            low *= 2
    gram = join(join(gram / float(picks.shape[0]), "wide"), "narrow")
    mixed = store(mixed)
    landed, mixed, gram = lax.optimization_barrier((landed, mixed, gram))
    sketch = jnp.take(landed.reshape(devices * most, width), spots, axis=0, mode="clip")
    return (mixed, sketch, gram)


def solution(mesh):
    in_specs = (P(AXES, None), P(AXES), P())
    out_specs = (P(AXES, None), P(AXES, None), P())
    return jax.shard_map(
        on_device, mesh=mesh, in_specs=in_specs, out_specs=out_specs, check_vma=False
    )
```

```python
import functools

import jax
import jax.numpy as jnp
from jax import lax
from jax.experimental import pallas as pl
from jax.experimental.pallas import tpu as pltpu
from jax.sharding import PartitionSpec as P

BLOCK = 256
AXES = ("narrow", "wide")
TURNED = ("wide", "narrow")


def signs(order):
    rows = lax.broadcasted_iota(jnp.int32, (order, order), 0)
    both = rows & lax.broadcasted_iota(jnp.int32, (order, order), 1)
    parity = jnp.zeros((order, order), jnp.int32)
    for level in range(order.bit_length() - 1):
        parity = parity ^ (both >> level & 1)
    return (1 - 2 * parity).astype(jnp.float32)


def local_kernel(scale, flips_ref, panel_ref, out_ref, flags, held, arrived, sent):
    blocks, _, width = panel_ref.shape
    per = BLOCK // flips_ref.shape[1]
    share = blocks // 4
    loads = [pltpu.make_async_copy(flips_ref, flags, arrived.at[4])]
    for part in range(4):
        span = pl.ds(part * share, share)
        loads.append(pltpu.make_async_copy(panel_ref.at[span], held.at[span], arrived.at[part]))
    for load in loads:
        load.start()
    base = signs(BLOCK)
    loads[0].wait()
    for b in range(blocks):
        if b % share == 0:
            loads[1 + b // share].wait()
        row = jnp.concatenate([flags[b * per + i : b * per + i + 1, :] for i in range(per)], axis=1)
        mixer = (base * (1 - 2 * row).astype(jnp.float32)).astype(jnp.bfloat16)
        values = held[b]
        high = values.astype(jnp.bfloat16)
        rest = values - high.astype(jnp.float32)
        middle = rest.astype(jnp.bfloat16)
        low = (rest - middle.astype(jnp.float32)).astype(jnp.bfloat16)
        parts = jnp.concatenate([high, middle, low], axis=1)
        out = jnp.dot(mixer, parts, preferred_element_type=jnp.float32)
        held[b] = out[:, :width] + out[:, width : 2 * width] + out[:, 2 * width :]
    strip = 16
    quarter = BLOCK // 4

    def body(step, carry):
        at = pl.multiple_of(step * strip, strip)
        items = [held[b, pl.ds(at, strip), :] for b in range(blocks)]
        apart = 1
        while apart < blocks:
            items = [
                items[b] + items[b ^ apart] if b & apart == 0 else items[b ^ apart] - items[b]
                for b in range(blocks)
            ]
            apart *= 2
        for b in range(blocks):
            held[b, pl.ds(at, strip), :] = items[b] * scale
        return carry

    copies = []
    for part in range(4):
        first = part * quarter // strip
        lax.fori_loop(first, first + quarter // strip, body, 0)
        span = pl.ds(part * quarter, quarter)
        copies.append(
            pltpu.make_async_copy(held.at[:, span, :], out_ref.at[:, span, :], sent.at[part])
        )
        copies[-1].start()
    for copy in copies:
        copy.wait()


def local_transform(panel, flips, scale):
    rows, width = panel.shape
    shape = (rows // BLOCK, BLOCK, width)
    return pl.pallas_call(
        functools.partial(local_kernel, scale),
        out_shape=jax.ShapeDtypeStruct(shape, jnp.float32),
        in_specs=[pl.BlockSpec(memory_space=pl.ANY)] * 2,
        out_specs=pl.BlockSpec(memory_space=pl.ANY),
        scratch_shapes=[
            pltpu.VMEM((rows // 128, 128), jnp.int32),
            pltpu.VMEM(shape, jnp.float32),
            pltpu.SemaphoreType.DMA((5,)),
            pltpu.SemaphoreType.DMA((4,)),
        ],
        compiler_params=pltpu.CompilerParams(vmem_limit_bytes=61 * 2**20),
    )(flips.reshape(rows // 128, 128), panel.reshape(shape))


def device_kernel(in_ref, out_ref, held, sent):
    devices, rows, _ = in_ref.shape
    strip = 8
    quarter = rows // 4

    def body(step, carry):
        at = pl.multiple_of(step * strip, strip)
        items = [in_ref[d, pl.ds(at, strip), :] for d in range(devices)]
        apart = 1
        while apart < devices:
            items = [
                items[d] + items[d ^ apart] if d & apart == 0 else items[d ^ apart] - items[d]
                for d in range(devices)
            ]
            apart *= 2
        for d in range(devices):
            held[d, pl.ds(at, strip), :] = items[d]
        return carry

    copies = []
    for part in range(4):
        first = part * quarter // strip
        lax.fori_loop(first, first + quarter // strip, body, 0)
        span = pl.ds(part * quarter, quarter)
        copies.append(
            pltpu.make_async_copy(held.at[:, span, :], out_ref.at[:, span, :], sent.at[part])
        )
        copies[-1].start()
    for copy in copies:
        copy.wait()


def device_sums(value):
    return pl.pallas_call(
        device_kernel,
        out_shape=jax.ShapeDtypeStruct(value.shape, jnp.float32),
        in_specs=[pl.BlockSpec(memory_space=pltpu.VMEM)],
        out_specs=pl.BlockSpec(memory_space=pl.ANY),
        scratch_shapes=[
            pltpu.VMEM(value.shape, jnp.float32),
            pltpu.SemaphoreType.DMA((4,)),
        ],
        compiler_params=pltpu.CompilerParams(vmem_limit_bytes=32 * 2**20),
    )(value)


def store_kernel(value_ref, out_ref, sent):
    copy = pltpu.make_async_copy(value_ref, out_ref, sent)
    copy.start()
    copy.wait()


def store(value):
    return pl.pallas_call(
        store_kernel,
        out_shape=jax.ShapeDtypeStruct(value.shape, jnp.float32),
        in_specs=[pl.BlockSpec(memory_space=pltpu.VMEM)],
        out_specs=pl.BlockSpec(memory_space=pl.ANY),
        scratch_shapes=[pltpu.SemaphoreType.DMA],
        compiler_params=pltpu.CompilerParams(vmem_limit_bytes=8 * 2**20),
    )(value)


def index_kernel(rows_here, most, bases_ref, picks_ref, out_ref):
    picks = picks_ref[...]
    devices, per = picks.shape
    before = lax.broadcasted_iota(jnp.int32, (per, per), 0)
    earlier = before < lax.broadcasted_iota(jnp.int32, (per, per), 1)
    earlier = jnp.where(earlier, 1.0, 0.0).astype(jnp.bfloat16)
    for which in range(out_ref.shape[0]):
        offsets = picks - bases_ref[which]
        owned = (offsets >= 0) & (offsets < rows_here)
        ones = jnp.where(owned, 1.0, 0.0).astype(jnp.bfloat16)
        rank = jnp.dot(ones, earlier, preferred_element_type=jnp.float32)
        rank = jnp.where(owned, rank, -1.0)
        marked = (offsets + 1).astype(jnp.float32)
        for slot in range(most):
            hit = jnp.where(rank == float(slot), marked, 0.0)
            row = jnp.sum(hit, axis=1, keepdims=True).astype(jnp.int32) - 1
            out_ref[which, :, slot : slot + 1] = row


def send_rows(picks, owners, rows_here, devices, most):
    bases = jnp.stack(owners) * rows_here
    rows = pl.pallas_call(
        functools.partial(index_kernel, rows_here, most),
        out_shape=jax.ShapeDtypeStruct((len(owners), devices, most), jnp.int32),
        in_specs=[
            pl.BlockSpec(memory_space=pltpu.SMEM),
            pl.BlockSpec(memory_space=pltpu.VMEM),
        ],
        out_specs=pl.BlockSpec(memory_space=pltpu.VMEM),
        compiler_params=pltpu.CompilerParams(vmem_limit_bytes=8 * 2**20),
    )(bases.astype(jnp.int32), picks.reshape(devices, -1))
    return rows.reshape(len(owners) * devices * most)


def count_kernel(rows_here, wide, me_ref, picks_ref, out_ref):
    picks = picks_ref[...]
    rows, devices = out_ref.shape
    owner = picks >> rows_here.bit_length() - 1
    owner = (owner & wide - 1) * (devices // wide) + (owner >> wide.bit_length() - 1)
    local = picks & rows_here - 1
    held = local >> rows.bit_length() - 1 == me_ref[0]
    place = jnp.where(held, local & rows - 1, -1)
    shape = (devices, picks.shape[1])
    owners = jnp.where(lax.broadcasted_iota(jnp.int32, shape, 0) == owner, 1.0, 0.0)
    shape = (rows, picks.shape[1])
    places = jnp.where(lax.broadcasted_iota(jnp.int32, shape, 0) == place, 1.0, 0.0)
    out_ref[...] = lax.dot_general(
        places.astype(jnp.bfloat16),
        owners.astype(jnp.bfloat16),
        (((1,), (1,)), ((), ())),
        preferred_element_type=jnp.float32,
    )


def count_picks(picks, me, rows_here, devices):
    return pl.pallas_call(
        functools.partial(count_kernel, rows_here, lax.axis_size("wide")),
        out_shape=jax.ShapeDtypeStruct((rows_here // devices, devices), jnp.float32),
        in_specs=[
            pl.BlockSpec(memory_space=pltpu.SMEM),
            pl.BlockSpec(memory_space=pltpu.VMEM),
        ],
        out_specs=pl.BlockSpec(memory_space=pltpu.VMEM),
        compiler_params=pltpu.CompilerParams(vmem_limit_bytes=32 * 2**20),
    )(me.reshape(1).astype(jnp.int32), picks.reshape(1, -1))


def halves(value):
    high = value.astype(jnp.bfloat16)
    return high, (value - high.astype(jnp.float32)).astype(jnp.bfloat16)


def part_kernel(counts_ref, held_ref, out_ref):
    devices, _, width = held_ref.shape
    total = jnp.zeros((width, 2 * width), jnp.float32)
    rest = jnp.zeros((width, width), jnp.float32)
    for d in range(devices):
        rows = held_ref[d]
        high, low = halves(rows)
        weighted, spare = halves(rows * counts_ref[:, d : d + 1])
        over_rows = (((0,), (0,)), ((), ()))
        both = jnp.concatenate([weighted, spare], axis=1)
        total += lax.dot_general(high, both, over_rows, preferred_element_type=jnp.float32)
        rest += lax.dot_general(low, weighted, over_rows, preferred_element_type=jnp.float32)
    out_ref[...] = total[:, :width] + total[:, width:] + rest


def gram_part(counts, held):
    width = held.shape[2]
    return pl.pallas_call(
        part_kernel,
        out_shape=jax.ShapeDtypeStruct((width, width), jnp.float32),
        in_specs=[pl.BlockSpec(memory_space=pltpu.VMEM)] * 2,
        out_specs=pl.BlockSpec(memory_space=pltpu.VMEM),
        compiler_params=pltpu.CompilerParams(vmem_limit_bytes=32 * 2**20),
    )(counts, held)


def swap(value, axis, apart):
    pairs = [(source, source ^ apart) for source in range(lax.axis_size(axis))]
    return lax.ppermute(value, axis, pairs)


def scatter_sum(value, axis):
    upper = lax.axis_index(axis) & 1
    half = value.shape[0] // 2
    keep = lax.dynamic_slice_in_dim(value, upper * half, half)
    give = lax.dynamic_slice_in_dim(value, (1 - upper) * half, half)
    return keep + swap(give, axis, 1)


def join(value, axis):
    upper = lax.axis_index(axis) & 1 == 1
    other = swap(value, axis, 1)
    first = jnp.where(upper, other, value)
    return jnp.concatenate([first, jnp.where(upper, value, other)], axis=0)


def landing(block, rows_here, most):
    owners = block // rows_here
    order = jnp.arange(block.shape[0], dtype=jnp.int32)
    earlier = (owners[:, None] == owners[None, :]) & (order[None, :] < order[:, None])
    return owners * most + jnp.sum(earlier.astype(jnp.int32), axis=1)


def on_device(panel, flips, picks):
    rows_here, width = panel.shape
    devices = lax.axis_size("narrow") * lax.axis_size("wide")
    scale = 1.0 / float(rows_here * devices) ** 0.5
    me = lax.axis_index(AXES)
    per = picks.shape[0] // devices
    most = -(-per // devices)

    local = local_transform(panel, flips, scale)
    local = local.reshape(devices, rows_here // devices, width)
    wanted = send_rows(picks, [me], rows_here, devices, most)
    spots = landing(lax.dynamic_slice(picks, (me * per,), (per,)), rows_here, most)
    counts = count_picks(picks, lax.axis_index(TURNED), rows_here, devices)
    slices = lax.all_to_all(local, TURNED, 0, 0, tiled=True)
    slices, wanted, spots, counts = lax.optimization_barrier((slices, wanted, spots, counts))
    slices = device_sums(slices)
    mixed = lax.all_to_all(slices, TURNED, 0, 0, tiled=True)
    gram = gram_part(counts, slices)
    gram = scatter_sum(gram, "narrow")
    far = lax.axis_size("wide") // 4
    for axis, low, high in (("wide", 1, far), ("narrow", 2, lax.axis_size("narrow"))):
        while low < high:
            gram = gram + swap(gram, axis, low)
            low *= 2
    near, one, two = [swap(gram, "wide", apart * far) for apart in (1, 2, 3)]
    gram = (gram + near) + (one + two)
    mixed, gram = lax.optimization_barrier((mixed, gram))
    mixed = mixed.reshape(rows_here, width)
    chosen = jnp.take(mixed, wanted, axis=0, mode="clip")
    chosen, gram = lax.optimization_barrier((chosen, gram))
    landed = lax.all_to_all(chosen.reshape(devices, most, width), AXES, 0, 0, tiled=True)
    gram = join(gram / float(picks.shape[0]), "narrow")
    mixed = store(mixed)
    landed, mixed, gram = lax.optimization_barrier((landed, mixed, gram))
    sketch = jnp.take(landed.reshape(devices * most, width), spots, axis=0, mode="clip")
    return (mixed, sketch, gram)


def solution(mesh):
    in_specs = (P(AXES, None), P(AXES), P())
    out_specs = (P(AXES, None), P(AXES, None), P())
    return jax.shard_map(
        on_device, mesh=mesh, in_specs=in_specs, out_specs=out_specs, check_vma=False
    )
```

```python
import functools

import jax
import jax.numpy as jnp
from jax import lax
from jax.experimental import pallas as pl
from jax.experimental.pallas import tpu as pltpu
from jax.sharding import PartitionSpec as P

BLOCK = 256
AXES = ("narrow", "wide")
TURNED = ("wide", "narrow")


def signs(order):
    rows = lax.broadcasted_iota(jnp.int32, (order, order), 0)
    both = rows & lax.broadcasted_iota(jnp.int32, (order, order), 1)
    parity = jnp.zeros((order, order), jnp.int32)
    for level in range(order.bit_length() - 1):
        parity = parity ^ (both >> level & 1)
    return (1 - 2 * parity).astype(jnp.float32)


def local_kernel(scale, flips_ref, panel_ref, out_ref, flags, held, arrived, sent):
    blocks, _, width = panel_ref.shape
    per = BLOCK // flips_ref.shape[1]
    share = blocks // 4
    loads = [pltpu.make_async_copy(flips_ref, flags, arrived.at[4])]
    for part in range(4):
        span = pl.ds(part * share, share)
        loads.append(pltpu.make_async_copy(panel_ref.at[span], held.at[span], arrived.at[part]))
    for load in loads:
        load.start()
    base = signs(BLOCK)
    loads[0].wait()
    for b in range(blocks):
        if b % share == 0:
            loads[1 + b // share].wait()
        row = jnp.concatenate([flags[b * per + i : b * per + i + 1, :] for i in range(per)], axis=1)
        mixer = (base * (1 - 2 * row).astype(jnp.float32)).astype(jnp.bfloat16)
        values = held[b]
        high = values.astype(jnp.bfloat16)
        rest = values - high.astype(jnp.float32)
        middle = rest.astype(jnp.bfloat16)
        low = (rest - middle.astype(jnp.float32)).astype(jnp.bfloat16)
        parts = jnp.concatenate([high, middle, low], axis=1)
        out = jnp.dot(mixer, parts, preferred_element_type=jnp.float32)
        held[b] = out[:, :width] + out[:, width : 2 * width] + out[:, 2 * width :]
    strip = 16
    quarter = BLOCK // 4

    def body(step, carry):
        at = pl.multiple_of(step * strip, strip)
        items = [held[b, pl.ds(at, strip), :] for b in range(blocks)]
        apart = 1
        while apart < blocks:
            items = [
                items[b] + items[b ^ apart] if b & apart == 0 else items[b ^ apart] - items[b]
                for b in range(blocks)
            ]
            apart *= 2
        for b in range(blocks):
            held[b, pl.ds(at, strip), :] = items[b] * scale
        return carry

    copies = []
    for part in range(4):
        first = part * quarter // strip
        lax.fori_loop(first, first + quarter // strip, body, 0)
        span = pl.ds(part * quarter, quarter)
        copies.append(
            pltpu.make_async_copy(held.at[:, span, :], out_ref.at[:, span, :], sent.at[part])
        )
        copies[-1].start()
    for copy in copies:
        copy.wait()


def local_transform(panel, flips, scale):
    rows, width = panel.shape
    shape = (rows // BLOCK, BLOCK, width)
    return pl.pallas_call(
        functools.partial(local_kernel, scale),
        out_shape=jax.ShapeDtypeStruct(shape, jnp.float32),
        in_specs=[pl.BlockSpec(memory_space=pl.ANY)] * 2,
        out_specs=pl.BlockSpec(memory_space=pl.ANY),
        scratch_shapes=[
            pltpu.VMEM((rows // 128, 128), jnp.int32),
            pltpu.VMEM(shape, jnp.float32),
            pltpu.SemaphoreType.DMA((5,)),
            pltpu.SemaphoreType.DMA((4,)),
        ],
        compiler_params=pltpu.CompilerParams(vmem_limit_bytes=61 * 2**20),
    )(flips.reshape(rows // 128, 128), panel.reshape(shape))


def device_kernel(in_ref, out_ref, held, sent):
    devices, rows, _ = in_ref.shape
    strip = 8
    quarter = rows // 4

    def body(step, carry):
        at = pl.multiple_of(step * strip, strip)
        items = [in_ref[d, pl.ds(at, strip), :] for d in range(devices)]
        apart = 1
        while apart < devices:
            items = [
                items[d] + items[d ^ apart] if d & apart == 0 else items[d ^ apart] - items[d]
                for d in range(devices)
            ]
            apart *= 2
        for d in range(devices):
            held[d, pl.ds(at, strip), :] = items[d]
        return carry

    copies = []
    for part in range(4):
        first = part * quarter // strip
        lax.fori_loop(first, first + quarter // strip, body, 0)
        span = pl.ds(part * quarter, quarter)
        copies.append(
            pltpu.make_async_copy(held.at[:, span, :], out_ref.at[:, span, :], sent.at[part])
        )
        copies[-1].start()
    for copy in copies:
        copy.wait()


def device_sums(value):
    return pl.pallas_call(
        device_kernel,
        out_shape=jax.ShapeDtypeStruct(value.shape, jnp.float32),
        in_specs=[pl.BlockSpec(memory_space=pltpu.VMEM)],
        out_specs=pl.BlockSpec(memory_space=pl.ANY),
        scratch_shapes=[
            pltpu.VMEM(value.shape, jnp.float32),
            pltpu.SemaphoreType.DMA((4,)),
        ],
        compiler_params=pltpu.CompilerParams(vmem_limit_bytes=32 * 2**20),
    )(value)


def store_kernel(value_ref, out_ref, sent):
    copy = pltpu.make_async_copy(value_ref, out_ref, sent)
    copy.start()
    copy.wait()


def store(value):
    return pl.pallas_call(
        store_kernel,
        out_shape=jax.ShapeDtypeStruct(value.shape, jnp.float32),
        in_specs=[pl.BlockSpec(memory_space=pltpu.VMEM)],
        out_specs=pl.BlockSpec(memory_space=pl.ANY),
        scratch_shapes=[pltpu.SemaphoreType.DMA],
        compiler_params=pltpu.CompilerParams(vmem_limit_bytes=8 * 2**20),
    )(value)


def index_kernel(rows_here, most, bases_ref, picks_ref, out_ref):
    picks = picks_ref[...]
    devices, per = picks.shape
    before = lax.broadcasted_iota(jnp.int32, (per, per), 0)
    earlier = before < lax.broadcasted_iota(jnp.int32, (per, per), 1)
    earlier = jnp.where(earlier, 1.0, 0.0).astype(jnp.bfloat16)
    for which in range(out_ref.shape[0]):
        offsets = picks - bases_ref[which]
        owned = (offsets >= 0) & (offsets < rows_here)
        ones = jnp.where(owned, 1.0, 0.0).astype(jnp.bfloat16)
        rank = jnp.dot(ones, earlier, preferred_element_type=jnp.float32)
        rank = jnp.where(owned, rank, -1.0)
        marked = (offsets + 1).astype(jnp.float32)
        for slot in range(most):
            hit = jnp.where(rank == float(slot), marked, 0.0)
            row = jnp.sum(hit, axis=1, keepdims=True).astype(jnp.int32) - 1
            out_ref[which, :, slot : slot + 1] = row


def send_rows(picks, owners, rows_here, devices, most):
    bases = jnp.stack(owners) * rows_here
    rows = pl.pallas_call(
        functools.partial(index_kernel, rows_here, most),
        out_shape=jax.ShapeDtypeStruct((len(owners), devices, most), jnp.int32),
        in_specs=[
            pl.BlockSpec(memory_space=pltpu.SMEM),
            pl.BlockSpec(memory_space=pltpu.VMEM),
        ],
        out_specs=pl.BlockSpec(memory_space=pltpu.VMEM),
        compiler_params=pltpu.CompilerParams(vmem_limit_bytes=8 * 2**20),
    )(bases.astype(jnp.int32), picks.reshape(devices, -1))
    return rows.reshape(len(owners) * devices * most)


def count_kernel(rows_here, wide, me_ref, picks_ref, out_ref):
    picks = picks_ref[...]
    rows, devices = out_ref.shape
    owner = picks >> rows_here.bit_length() - 1
    owner = (owner & wide - 1) * (devices // wide) + (owner >> wide.bit_length() - 1)
    local = picks & rows_here - 1
    held = local >> rows.bit_length() - 1 == me_ref[0]
    place = jnp.where(held, local & rows - 1, -1)
    shape = (devices, picks.shape[1])
    owners = jnp.where(lax.broadcasted_iota(jnp.int32, shape, 0) == owner, 1.0, 0.0)
    shape = (rows, picks.shape[1])
    places = jnp.where(lax.broadcasted_iota(jnp.int32, shape, 0) == place, 1.0, 0.0)
    out_ref[...] = lax.dot_general(
        places.astype(jnp.bfloat16),
        owners.astype(jnp.bfloat16),
        (((1,), (1,)), ((), ())),
        preferred_element_type=jnp.float32,
    )


def count_picks(picks, me, rows_here, devices):
    return pl.pallas_call(
        functools.partial(count_kernel, rows_here, lax.axis_size("wide")),
        out_shape=jax.ShapeDtypeStruct((rows_here // devices, devices), jnp.float32),
        in_specs=[
            pl.BlockSpec(memory_space=pltpu.SMEM),
            pl.BlockSpec(memory_space=pltpu.VMEM),
        ],
        out_specs=pl.BlockSpec(memory_space=pltpu.VMEM),
        compiler_params=pltpu.CompilerParams(vmem_limit_bytes=32 * 2**20),
    )(me.reshape(1).astype(jnp.int32), picks.reshape(1, -1))


def halves(value):
    high = value.astype(jnp.bfloat16)
    return high, (value - high.astype(jnp.float32)).astype(jnp.bfloat16)


def part_kernel(counts_ref, held_ref, out_ref):
    devices, _, width = held_ref.shape
    total = jnp.zeros((width, 2 * width), jnp.float32)
    rest = jnp.zeros((width, width), jnp.float32)
    for d in range(devices):
        rows = held_ref[d]
        high, low = halves(rows)
        weighted, spare = halves(rows * counts_ref[:, d : d + 1])
        over_rows = (((0,), (0,)), ((), ()))
        both = jnp.concatenate([weighted, spare], axis=1)
        total += lax.dot_general(high, both, over_rows, preferred_element_type=jnp.float32)
        rest += lax.dot_general(low, weighted, over_rows, preferred_element_type=jnp.float32)
    out_ref[...] = total[:, :width] + total[:, width:] + rest


def gram_part(counts, held):
    width = held.shape[2]
    return pl.pallas_call(
        part_kernel,
        out_shape=jax.ShapeDtypeStruct((width, width), jnp.float32),
        in_specs=[pl.BlockSpec(memory_space=pltpu.VMEM)] * 2,
        out_specs=pl.BlockSpec(memory_space=pltpu.VMEM),
        compiler_params=pltpu.CompilerParams(vmem_limit_bytes=32 * 2**20),
    )(counts, held)


def swap(value, axis, apart):
    pairs = [(source, source ^ apart) for source in range(lax.axis_size(axis))]
    return lax.ppermute(value, axis, pairs)


def scatter_sum(value, axis):
    upper = lax.axis_index(axis) & 1
    half = value.shape[0] // 2
    keep = lax.dynamic_slice_in_dim(value, upper * half, half)
    give = lax.dynamic_slice_in_dim(value, (1 - upper) * half, half)
    return keep + swap(give, axis, 1)


def join(lower, upper, axis):
    turned = lax.axis_index(axis) & 1 == 1
    first = jnp.where(turned, upper, lower)
    return jnp.concatenate([first, jnp.where(turned, lower, upper)], axis=0)


def gather_quarters(value):
    over_core, over_y = swap(value, "narrow", 1), swap(value, "wide", 1)
    over_both = swap(value, AXES, lax.axis_size("wide") + 1)
    mine = join(value, over_y, "wide")
    return join(mine, join(over_core, over_both, "wide"), "narrow")


def landing(block, rows_here, most):
    owners = block // rows_here
    order = jnp.arange(block.shape[0], dtype=jnp.int32)
    earlier = (owners[:, None] == owners[None, :]) & (order[None, :] < order[:, None])
    return owners * most + jnp.sum(earlier.astype(jnp.int32), axis=1)


def on_device(panel, flips, picks):
    rows_here, width = panel.shape
    devices = lax.axis_size("narrow") * lax.axis_size("wide")
    scale = 1.0 / float(rows_here * devices) ** 0.5
    me = lax.axis_index(AXES)
    per = picks.shape[0] // devices
    most = -(-per // devices)

    local = local_transform(panel, flips, scale)
    local = local.reshape(devices, rows_here // devices, width)
    wanted = send_rows(picks, [me], rows_here, devices, most)
    spots = landing(lax.dynamic_slice(picks, (me * per,), (per,)), rows_here, most)
    counts = count_picks(picks, lax.axis_index(TURNED), rows_here, devices)
    slices = lax.all_to_all(local, TURNED, 0, 0, tiled=True)
    slices, wanted, spots, counts = lax.optimization_barrier((slices, wanted, spots, counts))
    slices = device_sums(slices)
    mixed = lax.all_to_all(slices, TURNED, 0, 0, tiled=True)
    gram = gram_part(counts, slices)
    gram = scatter_sum(scatter_sum(gram, "narrow"), "wide")
    far = lax.axis_size("wide") // 4
    for axis, low, high in (("narrow", 2, lax.axis_size("narrow")), ("wide", 2, far)):
        while low < high:
            gram = gram + swap(gram, axis, low)
            low *= 2
    near, one, two = [swap(gram, "wide", apart * far) for apart in (1, 2, 3)]
    gram = (gram + near) + (one + two)
    mixed, gram = lax.optimization_barrier((mixed, gram))
    mixed = mixed.reshape(rows_here, width)
    chosen = jnp.take(mixed, wanted, axis=0, mode="clip")
    landed = lax.all_to_all(chosen.reshape(devices, most, width), AXES, 0, 0, tiled=True)
    gram = gather_quarters(gram) / float(picks.shape[0])
    mixed = store(mixed)
    landed, mixed, gram = lax.optimization_barrier((landed, mixed, gram))
    sketch = jnp.take(landed.reshape(devices * most, width), spots, axis=0, mode="clip")
    return (mixed, sketch, gram)


def solution(mesh):
    in_specs = (P(AXES, None), P(AXES), P())
    out_specs = (P(AXES, None), P(AXES, None), P())
    return jax.shard_map(
        on_device, mesh=mesh, in_specs=in_specs, out_specs=out_specs, check_vma=False
    )
```

```python
import functools

import jax
import jax.numpy as jnp
from jax import lax
from jax.experimental import pallas as pl
from jax.experimental.pallas import tpu as pltpu
from jax.sharding import PartitionSpec as P

BLOCK = 256
AXES = ("narrow", "wide")
TURNED = ("wide", "narrow")


def signs(order):
    rows = lax.broadcasted_iota(jnp.int32, (order, order), 0)
    both = rows & lax.broadcasted_iota(jnp.int32, (order, order), 1)
    parity = jnp.zeros((order, order), jnp.int32)
    for level in range(order.bit_length() - 1):
        parity = parity ^ (both >> level & 1)
    return (1 - 2 * parity).astype(jnp.float32)


def local_kernel(scale, flips_ref, panel_ref, out_ref, flags, held, arrived, sent):
    blocks, _, width = panel_ref.shape
    per = BLOCK // flips_ref.shape[1]
    share = blocks // 4
    loads = [pltpu.make_async_copy(flips_ref, flags, arrived.at[4])]
    for part in range(4):
        span = pl.ds(part * share, share)
        loads.append(pltpu.make_async_copy(panel_ref.at[span], held.at[span], arrived.at[part]))
    for load in loads:
        load.start()
    base = signs(BLOCK)
    loads[0].wait()
    for b in range(blocks):
        if b % share == 0:
            loads[1 + b // share].wait()
        row = jnp.concatenate([flags[b * per + i : b * per + i + 1, :] for i in range(per)], axis=1)
        mixer = (base * (1 - 2 * row).astype(jnp.float32)).astype(jnp.bfloat16)
        values = held[b]
        high = values.astype(jnp.bfloat16)
        rest = values - high.astype(jnp.float32)
        middle = rest.astype(jnp.bfloat16)
        low = (rest - middle.astype(jnp.float32)).astype(jnp.bfloat16)
        parts = jnp.concatenate([high, middle, low], axis=1)
        out = jnp.dot(mixer, parts, preferred_element_type=jnp.float32)
        held[b] = out[:, :width] + out[:, width : 2 * width] + out[:, 2 * width :]
    strip = 16
    quarter = BLOCK // 4

    def body(step, carry):
        at = pl.multiple_of(step * strip, strip)
        items = [held[b, pl.ds(at, strip), :] for b in range(blocks)]
        apart = 1
        while apart < blocks:
            items = [
                items[b] + items[b ^ apart] if b & apart == 0 else items[b ^ apart] - items[b]
                for b in range(blocks)
            ]
            apart *= 2
        for b in range(blocks):
            held[b, pl.ds(at, strip), :] = items[b] * scale
        return carry

    copies = []
    for part in range(4):
        first = part * quarter // strip
        lax.fori_loop(first, first + quarter // strip, body, 0)
        span = pl.ds(part * quarter, quarter)
        copies.append(
            pltpu.make_async_copy(held.at[:, span, :], out_ref.at[:, span, :], sent.at[part])
        )
        copies[-1].start()
    for copy in copies:
        copy.wait()


def local_transform(panel, flips, scale):
    rows, width = panel.shape
    shape = (rows // BLOCK, BLOCK, width)
    return pl.pallas_call(
        functools.partial(local_kernel, scale),
        out_shape=jax.ShapeDtypeStruct(shape, jnp.float32),
        in_specs=[pl.BlockSpec(memory_space=pl.ANY)] * 2,
        out_specs=pl.BlockSpec(memory_space=pl.ANY),
        scratch_shapes=[
            pltpu.VMEM((rows // 128, 128), jnp.int32),
            pltpu.VMEM(shape, jnp.float32),
            pltpu.SemaphoreType.DMA((5,)),
            pltpu.SemaphoreType.DMA((4,)),
        ],
        compiler_params=pltpu.CompilerParams(vmem_limit_bytes=61 * 2**20),
    )(flips.reshape(rows // 128, 128), panel.reshape(shape))


def device_kernel(in_ref, out_ref, held, sent):
    devices, rows, _ = in_ref.shape
    strip = 8
    quarter = rows // 4

    def body(step, carry):
        at = pl.multiple_of(step * strip, strip)
        items = [in_ref[d, pl.ds(at, strip), :] for d in range(devices)]
        apart = 1
        while apart < devices:
            items = [
                items[d] + items[d ^ apart] if d & apart == 0 else items[d ^ apart] - items[d]
                for d in range(devices)
            ]
            apart *= 2
        for d in range(devices):
            held[d, pl.ds(at, strip), :] = items[d]
        return carry

    copies = []
    for part in range(4):
        first = part * quarter // strip
        lax.fori_loop(first, first + quarter // strip, body, 0)
        span = pl.ds(part * quarter, quarter)
        copies.append(
            pltpu.make_async_copy(held.at[:, span, :], out_ref.at[:, span, :], sent.at[part])
        )
        copies[-1].start()
    for copy in copies:
        copy.wait()


def device_sums(value):
    return pl.pallas_call(
        device_kernel,
        out_shape=jax.ShapeDtypeStruct(value.shape, jnp.float32),
        in_specs=[pl.BlockSpec(memory_space=pltpu.VMEM)],
        out_specs=pl.BlockSpec(memory_space=pl.ANY),
        scratch_shapes=[
            pltpu.VMEM(value.shape, jnp.float32),
            pltpu.SemaphoreType.DMA((4,)),
        ],
        compiler_params=pltpu.CompilerParams(vmem_limit_bytes=32 * 2**20),
    )(value)


def store_kernel(value_ref, out_ref, sent):
    copy = pltpu.make_async_copy(value_ref, out_ref, sent)
    copy.start()
    copy.wait()


def store(value):
    return pl.pallas_call(
        store_kernel,
        out_shape=jax.ShapeDtypeStruct(value.shape, jnp.float32),
        in_specs=[pl.BlockSpec(memory_space=pltpu.VMEM)],
        out_specs=pl.BlockSpec(memory_space=pl.ANY),
        scratch_shapes=[pltpu.SemaphoreType.DMA],
        compiler_params=pltpu.CompilerParams(vmem_limit_bytes=8 * 2**20),
    )(value)


def index_kernel(rows_here, most, bases_ref, picks_ref, out_ref):
    picks = picks_ref[...]
    devices, per = picks.shape
    before = lax.broadcasted_iota(jnp.int32, (per, per), 0)
    earlier = before < lax.broadcasted_iota(jnp.int32, (per, per), 1)
    earlier = jnp.where(earlier, 1.0, 0.0).astype(jnp.bfloat16)
    for which in range(out_ref.shape[0]):
        offsets = picks - bases_ref[which]
        owned = (offsets >= 0) & (offsets < rows_here)
        ones = jnp.where(owned, 1.0, 0.0).astype(jnp.bfloat16)
        rank = jnp.dot(ones, earlier, preferred_element_type=jnp.float32)
        rank = jnp.where(owned, rank, -1.0)
        marked = (offsets + 1).astype(jnp.float32)
        for slot in range(most):
            hit = jnp.where(rank == float(slot), marked, 0.0)
            row = jnp.sum(hit, axis=1, keepdims=True).astype(jnp.int32) - 1
            out_ref[which, :, slot : slot + 1] = row


def send_rows(picks, owners, rows_here, devices, most):
    bases = jnp.stack(owners) * rows_here
    rows = pl.pallas_call(
        functools.partial(index_kernel, rows_here, most),
        out_shape=jax.ShapeDtypeStruct((len(owners), devices, most), jnp.int32),
        in_specs=[
            pl.BlockSpec(memory_space=pltpu.SMEM),
            pl.BlockSpec(memory_space=pltpu.VMEM),
        ],
        out_specs=pl.BlockSpec(memory_space=pltpu.VMEM),
        compiler_params=pltpu.CompilerParams(vmem_limit_bytes=8 * 2**20),
    )(bases.astype(jnp.int32), picks.reshape(devices, -1))
    return rows.reshape(len(owners) * devices * most)


def count_kernel(rows_here, wide, me_ref, picks_ref, out_ref):
    picks = picks_ref[...]
    rows, devices = out_ref.shape
    owner = picks >> rows_here.bit_length() - 1
    owner = (owner & wide - 1) * (devices // wide) + (owner >> wide.bit_length() - 1)
    local = picks & rows_here - 1
    held = local >> rows.bit_length() - 1 == me_ref[0]
    place = jnp.where(held, local & rows - 1, -1)
    shape = (devices, picks.shape[1])
    owners = jnp.where(lax.broadcasted_iota(jnp.int32, shape, 0) == owner, 1.0, 0.0)
    shape = (rows, picks.shape[1])
    places = jnp.where(lax.broadcasted_iota(jnp.int32, shape, 0) == place, 1.0, 0.0)
    out_ref[...] = lax.dot_general(
        places.astype(jnp.bfloat16),
        owners.astype(jnp.bfloat16),
        (((1,), (1,)), ((), ())),
        preferred_element_type=jnp.float32,
    )


def count_picks(picks, me, rows_here, devices):
    return pl.pallas_call(
        functools.partial(count_kernel, rows_here, lax.axis_size("wide")),
        out_shape=jax.ShapeDtypeStruct((rows_here // devices, devices), jnp.float32),
        in_specs=[
            pl.BlockSpec(memory_space=pltpu.SMEM),
            pl.BlockSpec(memory_space=pltpu.VMEM),
        ],
        out_specs=pl.BlockSpec(memory_space=pltpu.VMEM),
        compiler_params=pltpu.CompilerParams(vmem_limit_bytes=32 * 2**20),
    )(me.reshape(1).astype(jnp.int32), picks.reshape(1, -1))


def halves(value):
    high = value.astype(jnp.bfloat16)
    return high, (value - high.astype(jnp.float32)).astype(jnp.bfloat16)


def part_kernel(counts_ref, held_ref, out_ref):
    devices, _, width = held_ref.shape
    total = jnp.zeros((width, 2 * width), jnp.float32)
    rest = jnp.zeros((width, width), jnp.float32)
    for d in range(devices):
        rows = held_ref[d]
        high, low = halves(rows)
        weighted, spare = halves(rows * counts_ref[:, d : d + 1])
        over_rows = (((0,), (0,)), ((), ()))
        both = jnp.concatenate([weighted, spare], axis=1)
        total += lax.dot_general(high, both, over_rows, preferred_element_type=jnp.float32)
        rest += lax.dot_general(low, weighted, over_rows, preferred_element_type=jnp.float32)
    out_ref[...] = total[:, :width] + total[:, width:] + rest


def gram_part(counts, held):
    width = held.shape[2]
    return pl.pallas_call(
        part_kernel,
        out_shape=jax.ShapeDtypeStruct((width, width), jnp.float32),
        in_specs=[pl.BlockSpec(memory_space=pltpu.VMEM)] * 2,
        out_specs=pl.BlockSpec(memory_space=pltpu.VMEM),
        compiler_params=pltpu.CompilerParams(vmem_limit_bytes=32 * 2**20),
    )(counts, held)


def swap(value, axis, apart):
    pairs = [(source, source ^ apart) for source in range(lax.axis_size(axis))]
    return lax.ppermute(value, axis, pairs)


def scatter_sum(value, axis):
    upper = lax.axis_index(axis) & 1
    half = value.shape[0] // 2
    keep = lax.dynamic_slice_in_dim(value, upper * half, half)
    give = lax.dynamic_slice_in_dim(value, (1 - upper) * half, half)
    return keep + swap(give, axis, 1)


def gather_quarters(value):
    rows, width = value.shape
    place = 2 * (lax.axis_index("narrow") & 1) + (lax.axis_index("wide") & 1)
    blank = jnp.zeros((4 * rows, width), jnp.float32)
    value = lax.dynamic_update_slice_in_dim(blank, value, place * rows, 0)
    others = swap(value, "narrow", 1) + swap(value, AXES, lax.axis_size("wide") + 1)
    return value + swap(value, "wide", 1) + others


def landing(block, rows_here, most):
    owners = block // rows_here
    order = jnp.arange(block.shape[0], dtype=jnp.int32)
    earlier = (owners[:, None] == owners[None, :]) & (order[None, :] < order[:, None])
    return owners * most + jnp.sum(earlier.astype(jnp.int32), axis=1)


def on_device(panel, flips, picks):
    rows_here, width = panel.shape
    devices = lax.axis_size("narrow") * lax.axis_size("wide")
    scale = 1.0 / float(rows_here * devices) ** 0.5
    me = lax.axis_index(AXES)
    per = picks.shape[0] // devices
    most = -(-per // devices)

    local = local_transform(panel, flips, scale)
    local = local.reshape(devices, rows_here // devices, width)
    wanted = send_rows(picks, [me], rows_here, devices, most)
    spots = landing(lax.dynamic_slice(picks, (me * per,), (per,)), rows_here, most)
    counts = count_picks(picks, lax.axis_index(TURNED), rows_here, devices)
    slices = lax.all_to_all(local, TURNED, 0, 0, tiled=True)
    slices, wanted, spots, counts = lax.optimization_barrier((slices, wanted, spots, counts))
    slices = device_sums(slices)
    mixed = lax.all_to_all(slices, TURNED, 0, 0, tiled=True)
    gram = gram_part(counts, slices)
    gram = scatter_sum(scatter_sum(gram, "narrow"), "wide")
    far = lax.axis_size("wide") // 4
    for axis, low, high in (("narrow", 2, lax.axis_size("narrow")), ("wide", 2, far)):
        while low < high:
            gram = gram + swap(gram, axis, low)
            low *= 2
    near, one, two = [swap(gram, "wide", apart * far) for apart in (1, 2, 3)]
    gram = (gram + near) + (one + two)
    mixed, gram = lax.optimization_barrier((mixed, gram))
    mixed = mixed.reshape(rows_here, width)
    chosen = jnp.take(mixed, wanted, axis=0, mode="clip")
    landed = lax.all_to_all(chosen.reshape(devices, most, width), AXES, 0, 0, tiled=True)
    gram = gather_quarters(gram) / float(picks.shape[0])
    mixed = store(mixed)
    landed, mixed, gram = lax.optimization_barrier((landed, mixed, gram))
    sketch = jnp.take(landed.reshape(devices * most, width), spots, axis=0, mode="clip")
    return (mixed, sketch, gram)


def solution(mesh):
    in_specs = (P(AXES, None), P(AXES), P())
    out_specs = (P(AXES, None), P(AXES, None), P())
    return jax.shard_map(
        on_device, mesh=mesh, in_specs=in_specs, out_specs=out_specs, check_vma=False
    )
```

```python
import functools

import jax
import jax.numpy as jnp
from jax import lax
from jax.experimental import pallas as pl
from jax.experimental.pallas import tpu as pltpu
from jax.sharding import PartitionSpec as P

BLOCK = 256
AXES = ("narrow", "wide")
TURNED = ("wide", "narrow")


def signs(order):
    rows = lax.broadcasted_iota(jnp.int32, (order, order), 0)
    both = rows & lax.broadcasted_iota(jnp.int32, (order, order), 1)
    parity = jnp.zeros((order, order), jnp.int32)
    for level in range(order.bit_length() - 1):
        parity = parity ^ (both >> level & 1)
    return (1 - 2 * parity).astype(jnp.float32)


def local_kernel(scale, flips_ref, panel_ref, out_ref, flags, held, arrived, sent):
    blocks, _, width = panel_ref.shape
    per = BLOCK // flips_ref.shape[1]
    share = blocks // 4
    loads = [pltpu.make_async_copy(flips_ref, flags, arrived.at[4])]
    for part in range(4):
        span = pl.ds(part * share, share)
        loads.append(pltpu.make_async_copy(panel_ref.at[span], held.at[span], arrived.at[part]))
    for load in loads:
        load.start()
    base = signs(BLOCK)
    loads[0].wait()
    for b in range(blocks):
        if b % share == 0:
            loads[1 + b // share].wait()
        row = jnp.concatenate([flags[b * per + i : b * per + i + 1, :] for i in range(per)], axis=1)
        mixer = (base * (1 - 2 * row).astype(jnp.float32)).astype(jnp.bfloat16)
        values = held[b]
        high = values.astype(jnp.bfloat16)
        rest = values - high.astype(jnp.float32)
        middle = rest.astype(jnp.bfloat16)
        low = (rest - middle.astype(jnp.float32)).astype(jnp.bfloat16)
        parts = jnp.concatenate([high, middle, low], axis=1)
        out = jnp.dot(mixer, parts, preferred_element_type=jnp.float32)
        held[b] = out[:, :width] + out[:, width : 2 * width] + out[:, 2 * width :]
    strip = 16
    quarter = BLOCK // 4

    def body(step, carry):
        at = pl.multiple_of(step * strip, strip)
        items = [held[b, pl.ds(at, strip), :] for b in range(blocks)]
        apart = 1
        while apart < blocks:
            items = [
                items[b] + items[b ^ apart] if b & apart == 0 else items[b ^ apart] - items[b]
                for b in range(blocks)
            ]
            apart *= 2
        for b in range(blocks):
            held[b, pl.ds(at, strip), :] = items[b] * scale
        return carry

    copies = []
    for part in range(4):
        first = part * quarter // strip
        lax.fori_loop(first, first + quarter // strip, body, 0)
        span = pl.ds(part * quarter, quarter)
        copies.append(
            pltpu.make_async_copy(held.at[:, span, :], out_ref.at[:, span, :], sent.at[part])
        )
        copies[-1].start()
    for copy in copies:
        copy.wait()


def local_transform(panel, flips, scale):
    rows, width = panel.shape
    shape = (rows // BLOCK, BLOCK, width)
    return pl.pallas_call(
        functools.partial(local_kernel, scale),
        out_shape=jax.ShapeDtypeStruct(shape, jnp.float32),
        in_specs=[pl.BlockSpec(memory_space=pl.ANY)] * 2,
        out_specs=pl.BlockSpec(memory_space=pl.ANY),
        scratch_shapes=[
            pltpu.VMEM((rows // 128, 128), jnp.int32),
            pltpu.VMEM(shape, jnp.float32),
            pltpu.SemaphoreType.DMA((5,)),
            pltpu.SemaphoreType.DMA((4,)),
        ],
        compiler_params=pltpu.CompilerParams(vmem_limit_bytes=61 * 2**20),
    )(flips.reshape(rows // 128, 128), panel.reshape(shape))


def device_kernel(in_ref, out_ref, held, sent):
    devices, rows, _ = in_ref.shape
    strip = 8
    quarter = rows // 4

    def body(step, carry):
        at = pl.multiple_of(step * strip, strip)
        items = [in_ref[d, pl.ds(at, strip), :] for d in range(devices)]
        apart = 1
        while apart < devices:
            items = [
                items[d] + items[d ^ apart] if d & apart == 0 else items[d ^ apart] - items[d]
                for d in range(devices)
            ]
            apart *= 2
        for d in range(devices):
            held[d, pl.ds(at, strip), :] = items[d]
        return carry

    copies = []
    for part in range(4):
        first = part * quarter // strip
        lax.fori_loop(first, first + quarter // strip, body, 0)
        span = pl.ds(part * quarter, quarter)
        copies.append(
            pltpu.make_async_copy(held.at[:, span, :], out_ref.at[:, span, :], sent.at[part])
        )
        copies[-1].start()
    for copy in copies:
        copy.wait()


def device_sums(value):
    return pl.pallas_call(
        device_kernel,
        out_shape=jax.ShapeDtypeStruct(value.shape, jnp.float32),
        in_specs=[pl.BlockSpec(memory_space=pltpu.VMEM)],
        out_specs=pl.BlockSpec(memory_space=pl.ANY),
        scratch_shapes=[
            pltpu.VMEM(value.shape, jnp.float32),
            pltpu.SemaphoreType.DMA((4,)),
        ],
        compiler_params=pltpu.CompilerParams(vmem_limit_bytes=32 * 2**20),
    )(value)


def store_kernel(value_ref, out_ref, sent):
    copy = pltpu.make_async_copy(value_ref, out_ref, sent)
    copy.start()
    copy.wait()


def store(value):
    return pl.pallas_call(
        store_kernel,
        out_shape=jax.ShapeDtypeStruct(value.shape, jnp.float32),
        in_specs=[pl.BlockSpec(memory_space=pltpu.VMEM)],
        out_specs=pl.BlockSpec(memory_space=pl.ANY),
        scratch_shapes=[pltpu.SemaphoreType.DMA],
        compiler_params=pltpu.CompilerParams(vmem_limit_bytes=8 * 2**20),
    )(value)


def index_kernel(rows_here, most, bases_ref, picks_ref, out_ref):
    picks = picks_ref[...]
    devices, per = picks.shape
    before = lax.broadcasted_iota(jnp.int32, (per, per), 0)
    earlier = before < lax.broadcasted_iota(jnp.int32, (per, per), 1)
    earlier = jnp.where(earlier, 1.0, 0.0).astype(jnp.bfloat16)
    for which in range(out_ref.shape[0]):
        offsets = picks - bases_ref[which]
        owned = (offsets >= 0) & (offsets < rows_here)
        ones = jnp.where(owned, 1.0, 0.0).astype(jnp.bfloat16)
        rank = jnp.dot(ones, earlier, preferred_element_type=jnp.float32)
        rank = jnp.where(owned, rank, -1.0)
        marked = (offsets + 1).astype(jnp.float32)
        for slot in range(most):
            hit = jnp.where(rank == float(slot), marked, 0.0)
            row = jnp.sum(hit, axis=1, keepdims=True).astype(jnp.int32) - 1
            out_ref[which, :, slot : slot + 1] = row


def send_rows(picks, owners, rows_here, devices, most):
    bases = jnp.stack(owners) * rows_here
    rows = pl.pallas_call(
        functools.partial(index_kernel, rows_here, most),
        out_shape=jax.ShapeDtypeStruct((len(owners), devices, most), jnp.int32),
        in_specs=[
            pl.BlockSpec(memory_space=pltpu.SMEM),
            pl.BlockSpec(memory_space=pltpu.VMEM),
        ],
        out_specs=pl.BlockSpec(memory_space=pltpu.VMEM),
        compiler_params=pltpu.CompilerParams(vmem_limit_bytes=8 * 2**20),
    )(bases.astype(jnp.int32), picks.reshape(devices, -1))
    return rows.reshape(len(owners) * devices * most)


def count_kernel(rows_here, wide, me_ref, picks_ref, out_ref):
    picks = picks_ref[...]
    rows, devices = out_ref.shape
    owner = picks >> rows_here.bit_length() - 1
    owner = (owner & wide - 1) * (devices // wide) + (owner >> wide.bit_length() - 1)
    local = picks & rows_here - 1
    held = local >> rows.bit_length() - 1 == me_ref[0]
    place = jnp.where(held, local & rows - 1, -1)
    shape = (devices, picks.shape[1])
    owners = jnp.where(lax.broadcasted_iota(jnp.int32, shape, 0) == owner, 1.0, 0.0)
    shape = (rows, picks.shape[1])
    places = jnp.where(lax.broadcasted_iota(jnp.int32, shape, 0) == place, 1.0, 0.0)
    out_ref[...] = lax.dot_general(
        places.astype(jnp.bfloat16),
        owners.astype(jnp.bfloat16),
        (((1,), (1,)), ((), ())),
        preferred_element_type=jnp.float32,
    )


def count_picks(picks, me, rows_here, devices):
    return pl.pallas_call(
        functools.partial(count_kernel, rows_here, lax.axis_size("wide")),
        out_shape=jax.ShapeDtypeStruct((rows_here // devices, devices), jnp.float32),
        in_specs=[
            pl.BlockSpec(memory_space=pltpu.SMEM),
            pl.BlockSpec(memory_space=pltpu.VMEM),
        ],
        out_specs=pl.BlockSpec(memory_space=pltpu.VMEM),
        compiler_params=pltpu.CompilerParams(vmem_limit_bytes=32 * 2**20),
    )(me.reshape(1).astype(jnp.int32), picks.reshape(1, -1))


def halves(value):
    high = value.astype(jnp.bfloat16)
    return high, (value - high.astype(jnp.float32)).astype(jnp.bfloat16)


def part_kernel(counts_ref, held_ref, out_ref):
    devices, _, width = held_ref.shape
    total = jnp.zeros((width, 2 * width), jnp.float32)
    rest = jnp.zeros((width, width), jnp.float32)
    for d in range(devices):
        rows = held_ref[d]
        high, low = halves(rows)
        weighted, spare = halves(rows * counts_ref[:, d : d + 1])
        over_rows = (((0,), (0,)), ((), ()))
        both = jnp.concatenate([weighted, spare], axis=1)
        total += lax.dot_general(high, both, over_rows, preferred_element_type=jnp.float32)
        rest += lax.dot_general(low, weighted, over_rows, preferred_element_type=jnp.float32)
    out_ref[...] = total[:, :width] + total[:, width:] + rest


def gram_part(counts, held):
    width = held.shape[2]
    return pl.pallas_call(
        part_kernel,
        out_shape=jax.ShapeDtypeStruct((width, width), jnp.float32),
        in_specs=[pl.BlockSpec(memory_space=pltpu.VMEM)] * 2,
        out_specs=pl.BlockSpec(memory_space=pltpu.VMEM),
        compiler_params=pltpu.CompilerParams(vmem_limit_bytes=32 * 2**20),
    )(counts, held)


def swap(value, axis, apart):
    pairs = [(source, source ^ apart) for source in range(lax.axis_size(axis))]
    return lax.ppermute(value, axis, pairs)


def scatter_sum(value, axis):
    upper = lax.axis_index(axis) & 1
    half = value.shape[0] // 2
    keep = lax.dynamic_slice_in_dim(value, upper * half, half)
    give = lax.dynamic_slice_in_dim(value, (1 - upper) * half, half)
    return keep + swap(give, axis, 1)


def gather_halves(value, axis):
    rows, width = value.shape
    blank = jnp.zeros((2 * rows, width), jnp.float32)
    at = (lax.axis_index(axis) & 1) * rows
    value = lax.dynamic_update_slice_in_dim(blank, value, at, 0)
    return value + swap(value, axis, 1)


def landing(block, rows_here, most):
    owners = block // rows_here
    order = jnp.arange(block.shape[0], dtype=jnp.int32)
    earlier = (owners[:, None] == owners[None, :]) & (order[None, :] < order[:, None])
    return owners * most + jnp.sum(earlier.astype(jnp.int32), axis=1)


def on_device(panel, flips, picks):
    rows_here, width = panel.shape
    devices = lax.axis_size("narrow") * lax.axis_size("wide")
    scale = 1.0 / float(rows_here * devices) ** 0.5
    me = lax.axis_index(AXES)
    per = picks.shape[0] // devices
    most = -(-per // devices)

    local = local_transform(panel, flips, scale)
    local = local.reshape(devices, rows_here // devices, width)
    wanted = send_rows(picks, [me], rows_here, devices, most)
    spots = landing(lax.dynamic_slice(picks, (me * per,), (per,)), rows_here, most)
    counts = count_picks(picks, lax.axis_index(TURNED), rows_here, devices)
    slices = lax.all_to_all(local, TURNED, 0, 0, tiled=True)
    slices, wanted, spots, counts = lax.optimization_barrier((slices, wanted, spots, counts))
    slices = device_sums(slices)
    mixed = lax.all_to_all(slices, TURNED, 0, 0, tiled=True)
    gram = gram_part(counts, slices)
    gram = scatter_sum(gram, "narrow")
    for axis, low in (("narrow", 2), ("wide", 1)):
        while low < lax.axis_size(axis):
            gram = gram + swap(gram, axis, low)
            low *= 2
    mixed, gram = lax.optimization_barrier((mixed, gram))
    mixed = mixed.reshape(rows_here, width)
    chosen = jnp.take(mixed, wanted, axis=0, mode="clip")
    landed = lax.all_to_all(chosen.reshape(devices, most, width), AXES, 0, 0, tiled=True)
    gram = gather_halves(gram, "narrow") / float(picks.shape[0])
    mixed = store(mixed)
    landed, mixed, gram = lax.optimization_barrier((landed, mixed, gram))
    sketch = jnp.take(landed.reshape(devices * most, width), spots, axis=0, mode="clip")
    return (mixed, sketch, gram)


def solution(mesh):
    in_specs = (P(AXES, None), P(AXES), P())
    out_specs = (P(AXES, None), P(AXES, None), P())
    return jax.shard_map(
        on_device, mesh=mesh, in_specs=in_specs, out_specs=out_specs, check_vma=False
    )
```

```python
import functools

import jax
import jax.numpy as jnp
from jax import lax
from jax.experimental import pallas as pl
from jax.experimental.pallas import tpu as pltpu
from jax.sharding import PartitionSpec as P

BLOCK = 256
AXES = ("narrow", "wide")
TURNED = ("wide", "narrow")


def signs(order):
    rows = lax.broadcasted_iota(jnp.int32, (order, order), 0)
    both = rows & lax.broadcasted_iota(jnp.int32, (order, order), 1)
    parity = jnp.zeros((order, order), jnp.int32)
    for level in range(order.bit_length() - 1):
        parity = parity ^ (both >> level & 1)
    return (1 - 2 * parity).astype(jnp.float32)


def local_kernel(scale, flips_ref, panel_ref, out_ref, flags, held, arrived, sent):
    blocks, _, width = panel_ref.shape
    per = BLOCK // flips_ref.shape[1]
    share = blocks // 4
    loads = [pltpu.make_async_copy(flips_ref, flags, arrived.at[4])]
    for part in range(4):
        span = pl.ds(part * share, share)
        loads.append(pltpu.make_async_copy(panel_ref.at[span], held.at[span], arrived.at[part]))
    for load in loads:
        load.start()
    base = signs(BLOCK)
    loads[0].wait()
    for b in range(blocks):
        if b % share == 0:
            loads[1 + b // share].wait()
        row = jnp.concatenate([flags[b * per + i : b * per + i + 1, :] for i in range(per)], axis=1)
        mixer = (base * (1 - 2 * row).astype(jnp.float32)).astype(jnp.bfloat16)
        values = held[b]
        high = values.astype(jnp.bfloat16)
        rest = values - high.astype(jnp.float32)
        middle = rest.astype(jnp.bfloat16)
        low = (rest - middle.astype(jnp.float32)).astype(jnp.bfloat16)
        parts = jnp.concatenate([high, middle, low], axis=1)
        out = jnp.dot(mixer, parts, preferred_element_type=jnp.float32)
        held[b] = out[:, :width] + out[:, width : 2 * width] + out[:, 2 * width :]
    strip = 16
    quarter = BLOCK // 4

    def body(step, carry):
        at = pl.multiple_of(step * strip, strip)
        items = [held[b, pl.ds(at, strip), :] for b in range(blocks)]
        apart = 1
        while apart < blocks:
            items = [
                items[b] + items[b ^ apart] if b & apart == 0 else items[b ^ apart] - items[b]
                for b in range(blocks)
            ]
            apart *= 2
        for b in range(blocks):
            held[b, pl.ds(at, strip), :] = items[b] * scale
        return carry

    copies = []
    for part in range(4):
        first = part * quarter // strip
        lax.fori_loop(first, first + quarter // strip, body, 0)
        span = pl.ds(part * quarter, quarter)
        copies.append(
            pltpu.make_async_copy(held.at[:, span, :], out_ref.at[:, span, :], sent.at[part])
        )
        copies[-1].start()
    for copy in copies:
        copy.wait()


def local_transform(panel, flips, scale):
    rows, width = panel.shape
    shape = (rows // BLOCK, BLOCK, width)
    return pl.pallas_call(
        functools.partial(local_kernel, scale),
        out_shape=jax.ShapeDtypeStruct(shape, jnp.float32),
        in_specs=[pl.BlockSpec(memory_space=pl.ANY)] * 2,
        out_specs=pl.BlockSpec(memory_space=pl.ANY),
        scratch_shapes=[
            pltpu.VMEM((rows // 128, 128), jnp.int32),
            pltpu.VMEM(shape, jnp.float32),
            pltpu.SemaphoreType.DMA((5,)),
            pltpu.SemaphoreType.DMA((4,)),
        ],
        compiler_params=pltpu.CompilerParams(vmem_limit_bytes=61 * 2**20),
    )(flips.reshape(rows // 128, 128), panel.reshape(shape))


def device_kernel(in_ref, out_ref, held, sent):
    devices, rows, _ = in_ref.shape
    strip = 8
    quarter = rows // 4

    def body(step, carry):
        at = pl.multiple_of(step * strip, strip)
        items = [in_ref[d, pl.ds(at, strip), :] for d in range(devices)]
        apart = 1
        while apart < devices:
            items = [
                items[d] + items[d ^ apart] if d & apart == 0 else items[d ^ apart] - items[d]
                for d in range(devices)
            ]
            apart *= 2
        for d in range(devices):
            held[d, pl.ds(at, strip), :] = items[d]
        return carry

    copies = []
    for part in range(4):
        first = part * quarter // strip
        lax.fori_loop(first, first + quarter // strip, body, 0)
        span = pl.ds(part * quarter, quarter)
        copies.append(
            pltpu.make_async_copy(held.at[:, span, :], out_ref.at[:, span, :], sent.at[part])
        )
        copies[-1].start()
    for copy in copies:
        copy.wait()


def device_sums(value):
    return pl.pallas_call(
        device_kernel,
        out_shape=jax.ShapeDtypeStruct(value.shape, jnp.float32),
        in_specs=[pl.BlockSpec(memory_space=pltpu.VMEM)],
        out_specs=pl.BlockSpec(memory_space=pl.ANY),
        scratch_shapes=[
            pltpu.VMEM(value.shape, jnp.float32),
            pltpu.SemaphoreType.DMA((4,)),
        ],
        compiler_params=pltpu.CompilerParams(vmem_limit_bytes=32 * 2**20),
    )(value)


def store_kernel(value_ref, out_ref, sent):
    copy = pltpu.make_async_copy(value_ref, out_ref, sent)
    copy.start()
    copy.wait()


def store(value):
    return pl.pallas_call(
        store_kernel,
        out_shape=jax.ShapeDtypeStruct(value.shape, jnp.float32),
        in_specs=[pl.BlockSpec(memory_space=pltpu.VMEM)],
        out_specs=pl.BlockSpec(memory_space=pl.ANY),
        scratch_shapes=[pltpu.SemaphoreType.DMA],
        compiler_params=pltpu.CompilerParams(vmem_limit_bytes=8 * 2**20),
    )(value)


def index_kernel(rows_here, most, bases_ref, picks_ref, out_ref):
    picks = picks_ref[...]
    devices, per = picks.shape
    before = lax.broadcasted_iota(jnp.int32, (per, per), 0)
    earlier = before < lax.broadcasted_iota(jnp.int32, (per, per), 1)
    earlier = jnp.where(earlier, 1.0, 0.0).astype(jnp.bfloat16)
    for which in range(out_ref.shape[0]):
        offsets = picks - bases_ref[which]
        owned = (offsets >= 0) & (offsets < rows_here)
        ones = jnp.where(owned, 1.0, 0.0).astype(jnp.bfloat16)
        rank = jnp.dot(ones, earlier, preferred_element_type=jnp.float32)
        rank = jnp.where(owned, rank, -1.0)
        marked = (offsets + 1).astype(jnp.float32)
        for slot in range(most):
            hit = jnp.where(rank == float(slot), marked, 0.0)
            row = jnp.sum(hit, axis=1, keepdims=True).astype(jnp.int32) - 1
            out_ref[which, :, slot : slot + 1] = row


def send_rows(picks, owners, rows_here, devices, most):
    bases = jnp.stack(owners) * rows_here
    rows = pl.pallas_call(
        functools.partial(index_kernel, rows_here, most),
        out_shape=jax.ShapeDtypeStruct((len(owners), devices, most), jnp.int32),
        in_specs=[
            pl.BlockSpec(memory_space=pltpu.SMEM),
            pl.BlockSpec(memory_space=pltpu.VMEM),
        ],
        out_specs=pl.BlockSpec(memory_space=pltpu.VMEM),
        compiler_params=pltpu.CompilerParams(vmem_limit_bytes=8 * 2**20),
    )(bases.astype(jnp.int32), picks.reshape(devices, -1))
    return rows.reshape(len(owners) * devices * most)


def count_kernel(rows_here, wide, me_ref, picks_ref, out_ref):
    picks = picks_ref[...]
    rows, devices = out_ref.shape
    owner = picks >> rows_here.bit_length() - 1
    owner = (owner & wide - 1) * (devices // wide) + (owner >> wide.bit_length() - 1)
    local = picks & rows_here - 1
    held = local >> rows.bit_length() - 1 == me_ref[0]
    place = jnp.where(held, local & rows - 1, -1)
    shape = (devices, picks.shape[1])
    owners = jnp.where(lax.broadcasted_iota(jnp.int32, shape, 0) == owner, 1.0, 0.0)
    shape = (rows, picks.shape[1])
    places = jnp.where(lax.broadcasted_iota(jnp.int32, shape, 0) == place, 1.0, 0.0)
    out_ref[...] = lax.dot_general(
        places.astype(jnp.bfloat16),
        owners.astype(jnp.bfloat16),
        (((1,), (1,)), ((), ())),
        preferred_element_type=jnp.float32,
    )


def count_picks(picks, me, rows_here, devices):
    return pl.pallas_call(
        functools.partial(count_kernel, rows_here, lax.axis_size("wide")),
        out_shape=jax.ShapeDtypeStruct((rows_here // devices, devices), jnp.float32),
        in_specs=[
            pl.BlockSpec(memory_space=pltpu.SMEM),
            pl.BlockSpec(memory_space=pltpu.VMEM),
        ],
        out_specs=pl.BlockSpec(memory_space=pltpu.VMEM),
        compiler_params=pltpu.CompilerParams(vmem_limit_bytes=32 * 2**20),
    )(me.reshape(1).astype(jnp.int32), picks.reshape(1, -1))


def halves(value):
    high = value.astype(jnp.bfloat16)
    return high, (value - high.astype(jnp.float32)).astype(jnp.bfloat16)


def part_kernel(counts_ref, held_ref, out_ref):
    devices, _, width = held_ref.shape
    total = jnp.zeros((width, 2 * width), jnp.float32)
    rest = jnp.zeros((width, width), jnp.float32)
    for d in range(devices):
        rows = held_ref[d]
        high, low = halves(rows)
        weighted, spare = halves(rows * counts_ref[:, d : d + 1])
        over_rows = (((0,), (0,)), ((), ()))
        both = jnp.concatenate([weighted, spare], axis=1)
        total += lax.dot_general(high, both, over_rows, preferred_element_type=jnp.float32)
        rest += lax.dot_general(low, weighted, over_rows, preferred_element_type=jnp.float32)
    out_ref[...] = total[:, :width] + total[:, width:] + rest


def gram_part(counts, held):
    width = held.shape[2]
    return pl.pallas_call(
        part_kernel,
        out_shape=jax.ShapeDtypeStruct((width, width), jnp.float32),
        in_specs=[pl.BlockSpec(memory_space=pltpu.VMEM)] * 2,
        out_specs=pl.BlockSpec(memory_space=pltpu.VMEM),
        compiler_params=pltpu.CompilerParams(vmem_limit_bytes=32 * 2**20),
    )(counts, held)


def swap(value, axis, apart):
    pairs = [(source, source ^ apart) for source in range(lax.axis_size(axis))]
    return lax.ppermute(value, axis, pairs)


def scatter_sum(value, axis):
    upper = lax.axis_index(axis) & 1
    half = value.shape[0] // 2
    keep = lax.dynamic_slice_in_dim(value, upper * half, half)
    give = lax.dynamic_slice_in_dim(value, (1 - upper) * half, half)
    return keep + swap(give, axis, 1)


def gather_halves(value, axis):
    rows, width = value.shape
    blank = jnp.zeros((2 * rows, width), jnp.float32)
    at = (lax.axis_index(axis) & 1) * rows
    value = lax.dynamic_update_slice_in_dim(blank, value, at, 0)
    return value, swap(value, axis, 1)


def landing(block, rows_here, most):
    owners = block // rows_here
    order = jnp.arange(block.shape[0], dtype=jnp.int32)
    earlier = (owners[:, None] == owners[None, :]) & (order[None, :] < order[:, None])
    return owners * most + jnp.sum(earlier.astype(jnp.int32), axis=1)


def on_device(panel, flips, picks):
    rows_here, width = panel.shape
    devices = lax.axis_size("narrow") * lax.axis_size("wide")
    scale = 1.0 / float(rows_here * devices) ** 0.5
    me = lax.axis_index(AXES)
    per = picks.shape[0] // devices
    most = -(-per // devices)

    local = local_transform(panel, flips, scale)
    local = local.reshape(devices, rows_here // devices, width)
    wanted = send_rows(picks, [me], rows_here, devices, most)
    spots = landing(lax.dynamic_slice(picks, (me * per,), (per,)), rows_here, most)
    counts = count_picks(picks, lax.axis_index(TURNED), rows_here, devices)
    slices = lax.all_to_all(local, TURNED, 0, 0, tiled=True)
    slices, wanted, spots, counts = lax.optimization_barrier((slices, wanted, spots, counts))
    slices = device_sums(slices)
    mixed = lax.all_to_all(slices, TURNED, 0, 0, tiled=True)
    gram = gram_part(counts, slices)
    gram = scatter_sum(gram, "narrow")
    for axis, low in (("narrow", 2), ("wide", 1)):
        while low < lax.axis_size(axis):
            gram = gram + swap(gram, axis, low)
            low *= 2
    mixed, gram = lax.optimization_barrier((mixed, gram))
    mixed = mixed.reshape(rows_here, width)
    chosen = jnp.take(mixed, wanted, axis=0, mode="clip")
    landed = lax.all_to_all(chosen.reshape(devices, most, width), AXES, 0, 0, tiled=True)
    gram, other = gather_halves(gram, "narrow")
    mixed, other = lax.optimization_barrier((mixed, other))
    mixed = store(mixed)
    gram = (gram + other) / float(picks.shape[0])
    landed, mixed, gram = lax.optimization_barrier((landed, mixed, gram))
    sketch = jnp.take(landed.reshape(devices * most, width), spots, axis=0, mode="clip")
    return (mixed, sketch, gram)


def solution(mesh):
    in_specs = (P(AXES, None), P(AXES), P())
    out_specs = (P(AXES, None), P(AXES, None), P())
    return jax.shard_map(
        on_device, mesh=mesh, in_specs=in_specs, out_specs=out_specs, check_vma=False
    )
```

```python
import functools

import jax
import jax.numpy as jnp
from jax import lax
from jax.experimental import pallas as pl
from jax.experimental.pallas import tpu as pltpu
from jax.sharding import PartitionSpec as P

BLOCK = 256
AXES = ("narrow", "wide")
TURNED = ("wide", "narrow")


def signs(order):
    rows = lax.broadcasted_iota(jnp.int32, (order, order), 0)
    both = rows & lax.broadcasted_iota(jnp.int32, (order, order), 1)
    parity = jnp.zeros((order, order), jnp.int32)
    for level in range(order.bit_length() - 1):
        parity = parity ^ (both >> level & 1)
    return (1 - 2 * parity).astype(jnp.float32)


def local_kernel(scale, flips_ref, panel_ref, out_ref, flags, held, arrived, sent):
    blocks, _, width = panel_ref.shape
    per = BLOCK // flips_ref.shape[1]
    share = blocks // 8
    loads = [pltpu.make_async_copy(flips_ref, flags, arrived.at[8])]
    for part in range(8):
        span = pl.ds(part * share, share)
        loads.append(pltpu.make_async_copy(panel_ref.at[span], held.at[span], arrived.at[part]))
    for load in loads:
        load.start()
    base = signs(BLOCK)
    loads[0].wait()
    for b in range(blocks):
        if b % share == 0:
            loads[1 + b // share].wait()
        row = jnp.concatenate([flags[b * per + i : b * per + i + 1, :] for i in range(per)], axis=1)
        mixer = (base * (1 - 2 * row).astype(jnp.float32)).astype(jnp.bfloat16)
        values = held[b]
        high = values.astype(jnp.bfloat16)
        rest = values - high.astype(jnp.float32)
        middle = rest.astype(jnp.bfloat16)
        low = (rest - middle.astype(jnp.float32)).astype(jnp.bfloat16)
        parts = jnp.concatenate([high, middle, low], axis=1)
        out = jnp.dot(mixer, parts, preferred_element_type=jnp.float32)
        held[b] = out[:, :width] + out[:, width : 2 * width] + out[:, 2 * width :]
    strip = 16
    piece = BLOCK // 8

    def body(step, carry):
        at = pl.multiple_of(step * strip, strip)
        items = [held[b, pl.ds(at, strip), :] for b in range(blocks)]
        apart = 1
        while apart < blocks:
            items = [
                items[b] + items[b ^ apart] if b & apart == 0 else items[b ^ apart] - items[b]
                for b in range(blocks)
            ]
            apart *= 2
        for b in range(blocks):
            held[b, pl.ds(at, strip), :] = items[b] * scale
        return carry

    copies = []
    for part in range(8):
        first = part * piece // strip
        lax.fori_loop(first, first + piece // strip, body, 0)
        span = pl.ds(part * piece, piece)
        copies.append(
            pltpu.make_async_copy(held.at[:, span, :], out_ref.at[:, span, :], sent.at[part])
        )
        copies[-1].start()
    for copy in copies:
        copy.wait()


def local_transform(panel, flips, scale):
    rows, width = panel.shape
    shape = (rows // BLOCK, BLOCK, width)
    return pl.pallas_call(
        functools.partial(local_kernel, scale),
        out_shape=jax.ShapeDtypeStruct(shape, jnp.float32),
        in_specs=[pl.BlockSpec(memory_space=pl.ANY)] * 2,
        out_specs=pl.BlockSpec(memory_space=pl.ANY),
        scratch_shapes=[
            pltpu.VMEM((rows // 128, 128), jnp.int32),
            pltpu.VMEM(shape, jnp.float32),
            pltpu.SemaphoreType.DMA((9,)),
            pltpu.SemaphoreType.DMA((8,)),
        ],
        compiler_params=pltpu.CompilerParams(vmem_limit_bytes=61 * 2**20),
    )(flips.reshape(rows // 128, 128), panel.reshape(shape))


def device_kernel(in_ref, out_ref, held, sent):
    devices, rows, _ = in_ref.shape
    strip = 8
    parts = sent.shape[0]
    share = rows // parts

    def body(step, carry):
        at = pl.multiple_of(step * strip, strip)
        items = [in_ref[d, pl.ds(at, strip), :] for d in range(devices)]
        apart = 1
        while apart < devices:
            items = [
                items[d] + items[d ^ apart] if d & apart == 0 else items[d ^ apart] - items[d]
                for d in range(devices)
            ]
            apart *= 2
        for d in range(devices):
            held[d, pl.ds(at, strip), :] = items[d]
        return carry

    copies = []
    for part in range(parts):
        first = part * share // strip
        lax.fori_loop(first, first + share // strip, body, 0)
        span = pl.ds(part * share, share)
        copies.append(
            pltpu.make_async_copy(held.at[:, span, :], out_ref.at[:, span, :], sent.at[part])
        )
        copies[-1].start()
    for copy in copies:
        copy.wait()


def device_sums(value):
    return pl.pallas_call(
        device_kernel,
        out_shape=jax.ShapeDtypeStruct(value.shape, jnp.float32),
        in_specs=[pl.BlockSpec(memory_space=pltpu.VMEM)],
        out_specs=pl.BlockSpec(memory_space=pl.ANY),
        scratch_shapes=[
            pltpu.VMEM(value.shape, jnp.float32),
            pltpu.SemaphoreType.DMA((min(8, value.shape[1] // 8),)),
        ],
        compiler_params=pltpu.CompilerParams(vmem_limit_bytes=32 * 2**20),
    )(value)


def store_kernel(value_ref, out_ref, sent):
    copy = pltpu.make_async_copy(value_ref, out_ref, sent)
    copy.start()
    copy.wait()


def store(value):
    return pl.pallas_call(
        store_kernel,
        out_shape=jax.ShapeDtypeStruct(value.shape, jnp.float32),
        in_specs=[pl.BlockSpec(memory_space=pltpu.VMEM)],
        out_specs=pl.BlockSpec(memory_space=pl.ANY),
        scratch_shapes=[pltpu.SemaphoreType.DMA],
        compiler_params=pltpu.CompilerParams(vmem_limit_bytes=8 * 2**20),
    )(value)


def index_kernel(rows_here, most, bases_ref, picks_ref, out_ref):
    picks = picks_ref[...]
    devices, per = picks.shape
    before = lax.broadcasted_iota(jnp.int32, (per, per), 0)
    earlier = before < lax.broadcasted_iota(jnp.int32, (per, per), 1)
    earlier = jnp.where(earlier, 1.0, 0.0).astype(jnp.bfloat16)
    for which in range(out_ref.shape[0]):
        offsets = picks - bases_ref[which]
        owned = (offsets >= 0) & (offsets < rows_here)
        ones = jnp.where(owned, 1.0, 0.0).astype(jnp.bfloat16)
        rank = jnp.dot(ones, earlier, preferred_element_type=jnp.float32)
        rank = jnp.where(owned, rank, -1.0)
        marked = (offsets + 1).astype(jnp.float32)
        for slot in range(most):
            hit = jnp.where(rank == float(slot), marked, 0.0)
            row = jnp.sum(hit, axis=1, keepdims=True).astype(jnp.int32) - 1
            out_ref[which, :, slot : slot + 1] = row


def send_rows(picks, owners, rows_here, devices, most):
    bases = jnp.stack(owners) * rows_here
    rows = pl.pallas_call(
        functools.partial(index_kernel, rows_here, most),
        out_shape=jax.ShapeDtypeStruct((len(owners), devices, most), jnp.int32),
        in_specs=[
            pl.BlockSpec(memory_space=pltpu.SMEM),
            pl.BlockSpec(memory_space=pltpu.VMEM),
        ],
        out_specs=pl.BlockSpec(memory_space=pltpu.VMEM),
        compiler_params=pltpu.CompilerParams(vmem_limit_bytes=8 * 2**20),
    )(bases.astype(jnp.int32), picks.reshape(devices, -1))
    return rows.reshape(len(owners) * devices * most)


def count_kernel(rows_here, wide, me_ref, picks_ref, out_ref):
    picks = picks_ref[...]
    rows, devices = out_ref.shape
    owner = picks >> rows_here.bit_length() - 1
    owner = (owner & wide - 1) * (devices // wide) + (owner >> wide.bit_length() - 1)
    local = picks & rows_here - 1
    held = local >> rows.bit_length() - 1 == me_ref[0]
    place = jnp.where(held, local & rows - 1, -1)
    shape = (devices, picks.shape[1])
    owners = jnp.where(lax.broadcasted_iota(jnp.int32, shape, 0) == owner, 1.0, 0.0)
    shape = (rows, picks.shape[1])
    places = jnp.where(lax.broadcasted_iota(jnp.int32, shape, 0) == place, 1.0, 0.0)
    out_ref[...] = lax.dot_general(
        places.astype(jnp.bfloat16),
        owners.astype(jnp.bfloat16),
        (((1,), (1,)), ((), ())),
        preferred_element_type=jnp.float32,
    )


def count_picks(picks, me, rows_here, devices):
    return pl.pallas_call(
        functools.partial(count_kernel, rows_here, lax.axis_size("wide")),
        out_shape=jax.ShapeDtypeStruct((rows_here // devices, devices), jnp.float32),
        in_specs=[
            pl.BlockSpec(memory_space=pltpu.SMEM),
            pl.BlockSpec(memory_space=pltpu.VMEM),
        ],
        out_specs=pl.BlockSpec(memory_space=pltpu.VMEM),
        compiler_params=pltpu.CompilerParams(vmem_limit_bytes=32 * 2**20),
    )(me.reshape(1).astype(jnp.int32), picks.reshape(1, -1))


def halves(value):
    high = value.astype(jnp.bfloat16)
    return high, (value - high.astype(jnp.float32)).astype(jnp.bfloat16)


def part_kernel(counts_ref, held_ref, out_ref):
    devices, _, width = held_ref.shape
    total = jnp.zeros((width, 2 * width), jnp.float32)
    rest = jnp.zeros((width, width), jnp.float32)
    for d in range(devices):
        rows = held_ref[d]
        high, low = halves(rows)
        weighted, spare = halves(rows * counts_ref[:, d : d + 1])
        over_rows = (((0,), (0,)), ((), ()))
        both = jnp.concatenate([weighted, spare], axis=1)
        total += lax.dot_general(high, both, over_rows, preferred_element_type=jnp.float32)
        rest += lax.dot_general(low, weighted, over_rows, preferred_element_type=jnp.float32)
    out_ref[...] = total[:, :width] + total[:, width:] + rest


def gram_part(counts, held):
    width = held.shape[2]
    return pl.pallas_call(
        part_kernel,
        out_shape=jax.ShapeDtypeStruct((width, width), jnp.float32),
        in_specs=[pl.BlockSpec(memory_space=pltpu.VMEM)] * 2,
        out_specs=pl.BlockSpec(memory_space=pltpu.VMEM),
        compiler_params=pltpu.CompilerParams(vmem_limit_bytes=32 * 2**20),
    )(counts, held)


def swap(value, axis, apart):
    pairs = [(source, source ^ apart) for source in range(lax.axis_size(axis))]
    return lax.ppermute(value, axis, pairs)


def scatter_sum(value, axis):
    upper = lax.axis_index(axis) & 1
    half = value.shape[0] // 2
    keep = lax.dynamic_slice_in_dim(value, upper * half, half)
    give = lax.dynamic_slice_in_dim(value, (1 - upper) * half, half)
    return keep + swap(give, axis, 1)


def gather_halves(value, axis):
    rows, width = value.shape
    blank = jnp.zeros((2 * rows, width), jnp.float32)
    at = (lax.axis_index(axis) & 1) * rows
    value = lax.dynamic_update_slice_in_dim(blank, value, at, 0)
    return value, swap(value, axis, 1)


def landing(block, rows_here, most):
    owners = block // rows_here
    order = jnp.arange(block.shape[0], dtype=jnp.int32)
    earlier = (owners[:, None] == owners[None, :]) & (order[None, :] < order[:, None])
    return owners * most + jnp.sum(earlier.astype(jnp.int32), axis=1)


def on_device(panel, flips, picks):
    rows_here, width = panel.shape
    devices = lax.axis_size("narrow") * lax.axis_size("wide")
    scale = 1.0 / float(rows_here * devices) ** 0.5
    me = lax.axis_index(AXES)
    per = picks.shape[0] // devices
    most = -(-per // devices)

    local = local_transform(panel, flips, scale)
    local = local.reshape(devices, rows_here // devices, width)
    wanted = send_rows(picks, [me], rows_here, devices, most)
    spots = landing(lax.dynamic_slice(picks, (me * per,), (per,)), rows_here, most)
    slots = jnp.arange(devices * most, dtype=jnp.int32)
    order = (spots[:, None] == slots[None, :]).astype(jnp.float32)
    counts = count_picks(picks, lax.axis_index(TURNED), rows_here, devices)
    slices = lax.all_to_all(local, TURNED, 0, 0, tiled=True)
    slices, wanted, order, counts = lax.optimization_barrier((slices, wanted, order, counts))
    slices = device_sums(slices)
    mixed = lax.all_to_all(slices, TURNED, 0, 0, tiled=True)
    gram = gram_part(counts, slices)
    gram = scatter_sum(gram, "narrow")
    for axis, low in (("narrow", 2), ("wide", 1)):
        while low < lax.axis_size(axis):
            gram = gram + swap(gram, axis, low)
            low *= 2
    mixed, gram = lax.optimization_barrier((mixed, gram))
    mixed = mixed.reshape(rows_here, width)
    chosen = jnp.take(mixed, wanted, axis=0, mode="clip")
    landed = lax.all_to_all(chosen.reshape(devices, most, width), AXES, 0, 0, tiled=True)
    gram, other = gather_halves(gram, "narrow")
    mixed, other = lax.optimization_barrier((mixed, other))
    mixed = store(mixed)
    gram = (gram + other) / float(picks.shape[0])
    landed, mixed, gram = lax.optimization_barrier((landed, mixed, gram))
    landed = landed.reshape(devices * most, width)
    sketch = jnp.dot(order, landed, precision=lax.Precision.HIGHEST)
    return (mixed, sketch, gram)


def solution(mesh):
    in_specs = (P(AXES, None), P(AXES), P())
    out_specs = (P(AXES, None), P(AXES, None), P())
    return jax.shard_map(
        on_device, mesh=mesh, in_specs=in_specs, out_specs=out_specs, check_vma=False
    )
```

```python
import functools

import jax
import jax.numpy as jnp
from jax import lax
from jax.experimental import pallas as pl
from jax.experimental.pallas import tpu as pltpu
from jax.sharding import PartitionSpec as P

BLOCK = 256
AXES = ("narrow", "wide")
TURNED = ("wide", "narrow")


def signs(order):
    rows = lax.broadcasted_iota(jnp.int32, (order, order), 0)
    both = rows & lax.broadcasted_iota(jnp.int32, (order, order), 1)
    parity = jnp.zeros((order, order), jnp.int32)
    for level in range(order.bit_length() - 1):
        parity = parity ^ (both >> level & 1)
    return (1 - 2 * parity).astype(jnp.float32)


def halves(value):
    high = value.astype(jnp.bfloat16)
    return high, (value - high.astype(jnp.float32)).astype(jnp.bfloat16)


def local_kernel(scale, flips_ref, panel_ref, out_ref, flags, held, arrived, sent):
    blocks, _, width = panel_ref.shape
    per = BLOCK // flips_ref.shape[1]
    share = blocks // 4
    loads = [pltpu.make_async_copy(flips_ref, flags, arrived.at[4])]
    for part in range(4):
        span = pl.ds(part * share, share)
        loads.append(pltpu.make_async_copy(panel_ref.at[span], held.at[span], arrived.at[part]))
    for load in loads:
        load.start()
    base = signs(BLOCK)
    loads[0].wait()
    for b in range(blocks):
        if b % share == 0:
            loads[1 + b // share].wait()
        row = jnp.concatenate([flags[b * per + i : b * per + i + 1, :] for i in range(per)], axis=1)
        mixer = (base * (1 - 2 * row).astype(jnp.float32)).astype(jnp.bfloat16)
        parts = jnp.concatenate(halves(held[b]), axis=1)
        out = jnp.dot(mixer, parts, preferred_element_type=jnp.float32)
        held[b] = out[:, :width] + out[:, width:]
    strip = 16
    piece = BLOCK // 4

    def body(step, carry):
        at = pl.multiple_of(step * strip, strip)
        items = [held[b, pl.ds(at, strip), :] for b in range(blocks)]
        apart = 1
        while apart < blocks:
            items = [
                items[b] + items[b ^ apart] if b & apart == 0 else items[b ^ apart] - items[b]
                for b in range(blocks)
            ]
            apart *= 2
        for b in range(blocks):
            held[b, pl.ds(at, strip), :] = items[b] * scale
        return carry

    copies = []
    for part in range(4):
        first = part * piece // strip
        lax.fori_loop(first, first + piece // strip, body, 0)
        span = pl.ds(part * piece, piece)
        copies.append(
            pltpu.make_async_copy(held.at[:, span, :], out_ref.at[:, span, :], sent.at[part])
        )
        copies[-1].start()
    for copy in copies:
        copy.wait()


def local_transform(panel, flips, scale):
    rows, width = panel.shape
    shape = (rows // BLOCK, BLOCK, width)
    return pl.pallas_call(
        functools.partial(local_kernel, scale),
        out_shape=jax.ShapeDtypeStruct(shape, jnp.float32),
        in_specs=[pl.BlockSpec(memory_space=pl.ANY)] * 2,
        out_specs=pl.BlockSpec(memory_space=pl.ANY),
        scratch_shapes=[
            pltpu.VMEM((rows // 128, 128), jnp.int32),
            pltpu.VMEM(shape, jnp.float32),
            pltpu.SemaphoreType.DMA((5,)),
            pltpu.SemaphoreType.DMA((4,)),
        ],
        compiler_params=pltpu.CompilerParams(vmem_limit_bytes=61 * 2**20),
    )(flips.reshape(rows // 128, 128), panel.reshape(shape))


def device_kernel(in_ref, out_ref, held, sent):
    devices, rows, _ = in_ref.shape
    strip = 8
    parts = sent.shape[0]
    share = rows // parts

    def body(step, carry):
        at = pl.multiple_of(step * strip, strip)
        items = [in_ref[d, pl.ds(at, strip), :] for d in range(devices)]
        apart = 1
        while apart < devices:
            items = [
                items[d] + items[d ^ apart] if d & apart == 0 else items[d ^ apart] - items[d]
                for d in range(devices)
            ]
            apart *= 2
        for d in range(devices):
            held[d, pl.ds(at, strip), :] = items[d]
        return carry

    copies = []
    for part in range(parts):
        first = part * share // strip
        lax.fori_loop(first, first + share // strip, body, 0)
        span = pl.ds(part * share, share)
        copies.append(
            pltpu.make_async_copy(held.at[:, span, :], out_ref.at[:, span, :], sent.at[part])
        )
        copies[-1].start()
    for copy in copies:
        copy.wait()


def device_sums(value):
    return pl.pallas_call(
        device_kernel,
        out_shape=jax.ShapeDtypeStruct(value.shape, jnp.float32),
        in_specs=[pl.BlockSpec(memory_space=pltpu.VMEM)],
        out_specs=pl.BlockSpec(memory_space=pl.ANY),
        scratch_shapes=[
            pltpu.VMEM(value.shape, jnp.float32),
            pltpu.SemaphoreType.DMA((min(8, value.shape[1] // 8),)),
        ],
        compiler_params=pltpu.CompilerParams(vmem_limit_bytes=32 * 2**20),
    )(value)


def store_kernel(value_ref, out_ref, sent):
    copy = pltpu.make_async_copy(value_ref, out_ref, sent)
    copy.start()
    copy.wait()


def store(value):
    return pl.pallas_call(
        store_kernel,
        out_shape=jax.ShapeDtypeStruct(value.shape, jnp.float32),
        in_specs=[pl.BlockSpec(memory_space=pltpu.VMEM)],
        out_specs=pl.BlockSpec(memory_space=pl.ANY),
        scratch_shapes=[pltpu.SemaphoreType.DMA],
        compiler_params=pltpu.CompilerParams(vmem_limit_bytes=8 * 2**20),
    )(value)


def index_kernel(rows_here, most, bases_ref, picks_ref, out_ref):
    picks = picks_ref[...]
    devices, per = picks.shape
    before = lax.broadcasted_iota(jnp.int32, (per, per), 0)
    earlier = before < lax.broadcasted_iota(jnp.int32, (per, per), 1)
    earlier = jnp.where(earlier, 1.0, 0.0).astype(jnp.bfloat16)
    for which in range(out_ref.shape[0]):
        offsets = picks - bases_ref[which]
        owned = (offsets >= 0) & (offsets < rows_here)
        ones = jnp.where(owned, 1.0, 0.0).astype(jnp.bfloat16)
        rank = jnp.dot(ones, earlier, preferred_element_type=jnp.float32)
        rank = jnp.where(owned, rank, -1.0)
        marked = (offsets + 1).astype(jnp.float32)
        for slot in range(most):
            hit = jnp.where(rank == float(slot), marked, 0.0)
            row = jnp.sum(hit, axis=1, keepdims=True).astype(jnp.int32) - 1
            out_ref[which, :, slot : slot + 1] = row


def send_rows(picks, owners, rows_here, devices, most):
    bases = jnp.stack(owners) * rows_here
    rows = pl.pallas_call(
        functools.partial(index_kernel, rows_here, most),
        out_shape=jax.ShapeDtypeStruct((len(owners), devices, most), jnp.int32),
        in_specs=[
            pl.BlockSpec(memory_space=pltpu.SMEM),
            pl.BlockSpec(memory_space=pltpu.VMEM),
        ],
        out_specs=pl.BlockSpec(memory_space=pltpu.VMEM),
        compiler_params=pltpu.CompilerParams(vmem_limit_bytes=8 * 2**20),
    )(bases.astype(jnp.int32), picks.reshape(devices, -1))
    return rows.reshape(len(owners) * devices * most)


def count_kernel(rows_here, wide, me_ref, picks_ref, out_ref):
    picks = picks_ref[...]
    rows, devices = out_ref.shape
    owner = picks >> rows_here.bit_length() - 1
    owner = (owner & wide - 1) * (devices // wide) + (owner >> wide.bit_length() - 1)
    local = picks & rows_here - 1
    held = local >> rows.bit_length() - 1 == me_ref[0]
    place = jnp.where(held, local & rows - 1, -1)
    shape = (devices, picks.shape[1])
    owners = jnp.where(lax.broadcasted_iota(jnp.int32, shape, 0) == owner, 1.0, 0.0)
    shape = (rows, picks.shape[1])
    places = jnp.where(lax.broadcasted_iota(jnp.int32, shape, 0) == place, 1.0, 0.0)
    out_ref[...] = lax.dot_general(
        places.astype(jnp.bfloat16),
        owners.astype(jnp.bfloat16),
        (((1,), (1,)), ((), ())),
        preferred_element_type=jnp.float32,
    )


def count_picks(picks, me, rows_here, devices):
    return pl.pallas_call(
        functools.partial(count_kernel, rows_here, lax.axis_size("wide")),
        out_shape=jax.ShapeDtypeStruct((rows_here // devices, devices), jnp.float32),
        in_specs=[
            pl.BlockSpec(memory_space=pltpu.SMEM),
            pl.BlockSpec(memory_space=pltpu.VMEM),
        ],
        out_specs=pl.BlockSpec(memory_space=pltpu.VMEM),
        compiler_params=pltpu.CompilerParams(vmem_limit_bytes=32 * 2**20),
    )(me.reshape(1).astype(jnp.int32), picks.reshape(1, -1))


def part_kernel(counts_ref, held_ref, out_ref):
    devices, _, width = held_ref.shape
    total = jnp.zeros((width, 2 * width), jnp.float32)
    rest = jnp.zeros((width, width), jnp.float32)
    for d in range(devices):
        rows = held_ref[d]
        high, low = halves(rows)
        weighted, spare = halves(rows * counts_ref[:, d : d + 1])
        over_rows = (((0,), (0,)), ((), ()))
        both = jnp.concatenate([weighted, spare], axis=1)
        total += lax.dot_general(high, both, over_rows, preferred_element_type=jnp.float32)
        rest += lax.dot_general(low, weighted, over_rows, preferred_element_type=jnp.float32)
    out_ref[...] = total[:, :width] + total[:, width:] + rest


def gram_part(counts, held):
    width = held.shape[2]
    return pl.pallas_call(
        part_kernel,
        out_shape=jax.ShapeDtypeStruct((width, width), jnp.float32),
        in_specs=[pl.BlockSpec(memory_space=pltpu.VMEM)] * 2,
        out_specs=pl.BlockSpec(memory_space=pltpu.VMEM),
        compiler_params=pltpu.CompilerParams(vmem_limit_bytes=32 * 2**20),
    )(counts, held)


def swap(value, axis, apart):
    pairs = [(source, source ^ apart) for source in range(lax.axis_size(axis))]
    return lax.ppermute(value, axis, pairs)


def scatter_sum(value, axis):
    upper = lax.axis_index(axis) & 1
    half = value.shape[0] // 2
    keep = lax.dynamic_slice_in_dim(value, upper * half, half)
    give = lax.dynamic_slice_in_dim(value, (1 - upper) * half, half)
    return keep + swap(give, axis, 1)


def gather_halves(value, axis):
    rows, width = value.shape
    blank = jnp.zeros((2 * rows, width), jnp.float32)
    at = (lax.axis_index(axis) & 1) * rows
    value = lax.dynamic_update_slice_in_dim(blank, value, at, 0)
    return value, swap(value, axis, 1)


def landing(block, rows_here, most):
    owners = block // rows_here
    order = jnp.arange(block.shape[0], dtype=jnp.int32)
    earlier = (owners[:, None] == owners[None, :]) & (order[None, :] < order[:, None])
    return owners * most + jnp.sum(earlier.astype(jnp.int32), axis=1)


def on_device(panel, flips, picks):
    rows_here, width = panel.shape
    devices = lax.axis_size("narrow") * lax.axis_size("wide")
    scale = 1.0 / float(rows_here * devices) ** 0.5
    me = lax.axis_index(AXES)
    per = picks.shape[0] // devices
    most = -(-per // devices)

    local = local_transform(panel, flips, scale)
    local = local.reshape(devices, rows_here // devices, width)
    wanted = send_rows(picks, [me], rows_here, devices, most)
    spots = landing(lax.dynamic_slice(picks, (me * per,), (per,)), rows_here, most)
    slots = jnp.arange(devices * most, dtype=jnp.int32)
    order = (spots[:, None] == slots[None, :]).astype(jnp.float32)
    counts = count_picks(picks, lax.axis_index(TURNED), rows_here, devices)
    slices = lax.all_to_all(local, TURNED, 0, 0, tiled=True)
    slices, wanted, order, counts = lax.optimization_barrier((slices, wanted, order, counts))
    slices = device_sums(slices)
    mixed = lax.all_to_all(slices, TURNED, 0, 0, tiled=True)
    gram = gram_part(counts, slices)
    gram = scatter_sum(gram, "narrow")
    for axis, low in (("narrow", 2), ("wide", 1)):
        while low < lax.axis_size(axis):
            gram = gram + swap(gram, axis, low)
            low *= 2
    mixed, gram = lax.optimization_barrier((mixed, gram))
    mixed = mixed.reshape(rows_here, width)
    chosen = jnp.take(mixed, wanted, axis=0, mode="clip")
    landed = lax.all_to_all(chosen.reshape(devices, most, width), AXES, 0, 0, tiled=True)
    gram, other = gather_halves(gram, "narrow")
    mixed, other = lax.optimization_barrier((mixed, other))
    mixed = store(mixed)
    gram = (gram + other) / float(picks.shape[0])
    landed, mixed, gram = lax.optimization_barrier((landed, mixed, gram))
    landed = landed.reshape(devices * most, width)
    sketch = jnp.dot(order, landed, precision=lax.Precision.HIGHEST)
    return (mixed, sketch, gram)


def solution(mesh):
    in_specs = (P(AXES, None), P(AXES), P())
    out_specs = (P(AXES, None), P(AXES, None), P())
    return jax.shard_map(
        on_device, mesh=mesh, in_specs=in_specs, out_specs=out_specs, check_vma=False
    )
```

```python
import functools

import jax
import jax.numpy as jnp
from jax import lax
from jax.experimental import pallas as pl
from jax.experimental.pallas import tpu as pltpu
from jax.sharding import PartitionSpec as P

BLOCK = 256
AXES = ("narrow", "wide")


def signs(order):
    rows = lax.broadcasted_iota(jnp.int32, (order, order), 0)
    both = rows & lax.broadcasted_iota(jnp.int32, (order, order), 1)
    parity = jnp.zeros((order, order), jnp.int32)
    for level in range(order.bit_length() - 1):
        parity = parity ^ (both >> level & 1)
    return (1 - 2 * parity).astype(jnp.float32)


def halves(value):
    high = value.astype(jnp.bfloat16)
    return high, (value - high.astype(jnp.float32)).astype(jnp.bfloat16)


def local_kernel(scale, flips_ref, panel_ref, out_ref, flags, held, arrived, sent):
    blocks, _, width = panel_ref.shape
    per = BLOCK // flips_ref.shape[1]
    share = blocks // 4
    loads = [pltpu.make_async_copy(flips_ref, flags, arrived.at[4])]
    for part in range(4):
        span = pl.ds(part * share, share)
        loads.append(pltpu.make_async_copy(panel_ref.at[span], held.at[span], arrived.at[part]))
    for load in loads:
        load.start()
    base = signs(BLOCK)
    loads[0].wait()
    for b in range(blocks):
        if b % share == 0:
            loads[1 + b // share].wait()
        row = jnp.concatenate([flags[b * per + i : b * per + i + 1, :] for i in range(per)], axis=1)
        mixer = (base * (1 - 2 * row).astype(jnp.float32)).astype(jnp.bfloat16)
        parts = jnp.concatenate(halves(held[b]), axis=1)
        out = jnp.dot(mixer, parts, preferred_element_type=jnp.float32)
        held[b] = out[:, :width] + out[:, width:]
    strip = 16
    piece = BLOCK // 4

    def body(step, carry):
        at = pl.multiple_of(step * strip, strip)
        items = [held[b, pl.ds(at, strip), :] for b in range(blocks)]
        apart = 1
        while apart < blocks:
            items = [
                items[b] + items[b ^ apart] if b & apart == 0 else items[b ^ apart] - items[b]
                for b in range(blocks)
            ]
            apart *= 2
        for b in range(blocks):
            held[b, pl.ds(at, strip), :] = items[b] * scale
        return carry

    copies = []
    for part in range(4):
        first = part * piece // strip
        lax.fori_loop(first, first + piece // strip, body, 0)
        span = pl.ds(part * piece, piece)
        copies.append(
            pltpu.make_async_copy(held.at[:, span, :], out_ref.at[:, span, :], sent.at[part])
        )
        copies[-1].start()
    for copy in copies:
        copy.wait()


def local_transform(panel, flips, scale):
    rows, width = panel.shape
    shape = (rows // BLOCK, BLOCK, width)
    return pl.pallas_call(
        functools.partial(local_kernel, scale),
        out_shape=jax.ShapeDtypeStruct(shape, jnp.float32),
        in_specs=[pl.BlockSpec(memory_space=pl.ANY)] * 2,
        out_specs=pl.BlockSpec(memory_space=pl.ANY),
        scratch_shapes=[
            pltpu.VMEM((rows // 128, 128), jnp.int32),
            pltpu.VMEM(shape, jnp.float32),
            pltpu.SemaphoreType.DMA((5,)),
            pltpu.SemaphoreType.DMA((4,)),
        ],
        compiler_params=pltpu.CompilerParams(vmem_limit_bytes=61 * 2**20),
    )(flips.reshape(rows // 128, 128), panel.reshape(shape))


def device_kernel(in_ref, out_ref, held, sent):
    devices, rows, _ = in_ref.shape
    strip = 8
    parts = sent.shape[0]
    share = rows // parts

    def body(step, carry):
        at = pl.multiple_of(step * strip, strip)
        items = [in_ref[d, pl.ds(at, strip), :] for d in range(devices)]
        apart = 1
        while apart < devices:
            items = [
                items[d] + items[d ^ apart] if d & apart == 0 else items[d ^ apart] - items[d]
                for d in range(devices)
            ]
            apart *= 2
        for d in range(devices):
            held[d, pl.ds(at, strip), :] = items[d]
        return carry

    copies = []
    for part in range(parts):
        first = part * share // strip
        lax.fori_loop(first, first + share // strip, body, 0)
        span = pl.ds(part * share, share)
        copies.append(
            pltpu.make_async_copy(held.at[:, span, :], out_ref.at[:, span, :], sent.at[part])
        )
        copies[-1].start()
    for copy in copies:
        copy.wait()


def device_sums(value):
    return pl.pallas_call(
        device_kernel,
        out_shape=jax.ShapeDtypeStruct(value.shape, jnp.float32),
        in_specs=[pl.BlockSpec(memory_space=pltpu.VMEM)],
        out_specs=pl.BlockSpec(memory_space=pl.ANY),
        scratch_shapes=[
            pltpu.VMEM(value.shape, jnp.float32),
            pltpu.SemaphoreType.DMA((min(8, value.shape[1] // 8),)),
        ],
        compiler_params=pltpu.CompilerParams(vmem_limit_bytes=32 * 2**20),
    )(value)


def store_kernel(value_ref, out_ref, sent):
    copy = pltpu.make_async_copy(value_ref, out_ref, sent)
    copy.start()
    copy.wait()


def store(value):
    return pl.pallas_call(
        store_kernel,
        out_shape=jax.ShapeDtypeStruct(value.shape, jnp.float32),
        in_specs=[pl.BlockSpec(memory_space=pltpu.VMEM)],
        out_specs=pl.BlockSpec(memory_space=pl.ANY),
        scratch_shapes=[pltpu.SemaphoreType.DMA],
        compiler_params=pltpu.CompilerParams(vmem_limit_bytes=8 * 2**20),
    )(value)


def index_kernel(rows_here, most, bases_ref, picks_ref, out_ref):
    picks = picks_ref[...]
    devices, per = picks.shape
    before = lax.broadcasted_iota(jnp.int32, (per, per), 0)
    earlier = before < lax.broadcasted_iota(jnp.int32, (per, per), 1)
    earlier = jnp.where(earlier, 1.0, 0.0).astype(jnp.bfloat16)
    for which in range(out_ref.shape[0]):
        offsets = picks - bases_ref[which]
        owned = (offsets >= 0) & (offsets < rows_here)
        ones = jnp.where(owned, 1.0, 0.0).astype(jnp.bfloat16)
        rank = jnp.dot(ones, earlier, preferred_element_type=jnp.float32)
        rank = jnp.where(owned, rank, -1.0)
        marked = (offsets + 1).astype(jnp.float32)
        for slot in range(most):
            hit = jnp.where(rank == float(slot), marked, 0.0)
            row = jnp.sum(hit, axis=1, keepdims=True).astype(jnp.int32) - 1
            out_ref[which, :, slot : slot + 1] = row


def send_rows(picks, owners, rows_here, devices, most):
    bases = jnp.stack(owners) * rows_here
    rows = pl.pallas_call(
        functools.partial(index_kernel, rows_here, most),
        out_shape=jax.ShapeDtypeStruct((len(owners), devices, most), jnp.int32),
        in_specs=[
            pl.BlockSpec(memory_space=pltpu.SMEM),
            pl.BlockSpec(memory_space=pltpu.VMEM),
        ],
        out_specs=pl.BlockSpec(memory_space=pltpu.VMEM),
        compiler_params=pltpu.CompilerParams(vmem_limit_bytes=8 * 2**20),
    )(bases.astype(jnp.int32), picks.reshape(devices, -1))
    return rows.reshape(len(owners) * devices * most)


def count_kernel(rows_here, me_ref, picks_ref, out_ref):
    picks = picks_ref[...]
    rows, devices = out_ref.shape
    owner = picks >> rows_here.bit_length() - 1
    local = picks & rows_here - 1
    held = local >> rows.bit_length() - 1 == me_ref[0]
    place = jnp.where(held, local & rows - 1, -1)
    shape = (devices, picks.shape[1])
    owners = jnp.where(lax.broadcasted_iota(jnp.int32, shape, 0) == owner, 1.0, 0.0)
    shape = (rows, picks.shape[1])
    places = jnp.where(lax.broadcasted_iota(jnp.int32, shape, 0) == place, 1.0, 0.0)
    out_ref[...] = lax.dot_general(
        places.astype(jnp.bfloat16),
        owners.astype(jnp.bfloat16),
        (((1,), (1,)), ((), ())),
        preferred_element_type=jnp.float32,
    )


def count_picks(picks, me, rows_here, devices):
    return pl.pallas_call(
        functools.partial(count_kernel, rows_here),
        out_shape=jax.ShapeDtypeStruct((rows_here // devices, devices), jnp.float32),
        in_specs=[
            pl.BlockSpec(memory_space=pltpu.SMEM),
            pl.BlockSpec(memory_space=pltpu.VMEM),
        ],
        out_specs=pl.BlockSpec(memory_space=pltpu.VMEM),
        compiler_params=pltpu.CompilerParams(vmem_limit_bytes=32 * 2**20),
    )(me.reshape(1).astype(jnp.int32), picks.reshape(1, -1))


def part_kernel(counts_ref, held_ref, out_ref):
    devices, _, width = held_ref.shape
    total = jnp.zeros((width, 2 * width), jnp.float32)
    rest = jnp.zeros((width, width), jnp.float32)
    for d in range(devices):
        rows = held_ref[d]
        high, low = halves(rows)
        weighted, spare = halves(rows * counts_ref[:, d : d + 1])
        over_rows = (((0,), (0,)), ((), ()))
        both = jnp.concatenate([weighted, spare], axis=1)
        total += lax.dot_general(high, both, over_rows, preferred_element_type=jnp.float32)
        rest += lax.dot_general(low, weighted, over_rows, preferred_element_type=jnp.float32)
    out_ref[...] = total[:, :width] + total[:, width:] + rest


def gram_part(counts, held):
    width = held.shape[2]
    return pl.pallas_call(
        part_kernel,
        out_shape=jax.ShapeDtypeStruct((width, width), jnp.float32),
        in_specs=[pl.BlockSpec(memory_space=pltpu.VMEM)] * 2,
        out_specs=pl.BlockSpec(memory_space=pltpu.VMEM),
        compiler_params=pltpu.CompilerParams(vmem_limit_bytes=32 * 2**20),
    )(counts, held)


def swap(value, axis, apart):
    pairs = [(source, source ^ apart) for source in range(lax.axis_size(axis))]
    return lax.ppermute(value, axis, pairs)


def scatter_sum(value, axis):
    upper = lax.axis_index(axis) & 1
    half = value.shape[0] // 2
    keep = lax.dynamic_slice_in_dim(value, upper * half, half)
    give = lax.dynamic_slice_in_dim(value, (1 - upper) * half, half)
    return keep + swap(give, axis, 1)


def gather_halves(value, axis):
    rows, width = value.shape
    blank = jnp.zeros((2 * rows, width), jnp.float32)
    at = (lax.axis_index(axis) & 1) * rows
    value = lax.dynamic_update_slice_in_dim(blank, value, at, 0)
    return value, swap(value, axis, 1)


def landing(block, rows_here, most):
    owners = block // rows_here
    order = jnp.arange(block.shape[0], dtype=jnp.int32)
    earlier = (owners[:, None] == owners[None, :]) & (order[None, :] < order[:, None])
    return owners * most + jnp.sum(earlier.astype(jnp.int32), axis=1)


def on_device(panel, flips, picks):
    rows_here, width = panel.shape
    devices = lax.axis_size("narrow") * lax.axis_size("wide")
    scale = 1.0 / float(rows_here * devices) ** 0.5
    me = lax.axis_index(AXES)
    per = picks.shape[0] // devices
    most = -(-per // devices)

    local = local_transform(panel, flips, scale)
    local = local.reshape(devices, rows_here // devices, width)
    wanted = send_rows(picks, [me], rows_here, devices, most)
    spots = landing(lax.dynamic_slice(picks, (me * per,), (per,)), rows_here, most)
    slots = jnp.arange(devices * most, dtype=jnp.int32)
    order = (spots[:, None] == slots[None, :]).astype(jnp.float32)
    counts = count_picks(picks, me, rows_here, devices)
    slices = lax.all_to_all(local, AXES, 0, 0, tiled=True)
    slices, wanted, order, counts = lax.optimization_barrier((slices, wanted, order, counts))
    slices = device_sums(slices)
    mixed = lax.all_to_all(slices, AXES, 0, 0, tiled=True)
    gram = gram_part(counts, slices)
    gram = scatter_sum(gram, "narrow")
    for axis, low in (("narrow", 2), ("wide", 1)):
        while low < lax.axis_size(axis):
            gram = gram + swap(gram, axis, low)
            low *= 2
    mixed, gram = lax.optimization_barrier((mixed, gram))
    mixed = mixed.reshape(rows_here, width)
    chosen = jnp.take(mixed, wanted, axis=0, mode="clip")
    landed = lax.all_to_all(chosen.reshape(devices, most, width), AXES, 0, 0, tiled=True)
    gram, other = gather_halves(gram, "narrow")
    mixed, other = lax.optimization_barrier((mixed, other))
    mixed = store(mixed)
    gram = (gram + other) / float(picks.shape[0])
    landed, mixed, gram = lax.optimization_barrier((landed, mixed, gram))
    landed = landed.reshape(devices * most, width)
    sketch = jnp.dot(order, landed, precision=lax.Precision.HIGHEST)
    return (mixed, sketch, gram)


def solution(mesh):
    in_specs = (P(AXES, None), P(AXES), P())
    out_specs = (P(AXES, None), P(AXES, None), P())
    return jax.shard_map(
        on_device, mesh=mesh, in_specs=in_specs, out_specs=out_specs, check_vma=False
    )
```

```python
import functools

import jax
import jax.numpy as jnp
from jax import lax
from jax.experimental import pallas as pl
from jax.experimental.pallas import tpu as pltpu
from jax.sharding import PartitionSpec as P

BLOCK = 256
AXES = ("narrow", "wide")


def signs(order):
    rows = lax.broadcasted_iota(jnp.int32, (order, order), 0)
    both = rows & lax.broadcasted_iota(jnp.int32, (order, order), 1)
    parity = jnp.zeros((order, order), jnp.int32)
    for level in range(order.bit_length() - 1):
        parity = parity ^ (both >> level & 1)
    return (1 - 2 * parity).astype(jnp.float32)


def halves(value):
    high = value.astype(jnp.bfloat16)
    return high, (value - high.astype(jnp.float32)).astype(jnp.bfloat16)


def local_kernel(scale, flips_ref, panel_ref, out_ref, flags, held, arrived, sent):
    blocks, _, width = panel_ref.shape
    per = BLOCK // flips_ref.shape[1]
    share = blocks // 4
    loads = [pltpu.make_async_copy(flips_ref, flags, arrived.at[4])]
    for part in range(4):
        span = pl.ds(part * share, share)
        loads.append(pltpu.make_async_copy(panel_ref.at[span], held.at[span], arrived.at[part]))
    for load in loads:
        load.start()
    base = signs(BLOCK).astype(jnp.bfloat16)
    loads[0].wait()
    for b in range(blocks):
        if b % share == 0:
            loads[1 + b // share].wait()
        row = jnp.concatenate([flags[b * per + i : b * per + i + 1, :] for i in range(per)], axis=1)
        mixer = base * (1 - 2 * row).astype(jnp.float32).astype(jnp.bfloat16)
        parts = jnp.concatenate(halves(held[b]), axis=1)
        out = jnp.dot(mixer, parts, preferred_element_type=jnp.float32)
        held[b] = out[:, :width] + out[:, width:]
    strip = 16
    piece = BLOCK // 4

    def body(step, carry):
        at = pl.multiple_of(step * strip, strip)
        items = [held[b, pl.ds(at, strip), :] for b in range(blocks)]
        apart = 1
        while apart < blocks:
            items = [
                items[b] + items[b ^ apart] if b & apart == 0 else items[b ^ apart] - items[b]
                for b in range(blocks)
            ]
            apart *= 2
        for b in range(blocks):
            held[b, pl.ds(at, strip), :] = items[b] * scale
        return carry

    copies = []
    for part in range(4):
        first = part * piece // strip
        lax.fori_loop(first, first + piece // strip, body, 0)
        span = pl.ds(part * piece, piece)
        copies.append(
            pltpu.make_async_copy(held.at[:, span, :], out_ref.at[:, span, :], sent.at[part])
        )
        copies[-1].start()
    for copy in copies:
        copy.wait()


def local_transform(panel, flips, scale):
    rows, width = panel.shape
    shape = (rows // BLOCK, BLOCK, width)
    return pl.pallas_call(
        functools.partial(local_kernel, scale),
        out_shape=jax.ShapeDtypeStruct(shape, jnp.float32),
        in_specs=[pl.BlockSpec(memory_space=pl.ANY)] * 2,
        out_specs=pl.BlockSpec(memory_space=pl.ANY),
        scratch_shapes=[
            pltpu.VMEM((rows // 128, 128), jnp.int32),
            pltpu.VMEM(shape, jnp.float32),
            pltpu.SemaphoreType.DMA((5,)),
            pltpu.SemaphoreType.DMA((4,)),
        ],
        compiler_params=pltpu.CompilerParams(vmem_limit_bytes=61 * 2**20),
    )(flips.reshape(rows // 128, 128), panel.reshape(shape))


def device_kernel(in_ref, out_ref, held, sent):
    devices, rows, _ = in_ref.shape
    strip = 8
    parts = sent.shape[0]
    share = rows // parts

    def body(step, carry):
        at = pl.multiple_of(step * strip, strip)
        items = [in_ref[d, pl.ds(at, strip), :] for d in range(devices)]
        apart = 1
        while apart < devices:
            items = [
                items[d] + items[d ^ apart] if d & apart == 0 else items[d ^ apart] - items[d]
                for d in range(devices)
            ]
            apart *= 2
        for d in range(devices):
            held[d, pl.ds(at, strip), :] = items[d]
        return carry

    copies = []
    for part in range(parts):
        first = part * share // strip
        lax.fori_loop(first, first + share // strip, body, 0)
        span = pl.ds(part * share, share)
        copies.append(
            pltpu.make_async_copy(held.at[:, span, :], out_ref.at[:, span, :], sent.at[part])
        )
        copies[-1].start()
    for copy in copies:
        copy.wait()


def device_sums(value):
    return pl.pallas_call(
        device_kernel,
        out_shape=jax.ShapeDtypeStruct(value.shape, jnp.float32),
        in_specs=[pl.BlockSpec(memory_space=pltpu.VMEM)],
        out_specs=pl.BlockSpec(memory_space=pl.ANY),
        scratch_shapes=[
            pltpu.VMEM(value.shape, jnp.float32),
            pltpu.SemaphoreType.DMA((min(8, value.shape[1] // 8),)),
        ],
        compiler_params=pltpu.CompilerParams(vmem_limit_bytes=32 * 2**20),
    )(value)


def store_kernel(value_ref, out_ref, sent):
    copy = pltpu.make_async_copy(value_ref, out_ref, sent)
    copy.start()
    copy.wait()


def store(value):
    return pl.pallas_call(
        store_kernel,
        out_shape=jax.ShapeDtypeStruct(value.shape, jnp.float32),
        in_specs=[pl.BlockSpec(memory_space=pltpu.VMEM)],
        out_specs=pl.BlockSpec(memory_space=pl.ANY),
        scratch_shapes=[pltpu.SemaphoreType.DMA],
        compiler_params=pltpu.CompilerParams(vmem_limit_bytes=8 * 2**20),
    )(value)


def index_kernel(rows_here, most, bases_ref, picks_ref, out_ref):
    picks = picks_ref[...]
    devices, per = picks.shape
    before = lax.broadcasted_iota(jnp.int32, (per, per), 0)
    earlier = before < lax.broadcasted_iota(jnp.int32, (per, per), 1)
    earlier = jnp.where(earlier, 1.0, 0.0).astype(jnp.bfloat16)
    for which in range(out_ref.shape[0]):
        offsets = picks - bases_ref[which]
        owned = (offsets >= 0) & (offsets < rows_here)
        ones = jnp.where(owned, 1.0, 0.0).astype(jnp.bfloat16)
        rank = jnp.dot(ones, earlier, preferred_element_type=jnp.float32)
        rank = jnp.where(owned, rank, -1.0)
        marked = (offsets + 1).astype(jnp.float32)
        for slot in range(most):
            hit = jnp.where(rank == float(slot), marked, 0.0)
            row = jnp.sum(hit, axis=1, keepdims=True).astype(jnp.int32) - 1
            out_ref[which, :, slot : slot + 1] = row


def send_rows(picks, owners, rows_here, devices, most):
    bases = jnp.stack(owners) * rows_here
    rows = pl.pallas_call(
        functools.partial(index_kernel, rows_here, most),
        out_shape=jax.ShapeDtypeStruct((len(owners), devices, most), jnp.int32),
        in_specs=[
            pl.BlockSpec(memory_space=pltpu.SMEM),
            pl.BlockSpec(memory_space=pltpu.VMEM),
        ],
        out_specs=pl.BlockSpec(memory_space=pltpu.VMEM),
        compiler_params=pltpu.CompilerParams(vmem_limit_bytes=8 * 2**20),
    )(bases.astype(jnp.int32), picks.reshape(devices, -1))
    return rows.reshape(len(owners) * devices * most)


def count_kernel(rows_here, me_ref, picks_ref, out_ref):
    picks = picks_ref[...]
    rows, devices = out_ref.shape
    owner = picks >> rows_here.bit_length() - 1
    local = picks & rows_here - 1
    held = local >> rows.bit_length() - 1 == me_ref[0]
    place = jnp.where(held, local & rows - 1, -1)
    shape = (devices, picks.shape[1])
    owners = jnp.where(lax.broadcasted_iota(jnp.int32, shape, 0) == owner, 1.0, 0.0)
    shape = (rows, picks.shape[1])
    places = jnp.where(lax.broadcasted_iota(jnp.int32, shape, 0) == place, 1.0, 0.0)
    out_ref[...] = lax.dot_general(
        places.astype(jnp.bfloat16),
        owners.astype(jnp.bfloat16),
        (((1,), (1,)), ((), ())),
        preferred_element_type=jnp.float32,
    )


def count_picks(picks, me, rows_here, devices):
    return pl.pallas_call(
        functools.partial(count_kernel, rows_here),
        out_shape=jax.ShapeDtypeStruct((rows_here // devices, devices), jnp.float32),
        in_specs=[
            pl.BlockSpec(memory_space=pltpu.SMEM),
            pl.BlockSpec(memory_space=pltpu.VMEM),
        ],
        out_specs=pl.BlockSpec(memory_space=pltpu.VMEM),
        compiler_params=pltpu.CompilerParams(vmem_limit_bytes=32 * 2**20),
    )(me.reshape(1).astype(jnp.int32), picks.reshape(1, -1))


def part_kernel(counts_ref, held_ref, out_ref):
    devices, _, width = held_ref.shape
    total = jnp.zeros((width, 2 * width), jnp.float32)
    rest = jnp.zeros((width, width), jnp.float32)
    for d in range(devices):
        rows = held_ref[d]
        high, low = halves(rows)
        weighted, spare = halves(rows * counts_ref[:, d : d + 1])
        over_rows = (((0,), (0,)), ((), ()))
        both = jnp.concatenate([weighted, spare], axis=1)
        total += lax.dot_general(high, both, over_rows, preferred_element_type=jnp.float32)
        rest += lax.dot_general(low, weighted, over_rows, preferred_element_type=jnp.float32)
    out_ref[...] = total[:, :width] + total[:, width:] + rest


def gram_part(counts, held):
    width = held.shape[2]
    return pl.pallas_call(
        part_kernel,
        out_shape=jax.ShapeDtypeStruct((width, width), jnp.float32),
        in_specs=[pl.BlockSpec(memory_space=pltpu.VMEM)] * 2,
        out_specs=pl.BlockSpec(memory_space=pltpu.VMEM),
        compiler_params=pltpu.CompilerParams(vmem_limit_bytes=32 * 2**20),
    )(counts, held)


def swap(value, axis, apart):
    pairs = [(source, source ^ apart) for source in range(lax.axis_size(axis))]
    return lax.ppermute(value, axis, pairs)


def scatter_sum(value, axis):
    upper = lax.axis_index(axis) & 1
    half = value.shape[0] // 2
    keep = lax.dynamic_slice_in_dim(value, upper * half, half)
    give = lax.dynamic_slice_in_dim(value, (1 - upper) * half, half)
    return keep + swap(give, axis, 1)


def gather_halves(value, axis):
    rows, width = value.shape
    blank = jnp.zeros((2 * rows, width), jnp.float32)
    at = (lax.axis_index(axis) & 1) * rows
    value = lax.dynamic_update_slice_in_dim(blank, value, at, 0)
    return value, swap(value, axis, 1)


def order_kernel(order_ref, rows_ref, out_ref):
    width = rows_ref.shape[1]
    rows = rows_ref[...]
    high = rows.astype(jnp.bfloat16)
    middle, low = halves(rows - high.astype(jnp.float32))
    parts = jnp.concatenate([high, middle, low], axis=1)
    out = jnp.dot(order_ref[...], parts, preferred_element_type=jnp.float32)
    out_ref[...] = out[:, :width] + (out[:, width : 2 * width] + out[:, 2 * width :])


def put_in_order(order, rows):
    return pl.pallas_call(
        order_kernel,
        out_shape=jax.ShapeDtypeStruct((order.shape[0], rows.shape[1]), jnp.float32),
        in_specs=[pl.BlockSpec(memory_space=pltpu.VMEM)] * 2,
        out_specs=pl.BlockSpec(memory_space=pltpu.VMEM),
        compiler_params=pltpu.CompilerParams(vmem_limit_bytes=8 * 2**20),
    )(order, rows)


def landing(block, rows_here, most):
    owners = block // rows_here
    order = jnp.arange(block.shape[0], dtype=jnp.int32)
    earlier = (owners[:, None] == owners[None, :]) & (order[None, :] < order[:, None])
    return owners * most + jnp.sum(earlier.astype(jnp.int32), axis=1)


def on_device(panel, flips, picks):
    rows_here, width = panel.shape
    devices = lax.axis_size("narrow") * lax.axis_size("wide")
    scale = 1.0 / float(rows_here * devices) ** 0.5
    me = lax.axis_index(AXES)
    per = picks.shape[0] // devices
    most = -(-per // devices)

    local = local_transform(panel, flips, scale)
    local = local.reshape(devices, rows_here // devices, width)
    wanted = send_rows(picks, [me], rows_here, devices, most)
    spots = landing(lax.dynamic_slice(picks, (me * per,), (per,)), rows_here, most)
    slots = jnp.arange(devices * most, dtype=jnp.int32)
    order = (spots[:, None] == slots[None, :]).astype(jnp.bfloat16)
    counts = count_picks(picks, me, rows_here, devices)
    slices = lax.all_to_all(local, AXES, 0, 0, tiled=True)
    slices, wanted, order, counts = lax.optimization_barrier((slices, wanted, order, counts))
    slices = device_sums(slices)
    mixed = lax.all_to_all(slices, AXES, 0, 0, tiled=True)
    gram = gram_part(counts, slices)
    gram = scatter_sum(gram, "narrow")
    for axis, low in (("narrow", 2), ("wide", 1)):
        while low < lax.axis_size(axis):
            gram = gram + swap(gram, axis, low)
            low *= 2
    mixed, gram = lax.optimization_barrier((mixed, gram))
    mixed = mixed.reshape(rows_here, width)
    chosen = jnp.take(mixed, wanted, axis=0, mode="clip")
    landed = lax.all_to_all(chosen.reshape(devices, most, width), AXES, 0, 0, tiled=True)
    gram, other = gather_halves(gram, "narrow")
    mixed, other = lax.optimization_barrier((mixed, other))
    mixed = store(mixed)
    gram = (gram + other) / float(picks.shape[0])
    landed, mixed, gram = lax.optimization_barrier((landed, mixed, gram))
    landed = landed.reshape(devices * most, width)
    sketch = put_in_order(order, landed)
    return (mixed, sketch, gram)


def solution(mesh):
    in_specs = (P(AXES, None), P(AXES), P())
    out_specs = (P(AXES, None), P(AXES, None), P())
    return jax.shard_map(
        on_device, mesh=mesh, in_specs=in_specs, out_specs=out_specs, check_vma=False
    )
```

```python
import functools

import jax
import jax.numpy as jnp
from jax import lax
from jax.experimental import pallas as pl
from jax.experimental.pallas import tpu as pltpu
from jax.sharding import PartitionSpec as P

BLOCK = 256
AXES = ("narrow", "wide")


def signs(order):
    rows = lax.broadcasted_iota(jnp.int32, (order, order), 0)
    both = rows & lax.broadcasted_iota(jnp.int32, (order, order), 1)
    parity = jnp.zeros((order, order), jnp.int32)
    for level in range(order.bit_length() - 1):
        parity = parity ^ (both >> level & 1)
    return (1 - 2 * parity).astype(jnp.float32)


def halves(value):
    high = value.astype(jnp.bfloat16)
    return high, (value - high.astype(jnp.float32)).astype(jnp.bfloat16)


def local_kernel(scale, flips_ref, panel_ref, out_ref, flags, held, arrived, sent):
    blocks, _, width = panel_ref.shape
    per = BLOCK // flips_ref.shape[1]
    share = blocks // 4
    loads = [pltpu.make_async_copy(flips_ref, flags, arrived.at[4])]
    for part in range(4):
        span = pl.ds(part * share, share)
        loads.append(pltpu.make_async_copy(panel_ref.at[span], held.at[span], arrived.at[part]))
    for load in loads:
        load.start()
    base = signs(BLOCK).astype(jnp.bfloat16)
    loads[0].wait()
    for b in range(blocks):
        if b % share == 0:
            loads[1 + b // share].wait()
        row = jnp.concatenate([flags[b * per + i : b * per + i + 1, :] for i in range(per)], axis=1)
        mixer = base * (1 - 2 * row).astype(jnp.float32).astype(jnp.bfloat16)
        parts = jnp.concatenate(halves(held[b]), axis=1)
        out = jnp.dot(mixer, parts, preferred_element_type=jnp.float32)
        held[b] = out[:, :width] + out[:, width:]
    strip = 16
    piece = BLOCK // 4

    def body(step, carry):
        at = pl.multiple_of(step * strip, strip)
        items = [held[b, pl.ds(at, strip), :] for b in range(blocks)]
        apart = 1
        while apart < blocks:
            items = [
                items[b] + items[b ^ apart] if b & apart == 0 else items[b ^ apart] - items[b]
                for b in range(blocks)
            ]
            apart *= 2
        for b in range(blocks):
            held[b, pl.ds(at, strip), :] = items[b] * scale
        return carry

    copies = []
    for part in range(4):
        first = part * piece // strip
        lax.fori_loop(first, first + piece // strip, body, 0)
        span = pl.ds(part * piece, piece)
        copies.append(
            pltpu.make_async_copy(held.at[:, span, :], out_ref.at[:, span, :], sent.at[part])
        )
        copies[-1].start()
    for copy in copies:
        copy.wait()


def local_transform(panel, flips, scale):
    rows, width = panel.shape
    shape = (rows // BLOCK, BLOCK, width)
    return pl.pallas_call(
        functools.partial(local_kernel, scale),
        out_shape=jax.ShapeDtypeStruct(shape, jnp.float32),
        in_specs=[pl.BlockSpec(memory_space=pl.ANY)] * 2,
        out_specs=pl.BlockSpec(memory_space=pl.ANY),
        scratch_shapes=[
            pltpu.VMEM((rows // 128, 128), jnp.int32),
            pltpu.VMEM(shape, jnp.float32),
            pltpu.SemaphoreType.DMA((5,)),
            pltpu.SemaphoreType.DMA((4,)),
        ],
        compiler_params=pltpu.CompilerParams(vmem_limit_bytes=61 * 2**20),
    )(flips.reshape(rows // 128, 128), panel.reshape(shape))


def device_kernel(in_ref, out_ref, held, sent):
    devices, rows, _ = in_ref.shape
    strip = 8
    parts = sent.shape[0]
    share = rows // parts

    def body(step, carry):
        at = pl.multiple_of(step * strip, strip)
        items = [in_ref[d, pl.ds(at, strip), :] for d in range(devices)]
        apart = 1
        while apart < devices:
            items = [
                items[d] + items[d ^ apart] if d & apart == 0 else items[d ^ apart] - items[d]
                for d in range(devices)
            ]
            apart *= 2
        for d in range(devices):
            held[d, pl.ds(at, strip), :] = items[d]
        return carry

    copies = []
    for part in range(parts):
        first = part * share // strip
        lax.fori_loop(first, first + share // strip, body, 0)
        span = pl.ds(part * share, share)
        copies.append(
            pltpu.make_async_copy(held.at[:, span, :], out_ref.at[:, span, :], sent.at[part])
        )
        copies[-1].start()
    for copy in copies:
        copy.wait()


def device_sums(value):
    return pl.pallas_call(
        device_kernel,
        out_shape=jax.ShapeDtypeStruct(value.shape, jnp.float32),
        in_specs=[pl.BlockSpec(memory_space=pltpu.VMEM)],
        out_specs=pl.BlockSpec(memory_space=pl.ANY),
        scratch_shapes=[
            pltpu.VMEM(value.shape, jnp.float32),
            pltpu.SemaphoreType.DMA((min(8, value.shape[1] // 8),)),
        ],
        compiler_params=pltpu.CompilerParams(vmem_limit_bytes=32 * 2**20),
    )(value)


def pick_kernel(wanted_ref, mixed_ref, out_ref):
    def body(step, carry):
        at = step * 8
        for k in range(8):
            row = mixed_ref[pl.ds(wanted_ref[at + k], 1), :]
            out_ref[pl.ds(at + k, 1), :] = row
        return carry

    lax.fori_loop(0, out_ref.shape[0] // 8, body, 0)


def pick_rows(wanted, mixed):
    return pl.pallas_call(
        pick_kernel,
        out_shape=jax.ShapeDtypeStruct((wanted.shape[0], mixed.shape[1]), jnp.float32),
        in_specs=[
            pl.BlockSpec(memory_space=pltpu.SMEM),
            pl.BlockSpec(memory_space=pltpu.VMEM),
        ],
        out_specs=pl.BlockSpec(memory_space=pltpu.VMEM),
        compiler_params=pltpu.CompilerParams(vmem_limit_bytes=8 * 2**20),
    )(wanted, mixed)


def store_kernel(value_ref, out_ref, sent):
    copy = pltpu.make_async_copy(value_ref, out_ref, sent)
    copy.start()
    copy.wait()


def store(value):
    return pl.pallas_call(
        store_kernel,
        out_shape=jax.ShapeDtypeStruct(value.shape, jnp.float32),
        in_specs=[pl.BlockSpec(memory_space=pltpu.VMEM)],
        out_specs=pl.BlockSpec(memory_space=pl.ANY),
        scratch_shapes=[pltpu.SemaphoreType.DMA],
        compiler_params=pltpu.CompilerParams(vmem_limit_bytes=8 * 2**20),
    )(value)


def index_kernel(rows_here, most, bases_ref, picks_ref, out_ref):
    picks = picks_ref[...]
    devices, per = picks.shape
    before = lax.broadcasted_iota(jnp.int32, (per, per), 0)
    earlier = before < lax.broadcasted_iota(jnp.int32, (per, per), 1)
    earlier = jnp.where(earlier, 1.0, 0.0).astype(jnp.bfloat16)
    for which in range(out_ref.shape[0]):
        offsets = picks - bases_ref[which]
        owned = (offsets >= 0) & (offsets < rows_here)
        ones = jnp.where(owned, 1.0, 0.0).astype(jnp.bfloat16)
        rank = jnp.dot(ones, earlier, preferred_element_type=jnp.float32)
        rank = jnp.where(owned, rank, -1.0)
        marked = (offsets + 1).astype(jnp.float32)
        for slot in range(most):
            hit = jnp.where(rank == float(slot), marked, 0.0)
            row = jnp.sum(hit, axis=1, keepdims=True).astype(jnp.int32) - 1
            out_ref[which, :, slot : slot + 1] = row


def send_rows(picks, owners, rows_here, devices, most):
    bases = jnp.stack(owners) * rows_here
    rows = pl.pallas_call(
        functools.partial(index_kernel, rows_here, most),
        out_shape=jax.ShapeDtypeStruct((len(owners), devices, most), jnp.int32),
        in_specs=[
            pl.BlockSpec(memory_space=pltpu.SMEM),
            pl.BlockSpec(memory_space=pltpu.VMEM),
        ],
        out_specs=pl.BlockSpec(memory_space=pltpu.VMEM),
        compiler_params=pltpu.CompilerParams(vmem_limit_bytes=8 * 2**20),
    )(bases.astype(jnp.int32), picks.reshape(devices, -1))
    return rows.reshape(len(owners) * devices * most)


def count_kernel(rows_here, me_ref, picks_ref, out_ref):
    picks = picks_ref[...]
    rows, devices = out_ref.shape
    owner = picks >> rows_here.bit_length() - 1
    local = picks & rows_here - 1
    held = local >> rows.bit_length() - 1 == me_ref[0]
    place = jnp.where(held, local & rows - 1, -1)
    shape = (devices, picks.shape[1])
    owners = jnp.where(lax.broadcasted_iota(jnp.int32, shape, 0) == owner, 1.0, 0.0)
    shape = (rows, picks.shape[1])
    places = jnp.where(lax.broadcasted_iota(jnp.int32, shape, 0) == place, 1.0, 0.0)
    out_ref[...] = lax.dot_general(
        places.astype(jnp.bfloat16),
        owners.astype(jnp.bfloat16),
        (((1,), (1,)), ((), ())),
        preferred_element_type=jnp.float32,
    )


def count_picks(picks, me, rows_here, devices):
    return pl.pallas_call(
        functools.partial(count_kernel, rows_here),
        out_shape=jax.ShapeDtypeStruct((rows_here // devices, devices), jnp.float32),
        in_specs=[
            pl.BlockSpec(memory_space=pltpu.SMEM),
            pl.BlockSpec(memory_space=pltpu.VMEM),
        ],
        out_specs=pl.BlockSpec(memory_space=pltpu.VMEM),
        compiler_params=pltpu.CompilerParams(vmem_limit_bytes=32 * 2**20),
    )(me.reshape(1).astype(jnp.int32), picks.reshape(1, -1))


def part_kernel(counts_ref, held_ref, out_ref):
    devices, _, width = held_ref.shape
    total = jnp.zeros((width, 2 * width), jnp.float32)
    rest = jnp.zeros((width, width), jnp.float32)
    for d in range(devices):
        rows = held_ref[d]
        high, low = halves(rows)
        weighted, spare = halves(rows * counts_ref[:, d : d + 1])
        over_rows = (((0,), (0,)), ((), ()))
        both = jnp.concatenate([weighted, spare], axis=1)
        total += lax.dot_general(high, both, over_rows, preferred_element_type=jnp.float32)
        rest += lax.dot_general(low, weighted, over_rows, preferred_element_type=jnp.float32)
    out_ref[...] = total[:, :width] + total[:, width:] + rest


def gram_part(counts, held):
    width = held.shape[2]
    return pl.pallas_call(
        part_kernel,
        out_shape=jax.ShapeDtypeStruct((width, width), jnp.float32),
        in_specs=[pl.BlockSpec(memory_space=pltpu.VMEM)] * 2,
        out_specs=pl.BlockSpec(memory_space=pltpu.VMEM),
        compiler_params=pltpu.CompilerParams(vmem_limit_bytes=32 * 2**20),
    )(counts, held)


def swap(value, axis, apart):
    pairs = [(source, source ^ apart) for source in range(lax.axis_size(axis))]
    return lax.ppermute(value, axis, pairs)


def scatter_sum(value, axis):
    upper = lax.axis_index(axis) & 1
    half = value.shape[0] // 2
    keep = lax.dynamic_slice_in_dim(value, upper * half, half)
    give = lax.dynamic_slice_in_dim(value, (1 - upper) * half, half)
    return keep + swap(give, axis, 1)


def gather_halves(value, axis):
    rows, width = value.shape
    blank = jnp.zeros((2 * rows, width), jnp.float32)
    at = (lax.axis_index(axis) & 1) * rows
    value = lax.dynamic_update_slice_in_dim(blank, value, at, 0)
    return value, swap(value, axis, 1)


def order_kernel(order_ref, rows_ref, out_ref):
    width = rows_ref.shape[1]
    rows = rows_ref[...]
    high = rows.astype(jnp.bfloat16)
    middle, low = halves(rows - high.astype(jnp.float32))
    parts = jnp.concatenate([high, middle, low], axis=1)
    out = jnp.dot(order_ref[...], parts, preferred_element_type=jnp.float32)
    out_ref[...] = out[:, :width] + (out[:, width : 2 * width] + out[:, 2 * width :])


def put_in_order(order, rows):
    return pl.pallas_call(
        order_kernel,
        out_shape=jax.ShapeDtypeStruct((order.shape[0], rows.shape[1]), jnp.float32),
        in_specs=[pl.BlockSpec(memory_space=pltpu.VMEM)] * 2,
        out_specs=pl.BlockSpec(memory_space=pltpu.VMEM),
        compiler_params=pltpu.CompilerParams(vmem_limit_bytes=8 * 2**20),
    )(order, rows)


def landing(block, rows_here, most):
    owners = block // rows_here
    order = jnp.arange(block.shape[0], dtype=jnp.int32)
    earlier = (owners[:, None] == owners[None, :]) & (order[None, :] < order[:, None])
    return owners * most + jnp.sum(earlier.astype(jnp.int32), axis=1)


def on_device(panel, flips, picks):
    rows_here, width = panel.shape
    devices = lax.axis_size("narrow") * lax.axis_size("wide")
    scale = 1.0 / float(rows_here * devices) ** 0.5
    me = lax.axis_index(AXES)
    per = picks.shape[0] // devices
    most = -(-per // devices)

    local = local_transform(panel, flips, scale)
    local = local.reshape(devices, rows_here // devices, width)
    wanted = send_rows(picks, [me], rows_here, devices, most)
    wanted = jnp.maximum(wanted, 0)
    spots = landing(lax.dynamic_slice(picks, (me * per,), (per,)), rows_here, most)
    slots = jnp.arange(devices * most, dtype=jnp.int32)
    order = (spots[:, None] == slots[None, :]).astype(jnp.bfloat16)
    counts = count_picks(picks, me, rows_here, devices)
    slices = lax.all_to_all(local, AXES, 0, 0, tiled=True)
    slices, wanted, order, counts = lax.optimization_barrier((slices, wanted, order, counts))
    slices = device_sums(slices)
    mixed = lax.all_to_all(slices, AXES, 0, 0, tiled=True)
    gram = gram_part(counts, slices)
    gram = scatter_sum(gram, "narrow")
    for axis, low in (("narrow", 2), ("wide", 1)):
        while low < lax.axis_size(axis):
            gram = gram + swap(gram, axis, low)
            low *= 2
    mixed, gram = lax.optimization_barrier((mixed, gram))
    mixed = mixed.reshape(rows_here, width)
    chosen = pick_rows(wanted, mixed)
    landed = lax.all_to_all(chosen.reshape(devices, most, width), AXES, 0, 0, tiled=True)
    gram, other = gather_halves(gram, "narrow")
    mixed, other = lax.optimization_barrier((mixed, other))
    mixed = store(mixed)
    gram = (gram + other) / float(picks.shape[0])
    landed, mixed, gram = lax.optimization_barrier((landed, mixed, gram))
    landed = landed.reshape(devices * most, width)
    sketch = put_in_order(order, landed)
    return (mixed, sketch, gram)


def solution(mesh):
    in_specs = (P(AXES, None), P(AXES), P())
    out_specs = (P(AXES, None), P(AXES, None), P())
    return jax.shard_map(
        on_device, mesh=mesh, in_specs=in_specs, out_specs=out_specs, check_vma=False
    )
```

```python
import functools

import jax
import jax.numpy as jnp
from jax import lax
from jax.experimental import pallas as pl
from jax.experimental.pallas import tpu as pltpu
from jax.sharding import PartitionSpec as P

BLOCK = 256
AXES = ("narrow", "wide")


def signs(order):
    rows = lax.broadcasted_iota(jnp.int32, (order, order), 0)
    both = rows & lax.broadcasted_iota(jnp.int32, (order, order), 1)
    parity = jnp.zeros((order, order), jnp.int32)
    for level in range(order.bit_length() - 1):
        parity = parity ^ (both >> level & 1)
    return (1 - 2 * parity).astype(jnp.float32)


def halves(value):
    high = value.astype(jnp.bfloat16)
    return high, (value - high.astype(jnp.float32)).astype(jnp.bfloat16)


def local_kernel(scale, flips_ref, panel_ref, out_ref, flags, held, arrived, sent):
    blocks, _, width = panel_ref.shape
    per = BLOCK // flips_ref.shape[1]
    share = blocks // 2
    loads = [pltpu.make_async_copy(flips_ref, flags, arrived.at[2])]
    for part in range(2):
        span = pl.ds(part * share, share)
        loads.append(pltpu.make_async_copy(panel_ref.at[span], held.at[span], arrived.at[part]))
    for load in loads:
        load.start()
    base = signs(BLOCK).astype(jnp.bfloat16)
    loads[0].wait()
    for b in range(blocks):
        if b % share == 0:
            loads[1 + b // share].wait()
        row = jnp.concatenate([flags[b * per + i : b * per + i + 1, :] for i in range(per)], axis=1)
        mixer = base * (1 - 2 * row).astype(jnp.float32).astype(jnp.bfloat16)
        parts = jnp.concatenate(halves(held[b]), axis=1)
        out = jnp.dot(mixer, parts, preferred_element_type=jnp.float32)
        held[b] = out[:, :width] + out[:, width:]
    strip = 16
    piece = BLOCK // 2

    def body(step, carry):
        at = pl.multiple_of(step * strip, strip)
        items = [held[b, pl.ds(at, strip), :] for b in range(blocks)]
        apart = 1
        while apart < blocks:
            items = [
                items[b] + items[b ^ apart] if b & apart == 0 else items[b ^ apart] - items[b]
                for b in range(blocks)
            ]
            apart *= 2
        for b in range(blocks):
            held[b, pl.ds(at, strip), :] = items[b] * scale
        return carry

    copies = []
    for part in range(2):
        first = part * piece // strip
        lax.fori_loop(first, first + piece // strip, body, 0)
        span = pl.ds(part * piece, piece)
        copies.append(
            pltpu.make_async_copy(held.at[:, span, :], out_ref.at[:, span, :], sent.at[part])
        )
        copies[-1].start()
    for copy in copies:
        copy.wait()


def local_transform(panel, flips, scale):
    rows, width = panel.shape
    shape = (rows // BLOCK, BLOCK, width)
    return pl.pallas_call(
        functools.partial(local_kernel, scale),
        out_shape=jax.ShapeDtypeStruct(shape, jnp.float32),
        in_specs=[pl.BlockSpec(memory_space=pl.ANY)] * 2,
        out_specs=pl.BlockSpec(memory_space=pl.ANY),
        scratch_shapes=[
            pltpu.VMEM((rows // 128, 128), jnp.int32),
            pltpu.VMEM(shape, jnp.float32),
            pltpu.SemaphoreType.DMA((3,)),
            pltpu.SemaphoreType.DMA((2,)),
        ],
        compiler_params=pltpu.CompilerParams(vmem_limit_bytes=61 * 2**20),
    )(flips.reshape(rows // 128, 128), panel.reshape(shape))


def device_kernel(in_ref, out_ref, held, sent):
    devices, rows, _ = in_ref.shape
    strip = 8
    parts = sent.shape[0]
    share = rows // parts

    def body(step, carry):
        at = pl.multiple_of(step * strip, strip)
        items = [in_ref[d, pl.ds(at, strip), :] for d in range(devices)]
        apart = 1
        while apart < devices:
            items = [
                items[d] + items[d ^ apart] if d & apart == 0 else items[d ^ apart] - items[d]
                for d in range(devices)
            ]
            apart *= 2
        for d in range(devices):
            held[d, pl.ds(at, strip), :] = items[d]
        return carry

    copies = []
    for part in range(parts):
        first = part * share // strip
        lax.fori_loop(first, first + share // strip, body, 0)
        span = pl.ds(part * share, share)
        copies.append(
            pltpu.make_async_copy(held.at[:, span, :], out_ref.at[:, span, :], sent.at[part])
        )
        copies[-1].start()
    for copy in copies:
        copy.wait()


def device_sums(value):
    return pl.pallas_call(
        device_kernel,
        out_shape=jax.ShapeDtypeStruct(value.shape, jnp.float32),
        in_specs=[pl.BlockSpec(memory_space=pltpu.VMEM)],
        out_specs=pl.BlockSpec(memory_space=pl.ANY),
        scratch_shapes=[
            pltpu.VMEM(value.shape, jnp.float32),
            pltpu.SemaphoreType.DMA((min(8, value.shape[1] // 8),)),
        ],
        compiler_params=pltpu.CompilerParams(vmem_limit_bytes=32 * 2**20),
    )(value)


def store_kernel(value_ref, out_ref, sent):
    copy = pltpu.make_async_copy(value_ref, out_ref, sent)
    copy.start()
    copy.wait()


def store(value):
    return pl.pallas_call(
        store_kernel,
        out_shape=jax.ShapeDtypeStruct(value.shape, jnp.float32),
        in_specs=[pl.BlockSpec(memory_space=pltpu.VMEM)],
        out_specs=pl.BlockSpec(memory_space=pl.ANY),
        scratch_shapes=[pltpu.SemaphoreType.DMA],
        compiler_params=pltpu.CompilerParams(vmem_limit_bytes=8 * 2**20),
    )(value)


def index_kernel(rows_here, most, bases_ref, picks_ref, out_ref):
    picks = picks_ref[...]
    devices, per = picks.shape
    before = lax.broadcasted_iota(jnp.int32, (per, per), 0)
    earlier = before < lax.broadcasted_iota(jnp.int32, (per, per), 1)
    earlier = jnp.where(earlier, 1.0, 0.0).astype(jnp.bfloat16)
    for which in range(out_ref.shape[0]):
        offsets = picks - bases_ref[which]
        owned = (offsets >= 0) & (offsets < rows_here)
        ones = jnp.where(owned, 1.0, 0.0).astype(jnp.bfloat16)
        rank = jnp.dot(ones, earlier, preferred_element_type=jnp.float32)
        rank = jnp.where(owned, rank, -1.0)
        marked = (offsets + 1).astype(jnp.float32)
        for slot in range(most):
            hit = jnp.where(rank == float(slot), marked, 0.0)
            row = jnp.sum(hit, axis=1, keepdims=True).astype(jnp.int32) - 1
            out_ref[which, :, slot : slot + 1] = row


def send_rows(picks, owners, rows_here, devices, most):
    bases = jnp.stack(owners) * rows_here
    rows = pl.pallas_call(
        functools.partial(index_kernel, rows_here, most),
        out_shape=jax.ShapeDtypeStruct((len(owners), devices, most), jnp.int32),
        in_specs=[
            pl.BlockSpec(memory_space=pltpu.SMEM),
            pl.BlockSpec(memory_space=pltpu.VMEM),
        ],
        out_specs=pl.BlockSpec(memory_space=pltpu.VMEM),
        compiler_params=pltpu.CompilerParams(vmem_limit_bytes=8 * 2**20),
    )(bases.astype(jnp.int32), picks.reshape(devices, -1))
    return rows.reshape(len(owners) * devices * most)


def count_kernel(rows_here, me_ref, picks_ref, out_ref):
    picks = picks_ref[...]
    rows, devices = out_ref.shape
    owner = picks >> rows_here.bit_length() - 1
    local = picks & rows_here - 1
    held = local >> rows.bit_length() - 1 == me_ref[0]
    place = jnp.where(held, local & rows - 1, -1)
    shape = (devices, picks.shape[1])
    owners = jnp.where(lax.broadcasted_iota(jnp.int32, shape, 0) == owner, 1.0, 0.0)
    shape = (rows, picks.shape[1])
    places = jnp.where(lax.broadcasted_iota(jnp.int32, shape, 0) == place, 1.0, 0.0)
    out_ref[...] = lax.dot_general(
        places.astype(jnp.bfloat16),
        owners.astype(jnp.bfloat16),
        (((1,), (1,)), ((), ())),
        preferred_element_type=jnp.float32,
    )


def count_picks(picks, me, rows_here, devices):
    return pl.pallas_call(
        functools.partial(count_kernel, rows_here),
        out_shape=jax.ShapeDtypeStruct((rows_here // devices, devices), jnp.float32),
        in_specs=[
            pl.BlockSpec(memory_space=pltpu.SMEM),
            pl.BlockSpec(memory_space=pltpu.VMEM),
        ],
        out_specs=pl.BlockSpec(memory_space=pltpu.VMEM),
        compiler_params=pltpu.CompilerParams(vmem_limit_bytes=32 * 2**20),
    )(me.reshape(1).astype(jnp.int32), picks.reshape(1, -1))


def part_kernel(counts_ref, held_ref, out_ref):
    devices, _, width = held_ref.shape
    total = jnp.zeros((width, 2 * width), jnp.float32)
    rest = jnp.zeros((width, width), jnp.float32)
    for d in range(devices):
        rows = held_ref[d]
        high, low = halves(rows)
        weighted, spare = halves(rows * counts_ref[:, d : d + 1])
        over_rows = (((0,), (0,)), ((), ()))
        both = jnp.concatenate([weighted, spare], axis=1)
        total += lax.dot_general(high, both, over_rows, preferred_element_type=jnp.float32)
        rest += lax.dot_general(low, weighted, over_rows, preferred_element_type=jnp.float32)
    out_ref[...] = total[:, :width] + total[:, width:] + rest


def gram_part(counts, held):
    width = held.shape[2]
    return pl.pallas_call(
        part_kernel,
        out_shape=jax.ShapeDtypeStruct((width, width), jnp.float32),
        in_specs=[pl.BlockSpec(memory_space=pltpu.VMEM)] * 2,
        out_specs=pl.BlockSpec(memory_space=pltpu.VMEM),
        compiler_params=pltpu.CompilerParams(vmem_limit_bytes=32 * 2**20),
    )(counts, held)


def swap(value, axis, apart):
    pairs = [(source, source ^ apart) for source in range(lax.axis_size(axis))]
    return lax.ppermute(value, axis, pairs)


def scatter_sum(value, axis):
    upper = lax.axis_index(axis) & 1
    half = value.shape[0] // 2
    keep = lax.dynamic_slice_in_dim(value, upper * half, half)
    give = lax.dynamic_slice_in_dim(value, (1 - upper) * half, half)
    return keep + swap(give, axis, 1)


def gather_halves(value, axis):
    rows, width = value.shape
    blank = jnp.zeros((2 * rows, width), jnp.float32)
    at = (lax.axis_index(axis) & 1) * rows
    value = lax.dynamic_update_slice_in_dim(blank, value, at, 0)
    return value, swap(value, axis, 1)


def order_kernel(order_ref, rows_ref, out_ref):
    width = rows_ref.shape[1]
    rows = rows_ref[...]
    high = rows.astype(jnp.bfloat16)
    middle, low = halves(rows - high.astype(jnp.float32))
    parts = jnp.concatenate([high, middle, low], axis=1)
    out = jnp.dot(order_ref[...], parts, preferred_element_type=jnp.float32)
    out_ref[...] = out[:, :width] + (out[:, width : 2 * width] + out[:, 2 * width :])


def put_in_order(order, rows):
    return pl.pallas_call(
        order_kernel,
        out_shape=jax.ShapeDtypeStruct((order.shape[0], rows.shape[1]), jnp.float32),
        in_specs=[pl.BlockSpec(memory_space=pltpu.VMEM)] * 2,
        out_specs=pl.BlockSpec(memory_space=pltpu.VMEM),
        compiler_params=pltpu.CompilerParams(vmem_limit_bytes=8 * 2**20),
    )(order, rows)


def landing(block, rows_here, most):
    owners = block // rows_here
    order = jnp.arange(block.shape[0], dtype=jnp.int32)
    earlier = (owners[:, None] == owners[None, :]) & (order[None, :] < order[:, None])
    return owners * most + jnp.sum(earlier.astype(jnp.int32), axis=1)


def on_device(panel, flips, picks):
    rows_here, width = panel.shape
    devices = lax.axis_size("narrow") * lax.axis_size("wide")
    scale = 1.0 / float(rows_here * devices) ** 0.5
    me = lax.axis_index(AXES)
    per = picks.shape[0] // devices
    most = -(-per // devices)

    local = local_transform(panel, flips, scale)
    local = local.reshape(devices, rows_here // devices, width)
    wanted = send_rows(picks, [me], rows_here, devices, most)
    spots = landing(lax.dynamic_slice(picks, (me * per,), (per,)), rows_here, most)
    slots = jnp.arange(devices * most, dtype=jnp.int32)
    order = (spots[:, None] == slots[None, :]).astype(jnp.bfloat16)
    counts = count_picks(picks, me, rows_here, devices)
    slices = lax.all_to_all(local, AXES, 0, 0, tiled=True)
    slices, wanted, order, counts = lax.optimization_barrier((slices, wanted, order, counts))
    slices = device_sums(slices)
    mixed = lax.all_to_all(slices, AXES, 0, 0, tiled=True)
    gram = gram_part(counts, slices)
    gram = scatter_sum(gram, "narrow")
    for axis, low in (("narrow", 2), ("wide", 1)):
        while low < lax.axis_size(axis):
            gram = gram + swap(gram, axis, low)
            low *= 2
    mixed, gram = lax.optimization_barrier((mixed, gram))
    mixed = mixed.reshape(rows_here, width)
    chosen = jnp.take(mixed, wanted, axis=0, mode="clip")
    landed = lax.all_to_all(chosen.reshape(devices, most, width), AXES, 0, 0, tiled=True)
    gram, other = gather_halves(gram, "narrow")
    mixed, other = lax.optimization_barrier((mixed, other))
    mixed = store(mixed)
    gram = (gram + other) / float(picks.shape[0])
    landed, mixed, gram = lax.optimization_barrier((landed, mixed, gram))
    landed = landed.reshape(devices * most, width)
    sketch = put_in_order(order, landed)
    return (mixed, sketch, gram)


def solution(mesh):
    in_specs = (P(AXES, None), P(AXES), P())
    out_specs = (P(AXES, None), P(AXES, None), P())
    return jax.shard_map(
        on_device, mesh=mesh, in_specs=in_specs, out_specs=out_specs, check_vma=False
    )
```

```python
import functools

import jax
import jax.numpy as jnp
from jax import lax
from jax.experimental import pallas as pl
from jax.experimental.pallas import tpu as pltpu
from jax.sharding import PartitionSpec as P

BLOCK = 256
AXES = ("narrow", "wide")


def signs(order):
    rows = lax.broadcasted_iota(jnp.int32, (order, order), 0)
    both = rows & lax.broadcasted_iota(jnp.int32, (order, order), 1)
    parity = jnp.zeros((order, order), jnp.int32)
    for level in range(order.bit_length() - 1):
        parity = parity ^ (both >> level & 1)
    return (1 - 2 * parity).astype(jnp.float32)


def halves(value):
    high = value.astype(jnp.bfloat16)
    return high, (value - high.astype(jnp.float32)).astype(jnp.bfloat16)


def local_kernel(scale, flips_ref, panel_ref, out_ref, flags, held, arrived, sent):
    blocks, _, width = panel_ref.shape
    per = BLOCK // flips_ref.shape[1]
    share = blocks // 2
    loads = [pltpu.make_async_copy(flips_ref, flags, arrived.at[2])]
    for part in range(2):
        span = pl.ds(part * share, share)
        loads.append(pltpu.make_async_copy(panel_ref.at[span], held.at[span], arrived.at[part]))
    for load in loads:
        load.start()
    base = signs(BLOCK).astype(jnp.bfloat16)
    loads[0].wait()
    for b in range(blocks):
        if b % share == 0:
            loads[1 + b // share].wait()
        row = jnp.concatenate([flags[b * per + i : b * per + i + 1, :] for i in range(per)], axis=1)
        mixer = base * (1 - 2 * row).astype(jnp.float32).astype(jnp.bfloat16)
        parts = jnp.concatenate(halves(held[b]), axis=1)
        out = jnp.dot(mixer, parts, preferred_element_type=jnp.float32)
        held[b] = out[:, :width] + out[:, width:]
    strip = 8
    piece = BLOCK // 2

    def body(step, carry):
        at = pl.multiple_of(step * strip, strip)
        items = [held[b, pl.ds(at, strip), :] for b in range(blocks)]
        apart = 1
        while apart < blocks:
            items = [
                items[b] + items[b ^ apart] if b & apart == 0 else items[b ^ apart] - items[b]
                for b in range(blocks)
            ]
            apart *= 2
        for b in range(blocks):
            held[b, pl.ds(at, strip), :] = items[b] * scale
        return carry

    copies = []
    for part in range(2):
        first = part * piece // strip
        lax.fori_loop(first, first + piece // strip, body, 0)
        span = pl.ds(part * piece, piece)
        copies.append(
            pltpu.make_async_copy(held.at[:, span, :], out_ref.at[:, span, :], sent.at[part])
        )
        copies[-1].start()
    for copy in copies:
        copy.wait()


def local_transform(panel, flips, scale):
    rows, width = panel.shape
    shape = (rows // BLOCK, BLOCK, width)
    return pl.pallas_call(
        functools.partial(local_kernel, scale),
        out_shape=jax.ShapeDtypeStruct(shape, jnp.float32),
        in_specs=[pl.BlockSpec(memory_space=pl.ANY)] * 2,
        out_specs=pl.BlockSpec(memory_space=pl.ANY),
        scratch_shapes=[
            pltpu.VMEM((rows // 128, 128), jnp.int32),
            pltpu.VMEM(shape, jnp.float32),
            pltpu.SemaphoreType.DMA((3,)),
            pltpu.SemaphoreType.DMA((2,)),
        ],
        compiler_params=pltpu.CompilerParams(vmem_limit_bytes=61 * 2**20),
    )(flips.reshape(rows // 128, 128), panel.reshape(shape))


def device_kernel(in_ref, out_ref, held, sent):
    devices, rows, _ = in_ref.shape
    strip = 8
    parts = sent.shape[0]
    share = rows // parts

    def body(step, carry):
        at = pl.multiple_of(step * strip, strip)
        items = [in_ref[d, pl.ds(at, strip), :] for d in range(devices)]
        apart = 1
        while apart < devices:
            items = [
                items[d] + items[d ^ apart] if d & apart == 0 else items[d ^ apart] - items[d]
                for d in range(devices)
            ]
            apart *= 2
        for d in range(devices):
            held[d, pl.ds(at, strip), :] = items[d]
        return carry

    copies = []
    for part in range(parts):
        first = part * share // strip
        lax.fori_loop(first, first + share // strip, body, 0)
        span = pl.ds(part * share, share)
        copies.append(
            pltpu.make_async_copy(held.at[:, span, :], out_ref.at[:, span, :], sent.at[part])
        )
        copies[-1].start()
    for copy in copies:
        copy.wait()


def device_sums(value):
    return pl.pallas_call(
        device_kernel,
        out_shape=jax.ShapeDtypeStruct(value.shape, jnp.float32),
        in_specs=[pl.BlockSpec(memory_space=pltpu.VMEM)],
        out_specs=pl.BlockSpec(memory_space=pl.ANY),
        scratch_shapes=[
            pltpu.VMEM(value.shape, jnp.float32),
            pltpu.SemaphoreType.DMA((min(8, value.shape[1] // 8),)),
        ],
        compiler_params=pltpu.CompilerParams(vmem_limit_bytes=32 * 2**20),
    )(value)


def store_kernel(value_ref, out_ref, sent):
    copy = pltpu.make_async_copy(value_ref, out_ref, sent)
    copy.start()
    copy.wait()


def store(value):
    return pl.pallas_call(
        store_kernel,
        out_shape=jax.ShapeDtypeStruct(value.shape, jnp.float32),
        in_specs=[pl.BlockSpec(memory_space=pltpu.VMEM)],
        out_specs=pl.BlockSpec(memory_space=pl.ANY),
        scratch_shapes=[pltpu.SemaphoreType.DMA],
        compiler_params=pltpu.CompilerParams(vmem_limit_bytes=8 * 2**20),
    )(value)


def index_kernel(rows_here, most, bases_ref, picks_ref, out_ref):
    picks = picks_ref[...]
    devices, per = picks.shape
    before = lax.broadcasted_iota(jnp.int32, (per, per), 0)
    earlier = before < lax.broadcasted_iota(jnp.int32, (per, per), 1)
    earlier = jnp.where(earlier, 1.0, 0.0).astype(jnp.bfloat16)
    for which in range(out_ref.shape[0]):
        offsets = picks - bases_ref[which]
        owned = (offsets >= 0) & (offsets < rows_here)
        ones = jnp.where(owned, 1.0, 0.0).astype(jnp.bfloat16)
        rank = jnp.dot(ones, earlier, preferred_element_type=jnp.float32)
        rank = jnp.where(owned, rank, -1.0)
        marked = (offsets + 1).astype(jnp.float32)
        for slot in range(most):
            hit = jnp.where(rank == float(slot), marked, 0.0)
            row = jnp.sum(hit, axis=1, keepdims=True).astype(jnp.int32) - 1
            out_ref[which, :, slot : slot + 1] = row


def send_rows(picks, owners, rows_here, devices, most):
    bases = jnp.stack(owners) * rows_here
    rows = pl.pallas_call(
        functools.partial(index_kernel, rows_here, most),
        out_shape=jax.ShapeDtypeStruct((len(owners), devices, most), jnp.int32),
        in_specs=[
            pl.BlockSpec(memory_space=pltpu.SMEM),
            pl.BlockSpec(memory_space=pltpu.VMEM),
        ],
        out_specs=pl.BlockSpec(memory_space=pltpu.VMEM),
        compiler_params=pltpu.CompilerParams(vmem_limit_bytes=8 * 2**20),
    )(bases.astype(jnp.int32), picks.reshape(devices, -1))
    return rows.reshape(len(owners) * devices * most)


def count_kernel(rows_here, me_ref, picks_ref, out_ref):
    picks = picks_ref[...]
    rows, devices = out_ref.shape
    owner = picks >> rows_here.bit_length() - 1
    local = picks & rows_here - 1
    held = local >> rows.bit_length() - 1 == me_ref[0]
    place = jnp.where(held, local & rows - 1, -1)
    shape = (devices, picks.shape[1])
    owners = jnp.where(lax.broadcasted_iota(jnp.int32, shape, 0) == owner, 1.0, 0.0)
    shape = (rows, picks.shape[1])
    places = jnp.where(lax.broadcasted_iota(jnp.int32, shape, 0) == place, 1.0, 0.0)
    out_ref[...] = lax.dot_general(
        places.astype(jnp.bfloat16),
        owners.astype(jnp.bfloat16),
        (((1,), (1,)), ((), ())),
        preferred_element_type=jnp.float32,
    )


def count_picks(picks, me, rows_here, devices):
    return pl.pallas_call(
        functools.partial(count_kernel, rows_here),
        out_shape=jax.ShapeDtypeStruct((rows_here // devices, devices), jnp.float32),
        in_specs=[
            pl.BlockSpec(memory_space=pltpu.SMEM),
            pl.BlockSpec(memory_space=pltpu.VMEM),
        ],
        out_specs=pl.BlockSpec(memory_space=pltpu.VMEM),
        compiler_params=pltpu.CompilerParams(vmem_limit_bytes=32 * 2**20),
    )(me.reshape(1).astype(jnp.int32), picks.reshape(1, -1))


def part_kernel(counts_ref, held_ref, out_ref):
    devices, _, width = held_ref.shape
    total = jnp.zeros((width, 2 * width), jnp.float32)
    rest = jnp.zeros((width, width), jnp.float32)
    for d in range(devices):
        rows = held_ref[d]
        high, low = halves(rows)
        weighted, spare = halves(rows * counts_ref[:, d : d + 1])
        over_rows = (((0,), (0,)), ((), ()))
        both = jnp.concatenate([weighted, spare], axis=1)
        total += lax.dot_general(high, both, over_rows, preferred_element_type=jnp.float32)
        rest += lax.dot_general(low, weighted, over_rows, preferred_element_type=jnp.float32)
    out_ref[...] = total[:, :width] + total[:, width:] + rest


def gram_part(counts, held):
    width = held.shape[2]
    return pl.pallas_call(
        part_kernel,
        out_shape=jax.ShapeDtypeStruct((width, width), jnp.float32),
        in_specs=[pl.BlockSpec(memory_space=pltpu.VMEM)] * 2,
        out_specs=pl.BlockSpec(memory_space=pltpu.VMEM),
        compiler_params=pltpu.CompilerParams(vmem_limit_bytes=32 * 2**20),
    )(counts, held)


def swap(value, axis, apart):
    pairs = [(source, source ^ apart) for source in range(lax.axis_size(axis))]
    return lax.ppermute(value, axis, pairs)


def scatter_sum(value, axis):
    upper = lax.axis_index(axis) & 1
    half = value.shape[0] // 2
    keep = lax.dynamic_slice_in_dim(value, upper * half, half)
    give = lax.dynamic_slice_in_dim(value, (1 - upper) * half, half)
    return keep + swap(give, axis, 1)


def gather_halves(value, axis):
    rows, width = value.shape
    blank = jnp.zeros((2 * rows, width), jnp.float32)
    at = (lax.axis_index(axis) & 1) * rows
    value = lax.dynamic_update_slice_in_dim(blank, value, at, 0)
    return value, swap(value, axis, 1)


def order_kernel(order_ref, rows_ref, out_ref):
    width = rows_ref.shape[1]
    rows = rows_ref[...]
    high = rows.astype(jnp.bfloat16)
    middle, low = halves(rows - high.astype(jnp.float32))
    parts = jnp.concatenate([high, middle, low], axis=1)
    out = jnp.dot(order_ref[...], parts, preferred_element_type=jnp.float32)
    out_ref[...] = out[:, :width] + (out[:, width : 2 * width] + out[:, 2 * width :])


def put_in_order(order, rows):
    return pl.pallas_call(
        order_kernel,
        out_shape=jax.ShapeDtypeStruct((order.shape[0], rows.shape[1]), jnp.float32),
        in_specs=[pl.BlockSpec(memory_space=pltpu.VMEM)] * 2,
        out_specs=pl.BlockSpec(memory_space=pltpu.VMEM),
        compiler_params=pltpu.CompilerParams(vmem_limit_bytes=8 * 2**20),
    )(order, rows)


def landing(block, rows_here, most):
    owners = block // rows_here
    order = jnp.arange(block.shape[0], dtype=jnp.int32)
    earlier = (owners[:, None] == owners[None, :]) & (order[None, :] < order[:, None])
    return owners * most + jnp.sum(earlier.astype(jnp.int32), axis=1)


def on_device(panel, flips, picks):
    rows_here, width = panel.shape
    devices = lax.axis_size("narrow") * lax.axis_size("wide")
    scale = 1.0 / float(rows_here * devices) ** 0.5
    me = lax.axis_index(AXES)
    per = picks.shape[0] // devices
    most = -(-per // devices)

    local = local_transform(panel, flips, scale)
    local = local.reshape(devices, rows_here // devices, width)
    wanted = send_rows(picks, [me], rows_here, devices, most)
    spots = landing(lax.dynamic_slice(picks, (me * per,), (per,)), rows_here, most)
    slots = jnp.arange(devices * most, dtype=jnp.int32)
    order = (spots[:, None] == slots[None, :]).astype(jnp.bfloat16)
    counts = count_picks(picks, me, rows_here, devices)
    slices = lax.all_to_all(local, AXES, 0, 0, tiled=True)
    slices, wanted, order, counts = lax.optimization_barrier((slices, wanted, order, counts))
    slices = device_sums(slices)
    mixed = lax.all_to_all(slices, AXES, 0, 0, tiled=True)
    gram = gram_part(counts, slices)
    gram = scatter_sum(gram, "narrow")
    for axis, low in (("narrow", 2), ("wide", 1)):
        while low < lax.axis_size(axis):
            gram = gram + swap(gram, axis, low)
            low *= 2
    mixed, gram = lax.optimization_barrier((mixed, gram))
    mixed = mixed.reshape(rows_here, width)
    chosen = jnp.take(mixed, wanted, axis=0, mode="clip")
    landed = lax.all_to_all(chosen.reshape(devices, most, width), AXES, 0, 0, tiled=True)
    gram, other = gather_halves(gram, "narrow")
    mixed, other = lax.optimization_barrier((mixed, other))
    mixed = store(mixed)
    gram = (gram + other) / float(picks.shape[0])
    landed, mixed, gram = lax.optimization_barrier((landed, mixed, gram))
    landed = landed.reshape(devices * most, width)
    sketch = put_in_order(order, landed)
    return (mixed, sketch, gram)


def solution(mesh):
    in_specs = (P(AXES, None), P(AXES), P())
    out_specs = (P(AXES, None), P(AXES, None), P())
    return jax.shard_map(
        on_device, mesh=mesh, in_specs=in_specs, out_specs=out_specs, check_vma=False
    )
```

```python
import functools

import jax
import jax.numpy as jnp
from jax import lax
from jax.experimental import pallas as pl
from jax.experimental.pallas import tpu as pltpu
from jax.sharding import PartitionSpec as P

BLOCK = 256
AXES = ("narrow", "wide")


def signs(order):
    rows = lax.broadcasted_iota(jnp.int32, (order, order), 0)
    both = rows & lax.broadcasted_iota(jnp.int32, (order, order), 1)
    parity = jnp.zeros((order, order), jnp.int32)
    for level in range(order.bit_length() - 1):
        parity = parity ^ (both >> level & 1)
    return (1 - 2 * parity).astype(jnp.float32)


def halves(value):
    high = value.astype(jnp.bfloat16)
    return high, (value - high.astype(jnp.float32)).astype(jnp.bfloat16)


def local_kernel(scale, flips_ref, panel_ref, out_ref, flags, held, arrived, sent):
    blocks, _, width = panel_ref.shape
    per = BLOCK // flips_ref.shape[1]
    share = blocks // 4
    loads = [pltpu.make_async_copy(flips_ref, flags, arrived.at[4])]
    for part in range(4):
        span = pl.ds(part * share, share)
        loads.append(pltpu.make_async_copy(panel_ref.at[span], held.at[span], arrived.at[part]))
    for load in loads:
        load.start()
    base = signs(BLOCK).astype(jnp.bfloat16)
    loads[0].wait()
    for b in range(blocks):
        if b % share == 0:
            loads[1 + b // share].wait()
        row = jnp.concatenate([flags[b * per + i : b * per + i + 1, :] for i in range(per)], axis=1)
        mixer = base * (1 - 2 * row).astype(jnp.float32).astype(jnp.bfloat16)
        parts = jnp.concatenate(halves(held[b]), axis=1)
        out = jnp.dot(mixer, parts, preferred_element_type=jnp.float32)
        held[b] = out[:, :width] + out[:, width:]
    strip = 16
    piece = BLOCK // 2

    def body(step, carry):
        at = pl.multiple_of(step * strip, strip)
        items = [held[b, pl.ds(at, strip), :] for b in range(blocks)]
        apart = 1
        while apart < blocks:
            items = [
                items[b] + items[b ^ apart] if b & apart == 0 else items[b ^ apart] - items[b]
                for b in range(blocks)
            ]
            apart *= 2
        for b in range(blocks):
            held[b, pl.ds(at, strip), :] = items[b] * scale
        return carry

    copies = []
    for part in range(2):
        first = part * piece // strip
        lax.fori_loop(first, first + piece // strip, body, 0)
        span = pl.ds(part * piece, piece)
        copies.append(
            pltpu.make_async_copy(held.at[:, span, :], out_ref.at[:, span, :], sent.at[part])
        )
        copies[-1].start()
    for copy in copies:
        copy.wait()


def local_transform(panel, flips, scale):
    rows, width = panel.shape
    shape = (rows // BLOCK, BLOCK, width)
    return pl.pallas_call(
        functools.partial(local_kernel, scale),
        out_shape=jax.ShapeDtypeStruct(shape, jnp.float32),
        in_specs=[pl.BlockSpec(memory_space=pl.ANY)] * 2,
        out_specs=pl.BlockSpec(memory_space=pl.ANY),
        scratch_shapes=[
            pltpu.VMEM((rows // 128, 128), jnp.int32),
            pltpu.VMEM(shape, jnp.float32),
            pltpu.SemaphoreType.DMA((5,)),
            pltpu.SemaphoreType.DMA((2,)),
        ],
        compiler_params=pltpu.CompilerParams(vmem_limit_bytes=61 * 2**20),
    )(flips.reshape(rows // 128, 128), panel.reshape(shape))


def device_kernel(in_ref, out_ref, held, sent):
    devices, rows, _ = in_ref.shape
    strip = 8
    parts = sent.shape[0]
    share = rows // parts

    def body(step, carry):
        at = pl.multiple_of(step * strip, strip)
        items = [in_ref[d, pl.ds(at, strip), :] for d in range(devices)]
        apart = 1
        while apart < devices:
            items = [
                items[d] + items[d ^ apart] if d & apart == 0 else items[d ^ apart] - items[d]
                for d in range(devices)
            ]
            apart *= 2
        for d in range(devices):
            held[d, pl.ds(at, strip), :] = items[d]
        return carry

    copies = []
    for part in range(parts):
        first = part * share // strip
        lax.fori_loop(first, first + share // strip, body, 0)
        span = pl.ds(part * share, share)
        copies.append(
            pltpu.make_async_copy(held.at[:, span, :], out_ref.at[:, span, :], sent.at[part])
        )
        copies[-1].start()
    for copy in copies:
        copy.wait()


def device_sums(value):
    return pl.pallas_call(
        device_kernel,
        out_shape=jax.ShapeDtypeStruct(value.shape, jnp.float32),
        in_specs=[pl.BlockSpec(memory_space=pltpu.VMEM)],
        out_specs=pl.BlockSpec(memory_space=pl.ANY),
        scratch_shapes=[
            pltpu.VMEM(value.shape, jnp.float32),
            pltpu.SemaphoreType.DMA((min(8, value.shape[1] // 8),)),
        ],
        compiler_params=pltpu.CompilerParams(vmem_limit_bytes=32 * 2**20),
    )(value)


def store_kernel(value_ref, out_ref, sent):
    copy = pltpu.make_async_copy(value_ref, out_ref, sent)
    copy.start()
    copy.wait()


def store(value):
    return pl.pallas_call(
        store_kernel,
        out_shape=jax.ShapeDtypeStruct(value.shape, jnp.float32),
        in_specs=[pl.BlockSpec(memory_space=pltpu.VMEM)],
        out_specs=pl.BlockSpec(memory_space=pl.ANY),
        scratch_shapes=[pltpu.SemaphoreType.DMA],
        compiler_params=pltpu.CompilerParams(vmem_limit_bytes=8 * 2**20),
    )(value)


def index_kernel(rows_here, most, bases_ref, picks_ref, out_ref):
    picks = picks_ref[...]
    devices, per = picks.shape
    before = lax.broadcasted_iota(jnp.int32, (per, per), 0)
    earlier = before < lax.broadcasted_iota(jnp.int32, (per, per), 1)
    earlier = jnp.where(earlier, 1.0, 0.0).astype(jnp.bfloat16)
    for which in range(out_ref.shape[0]):
        offsets = picks - bases_ref[which]
        owned = (offsets >= 0) & (offsets < rows_here)
        ones = jnp.where(owned, 1.0, 0.0).astype(jnp.bfloat16)
        rank = jnp.dot(ones, earlier, preferred_element_type=jnp.float32)
        rank = jnp.where(owned, rank, -1.0)
        marked = (offsets + 1).astype(jnp.float32)
        for slot in range(most):
            hit = jnp.where(rank == float(slot), marked, 0.0)
            row = jnp.sum(hit, axis=1, keepdims=True).astype(jnp.int32) - 1
            out_ref[which, :, slot : slot + 1] = row


def send_rows(picks, owners, rows_here, devices, most):
    bases = jnp.stack(owners) * rows_here
    rows = pl.pallas_call(
        functools.partial(index_kernel, rows_here, most),
        out_shape=jax.ShapeDtypeStruct((len(owners), devices, most), jnp.int32),
        in_specs=[
            pl.BlockSpec(memory_space=pltpu.SMEM),
            pl.BlockSpec(memory_space=pltpu.VMEM),
        ],
        out_specs=pl.BlockSpec(memory_space=pltpu.VMEM),
        compiler_params=pltpu.CompilerParams(vmem_limit_bytes=8 * 2**20),
    )(bases.astype(jnp.int32), picks.reshape(devices, -1))
    return rows.reshape(len(owners) * devices * most)


def count_kernel(rows_here, me_ref, picks_ref, out_ref):
    picks = picks_ref[...]
    rows, devices = out_ref.shape
    owner = picks >> rows_here.bit_length() - 1
    local = picks & rows_here - 1
    held = local >> rows.bit_length() - 1 == me_ref[0]
    place = jnp.where(held, local & rows - 1, -1)
    shape = (devices, picks.shape[1])
    owners = jnp.where(lax.broadcasted_iota(jnp.int32, shape, 0) == owner, 1.0, 0.0)
    shape = (rows, picks.shape[1])
    places = jnp.where(lax.broadcasted_iota(jnp.int32, shape, 0) == place, 1.0, 0.0)
    out_ref[...] = lax.dot_general(
        places.astype(jnp.bfloat16),
        owners.astype(jnp.bfloat16),
        (((1,), (1,)), ((), ())),
        preferred_element_type=jnp.float32,
    )


def count_picks(picks, me, rows_here, devices):
    return pl.pallas_call(
        functools.partial(count_kernel, rows_here),
        out_shape=jax.ShapeDtypeStruct((rows_here // devices, devices), jnp.float32),
        in_specs=[
            pl.BlockSpec(memory_space=pltpu.SMEM),
            pl.BlockSpec(memory_space=pltpu.VMEM),
        ],
        out_specs=pl.BlockSpec(memory_space=pltpu.VMEM),
        compiler_params=pltpu.CompilerParams(vmem_limit_bytes=32 * 2**20),
    )(me.reshape(1).astype(jnp.int32), picks.reshape(1, -1))


def part_kernel(counts_ref, held_ref, out_ref):
    devices, _, width = held_ref.shape
    total = jnp.zeros((width, 2 * width), jnp.float32)
    rest = jnp.zeros((width, width), jnp.float32)
    for d in range(devices):
        rows = held_ref[d]
        high, low = halves(rows)
        weighted, spare = halves(rows * counts_ref[:, d : d + 1])
        over_rows = (((0,), (0,)), ((), ()))
        both = jnp.concatenate([weighted, spare], axis=1)
        total += lax.dot_general(high, both, over_rows, preferred_element_type=jnp.float32)
        rest += lax.dot_general(low, weighted, over_rows, preferred_element_type=jnp.float32)
    out_ref[...] = total[:, :width] + total[:, width:] + rest


def gram_part(counts, held):
    width = held.shape[2]
    return pl.pallas_call(
        part_kernel,
        out_shape=jax.ShapeDtypeStruct((width, width), jnp.float32),
        in_specs=[pl.BlockSpec(memory_space=pltpu.VMEM)] * 2,
        out_specs=pl.BlockSpec(memory_space=pltpu.VMEM),
        compiler_params=pltpu.CompilerParams(vmem_limit_bytes=32 * 2**20),
    )(counts, held)


def swap(value, axis, apart):
    pairs = [(source, source ^ apart) for source in range(lax.axis_size(axis))]
    return lax.ppermute(value, axis, pairs)


def scatter_sum(value, axis):
    upper = lax.axis_index(axis) & 1
    half = value.shape[0] // 2
    keep = lax.dynamic_slice_in_dim(value, upper * half, half)
    give = lax.dynamic_slice_in_dim(value, (1 - upper) * half, half)
    return keep + swap(give, axis, 1)


def gather_halves(value, axis):
    rows, width = value.shape
    blank = jnp.zeros((2 * rows, width), jnp.float32)
    at = (lax.axis_index(axis) & 1) * rows
    value = lax.dynamic_update_slice_in_dim(blank, value, at, 0)
    return value, swap(value, axis, 1)


def order_kernel(order_ref, rows_ref, out_ref):
    width = rows_ref.shape[1]
    rows = rows_ref[...]
    high = rows.astype(jnp.bfloat16)
    middle, low = halves(rows - high.astype(jnp.float32))
    parts = jnp.concatenate([high, middle, low], axis=1)
    out = jnp.dot(order_ref[...], parts, preferred_element_type=jnp.float32)
    out_ref[...] = out[:, :width] + (out[:, width : 2 * width] + out[:, 2 * width :])


def put_in_order(order, rows):
    return pl.pallas_call(
        order_kernel,
        out_shape=jax.ShapeDtypeStruct((order.shape[0], rows.shape[1]), jnp.float32),
        in_specs=[pl.BlockSpec(memory_space=pltpu.VMEM)] * 2,
        out_specs=pl.BlockSpec(memory_space=pltpu.VMEM),
        compiler_params=pltpu.CompilerParams(vmem_limit_bytes=8 * 2**20),
    )(order, rows)


def landing(block, rows_here, most):
    owners = block // rows_here
    order = jnp.arange(block.shape[0], dtype=jnp.int32)
    earlier = (owners[:, None] == owners[None, :]) & (order[None, :] < order[:, None])
    return owners * most + jnp.sum(earlier.astype(jnp.int32), axis=1)


def on_device(panel, flips, picks):
    rows_here, width = panel.shape
    devices = lax.axis_size("narrow") * lax.axis_size("wide")
    scale = 1.0 / float(rows_here * devices) ** 0.5
    me = lax.axis_index(AXES)
    per = picks.shape[0] // devices
    most = -(-per // devices)

    local = local_transform(panel, flips, scale)
    local = local.reshape(devices, rows_here // devices, width)
    wanted = send_rows(picks, [me], rows_here, devices, most)
    spots = landing(lax.dynamic_slice(picks, (me * per,), (per,)), rows_here, most)
    slots = jnp.arange(devices * most, dtype=jnp.int32)
    order = (spots[:, None] == slots[None, :]).astype(jnp.bfloat16)
    counts = count_picks(picks, me, rows_here, devices)
    slices = lax.all_to_all(local, AXES, 0, 0, tiled=True)
    slices, wanted, order, counts = lax.optimization_barrier((slices, wanted, order, counts))
    slices = device_sums(slices)
    mixed = lax.all_to_all(slices, AXES, 0, 0, tiled=True)
    gram = gram_part(counts, slices)
    gram = scatter_sum(gram, "narrow")
    for axis, low in (("narrow", 2), ("wide", 1)):
        while low < lax.axis_size(axis):
            gram = gram + swap(gram, axis, low)
            low *= 2
    mixed, gram = lax.optimization_barrier((mixed, gram))
    mixed = mixed.reshape(rows_here, width)
    chosen = jnp.take(mixed, wanted, axis=0, mode="clip")
    landed = lax.all_to_all(chosen.reshape(devices, most, width), AXES, 0, 0, tiled=True)
    gram, other = gather_halves(gram, "narrow")
    mixed, other = lax.optimization_barrier((mixed, other))
    mixed = store(mixed)
    gram = (gram + other) / float(picks.shape[0])
    landed, mixed, gram = lax.optimization_barrier((landed, mixed, gram))
    landed = landed.reshape(devices * most, width)
    sketch = put_in_order(order, landed)
    return (mixed, sketch, gram)


def solution(mesh):
    in_specs = (P(AXES, None), P(AXES), P())
    out_specs = (P(AXES, None), P(AXES, None), P())
    return jax.shard_map(
        on_device, mesh=mesh, in_specs=in_specs, out_specs=out_specs, check_vma=False
    )
```
